32 devices in a mesh: seq: 8 (over z, y), fsdp: 4 (over x, core).
Axes of the slice: x: 2, y: 2, z: 4, core: 2. Of those that a mesh axis runs over, the one named last changes fastest.
Arguments:
- features: bfloat16 [2, 4, 2048, 512], P(None, 'fsdp', 'seq'), may hold values from -6 to 6
- lengths: int32 [2, 4, 12], P(None, 'fsdp'), may hold values from 1 to 896, as said below
- conv_weight: bfloat16 [1536, 512], P(('seq', 'fsdp')), may hold values from -0.15625 to 0.15625
- feature_gain: bfloat16 [512], P(('seq', 'fsdp')), may hold values from 0.25 to 1.75
- projection_weight: bfloat16 [512, 768], P(('seq', 'fsdp')), may hold values from -0.25 to 0.25
- position_weight: bfloat16 [6144, 768], P(('seq', 'fsdp')), may hold values from -0.078125 to 0.078125
- encoder_gain: bfloat16 [768], P(('seq', 'fsdp')), may hold values from 0.25 to 1.75
- qkv_weight: bfloat16 [768, 2304], P(('seq', 'fsdp')), may hold values from -0.21875 to 0.21875
- output_weight: bfloat16 [768, 768], P(('seq', 'fsdp')), may hold values from -3.5 to 3.5
- attention_gain: bfloat16 [768], P(('seq', 'fsdp')), may hold values from 0.25 to 1.75
- up_weight: bfloat16 [768, 3072], P(('seq', 'fsdp')), may hold values from -0.21875 to 0.21875
- down_weight: bfloat16 [3072, 768], P(('seq', 'fsdp')), may hold values from -0.109375 to 0.109375
- final_gain: bfloat16 [768], P(('seq', 'fsdp')), may hold values from 0.25 to 1.75
- cotangent: bfloat16 [2, 4, 1024, 768], P(None, 'fsdp', 'seq'), may hold values from -6 to 6
Outputs:
- block_output: float32 [2, 4, 1024, 768], P(None, 'fsdp', 'seq')
- feature_grad: float32 [2, 4, 2048, 512], P(None, 'fsdp', 'seq')
- conv_weight_grad: float32 [1536, 512], P(('seq', 'fsdp'))
- feature_gain_grad: float32 [512], P(('seq', 'fsdp'))
- projection_weight_grad: float32 [512, 768], P(('seq', 'fsdp'))
- position_weight_grad: float32 [6144, 768], P(('seq', 'fsdp'))
- encoder_gain_grad: float32 [768], P(('seq', 'fsdp'))
- qkv_weight_grad: float32 [768, 2304], P(('seq', 'fsdp'))
- output_weight_grad: float32 [768, 768], P(('seq', 'fsdp'))
- attention_gain_grad: float32 [768], P(('seq', 'fsdp'))
- up_weight_grad: float32 [768, 3072], P(('seq', 'fsdp'))
- down_weight_grad: float32 [3072, 768], P(('seq', 'fsdp'))
- final_gain_grad: float32 [768], P(('seq', 'fsdp'))
The draws below stay inside these ranges and needn't reach their ends.
Inputs may be any that keep to these rules, and one draw needn't show every extreme that they name: For each micro-batch and stream, 12 utterance lengths in output frames, in order along the stream, summing to 1024.
All inputs are finite; a program needn't handle non-finite values.
Results may differ from the reference program's by a relative error of at most 0.023.
Values may be sent and summed in bfloat16 or wider, within the bound.
No kernel may reach another device: no remote copies, remote signals or barrier semaphores. Data moves between devices by JAX's collectives and lax.ppermute only.
A program may use at most 320 MiB of HBM per device.

```python
import math
import jax
import jax.numpy as jnp
from jax import lax

D = 768
HEADS = 12
FF = 3072
C_CNN = 512
POS_K = 128
GROUPS = 16
HEAD_DIM = 64
CG = 48
FRAMES_DEV = 128
UTT = 12
MICRO = 2
STREAMS = 4
STREAM = 1024


def draw_lengths(key, part):
    key = jax.random.fold_in(key, 11)
    count_rows = MICRO * STREAMS
    first_key, second_key, third_key = jax.random.split(key, 3)
    long_slot = jax.random.randint(first_key, (count_rows, 1), 1, UTT - 1)
    powers = jax.random.randint(second_key, (count_rows, UTT - 1), 0, 8)
    factors = jax.random.randint(third_key, (count_rows, UTT - 1), 1, 5)
    weights = jnp.left_shift(jnp.ones_like(powers), powers) * factors
    spare_frames = FRAMES_DEV - (UTT - 1)
    shares = 1 + spare_frames * weights // jnp.sum(weights, axis=1, keepdims=True, dtype=jnp.int32)
    shares = shares.at[:, 0].add(FRAMES_DEV - jnp.sum(shares, axis=1, dtype=jnp.int32))
    column = jnp.arange(UTT, dtype=jnp.int32)[None, :]
    source = jnp.clip(jnp.where(column < long_slot, column, column - 1), 0, UTT - 2)
    picked = jnp.take_along_axis(shares, source, axis=1)
    result = jnp.where(column == long_slot, STREAM - FRAMES_DEV, picked)
    return result.reshape(MICRO, STREAMS, UTT).astype(jnp.int32)


def levels(key, shape, shards, low, high):
    def one(dim, shards_of):
        steps = jax.random.uniform(jax.random.fold_in(jax.random.fold_in(key, 6), dim), (shards_of,), jnp.float32, low / len(shards), high / len(shards))
        return jnp.repeat(jnp.exp(steps), shape[dim] // shards_of).reshape((-1,) + (1,) * (len(shape) - dim - 1))

    level = one(*shards[0])
    for cut in shards[1:]:
        level = level * one(*cut)
    return level


def normal_values(stream_key, shape, scale, most, cuts=(), kind=jnp.bfloat16):
    loudness = levels(stream_key, shape, cuts, -0.22, 0.18) if cuts else 1.0
    entries = jax.random.normal(stream_key, shape, jnp.float32) * scale * loudness
    return jnp.minimum(jnp.maximum(entries, -most), most).astype(kind)


def setup_inputs(seed: int = 0) -> dict:
    key_list = jax.random.split(jax.random.key(seed), 15)
    features = normal_values(key_list[0], (MICRO, STREAMS, 2 * STREAM, C_CNN), 1.0, 6.0, ((1, 4), (2, 8)))
    lengths = draw_lengths(jax.random.fold_in(key_list[14], 71), 0)
    conv_weight = normal_values(key_list[2], (3 * C_CNN, C_CNN), (3 * C_CNN) ** -0.5, 0.15625, ((0, 32),))
    feature_gain = jnp.clip(1.0 + 0.15 * jax.random.normal(key_list[3], (C_CNN,), jnp.float32), 0.25, 1.75).astype(jnp.bfloat16)
    projection_weight = normal_values(key_list[4], (C_CNN, D), C_CNN ** -0.5, 0.25, ((0, 32),))
    position_weight = normal_values(key_list[5], (POS_K * CG, D), (POS_K * CG) ** -0.5, 0.078125, ((0, 32),))
    encoder_gain = jnp.clip(1.0 + 0.15 * jax.random.normal(key_list[6], (D,), jnp.float32), 0.25, 1.75).astype(jnp.bfloat16)
    qkv_weight = normal_values(key_list[7], (D, 3 * D), D ** -0.5, 0.21875, ((0, 32),))
    output_weight = normal_values(key_list[8], (D, D), (max(1, D * 4 // STREAM)) ** -0.5, 3.5, ((0, 32),))
    attention_gain = jnp.clip(1.0 + 0.15 * jax.random.normal(key_list[9], (D,), jnp.float32), 0.25, 1.75).astype(jnp.bfloat16)
    up_weight = normal_values(key_list[10], (D, FF), D ** -0.5, 0.21875, ((0, 32),))
    down_weight = normal_values(key_list[11], (FF, D), FF ** -0.5, 0.109375, ((0, 32),))
    final_gain = jnp.clip(1.0 + 0.15 * jax.random.normal(key_list[12], (D,), jnp.float32), 0.25, 1.75).astype(jnp.bfloat16)
    cotangent = normal_values(key_list[13], (MICRO, STREAMS, STREAM, D), 1.0, 6.0, ((1, 4), (2, 8)))
    return {"features": features, "lengths": lengths, "conv_weight": conv_weight, "feature_gain": feature_gain, "projection_weight": projection_weight, "position_weight": position_weight, "encoder_gain": encoder_gain, "qkv_weight": qkv_weight, "output_weight": output_weight, "attention_gain": attention_gain, "up_weight": up_weight, "down_weight": down_weight, "final_gain": final_gain, "cotangent": cotangent}


@jax.custom_vjp
def low(v):
    return lax.optimization_barrier(v.astype(jnp.bfloat16)).astype(jnp.float32)

@jax.custom_vjp
def low_back(v):
    return v

def low_keep(v):
    return (low(v), None)

def low_pass(kept, grad):
    return (grad,)

def back_keep(v):
    return (v, None)

def back_low(kept, grad):
    return (low(grad),)
low.defvjp(low_keep, low_pass)
low_back.defvjp(back_keep, back_low)
HIGHEST = lax.Precision.HIGHEST
NORM_EPS = 1e-05

def norm_rows(values, scales):
    center = values - lax.optimization_barrier(jnp.mean(values, axis=-1, keepdims=True))
    spread = lax.optimization_barrier(jnp.mean(center * center, axis=-1, keepdims=True))
    return center * lax.rsqrt(spread + NORM_EPS) * scales

def smooth_gate(values):
    return jax.nn.gelu(values, approximate=False)

def segment_of(utterance_ends, positions):
    return lax.optimization_barrier(jnp.sum((utterance_ends[None, :] <= positions[:, None]).astype(jnp.int32), axis=1, dtype=jnp.int32))

def group_conv(padded, kernel):
    result = lax.conv_general_dilated(padded[None], kernel, (1,), 'VALID', dimension_numbers=('NWC', 'WIO', 'NWC'), feature_group_count=GROUPS, precision=HIGHEST, preferred_element_type=jnp.float32)
    return result[0]

def attention(queries, key_rows, value_rows, segment_ids):
    frame_count = queries.shape[1]
    block_rows = math.gcd(frame_count, 512)
    score_scale = HEAD_DIM ** (-0.5)

    def one_block(start):
        query_part = lax.dynamic_slice_in_dim(queries, start, block_rows, 1)
        segment_part = lax.dynamic_slice_in_dim(segment_ids, start, block_rows, 0)
        scores = low_back(jnp.einsum('hqd,hkd->hqk', query_part, key_rows, precision=HIGHEST) * score_scale)
        allowed = (segment_part[:, None] == segment_ids[None, :])[None]
        exponent = jnp.where(allowed, jnp.exp(scores), 0.0)
        totals = lax.optimization_barrier(jnp.sum(exponent, axis=-1))
        summed = low_back(jnp.einsum('hqk,hkd->hqd', low(exponent), value_rows, precision=HIGHEST))
        return summed / totals[:, :, None]
    starts = jnp.arange(frame_count // block_rows, dtype=jnp.int32) * block_rows
    blocks = lax.map(jax.checkpoint(one_block), starts)
    return blocks.transpose(0, 2, 1, 3).reshape(frame_count, HEADS * HEAD_DIM)

def stream_forward(params, stream_feats, stream_lengths):
    conv_weight, feature_gain, projection_weight, position_weight, encoder_gain, qkv_weight, output_weight, attention_gain, up_weight, down_weight, final_gain = params
    frame_count = stream_feats.shape[0] // 2
    segment_ids = segment_of(jnp.cumsum(stream_lengths, dtype=jnp.int32), jnp.arange(frame_count + 1, dtype=jnp.int32))
    same_next = (segment_ids[1:] == segment_ids[:-1]).astype(jnp.float32)
    frame_pairs = stream_feats.reshape(frame_count, 2 * C_CNN)
    following = jnp.concatenate([frame_pairs[1:, :C_CNN], jnp.zeros((1, C_CNN), jnp.float32)], axis=0) * same_next[:, None]
    unfolded = jnp.concatenate([frame_pairs, following], axis=1)
    before = low_back(jnp.dot(unfolded, conv_weight, precision=HIGHEST))
    normed = low(norm_rows(smooth_gate(before), feature_gain))
    projected = low_back(jnp.dot(normed, projection_weight, precision=HIGHEST))
    half_width = POS_K // 2
    padded = jnp.pad(low(projected), ((half_width, half_width), (0, 0)))
    position = low_back(group_conv(padded, position_weight.reshape(POS_K, CG, D))[:frame_count])
    encoded = norm_rows(projected + smooth_gate(position), encoder_gain)
    mixed_rows = low(low_back(jnp.dot(low(encoded), qkv_weight, precision=HIGHEST)))
    queries = mixed_rows[:, :D].reshape(frame_count, HEADS, HEAD_DIM).transpose(1, 0, 2)
    key_rows = mixed_rows[:, D:2 * D].reshape(frame_count, HEADS, HEAD_DIM).transpose(1, 0, 2)
    value_rows = mixed_rows[:, 2 * D:].reshape(frame_count, HEADS, HEAD_DIM).transpose(1, 0, 2)
    context = attention(queries, key_rows, value_rows, segment_ids[:frame_count])
    branch = low_back(jnp.dot(low(context), output_weight, precision=HIGHEST))
    settled = norm_rows(encoded + branch, attention_gain)
    up_values = low_back(jnp.dot(low(settled), up_weight, precision=HIGHEST))
    fed_result = low_back(jnp.dot(low(smooth_gate(up_values)), down_weight, precision=HIGHEST))
    return norm_rows(settled + fed_result, final_gain)

def reference(features, lengths, conv_weight, feature_gain, projection_weight, position_weight, encoder_gain, qkv_weight, output_weight, attention_gain, up_weight, down_weight, final_gain, cotangent):
    params = tuple((weight.astype(jnp.float32) for weight in (conv_weight, feature_gain, projection_weight, position_weight, encoder_gain, qkv_weight, output_weight, attention_gain, up_weight, down_weight, final_gain)))
    stream_total = MICRO * STREAMS
    stacked = features.astype(jnp.float32).reshape(stream_total, 2 * STREAM, C_CNN)
    stream_lens = lengths.reshape(stream_total, UTT)

    def forward(weights, inputs):

        def scan_step(carried, stream_item):
            return (carried, stream_forward(weights, stream_item[0], stream_item[1]))
        return lax.scan(scan_step, jnp.zeros((), jnp.float32), (inputs, stream_lens))[1]
    outputs, pullback = jax.vjp(forward, params, stacked)
    weight_grads, input_grad = pullback(cotangent.astype(jnp.float32).reshape(stream_total, STREAM, D))
    return (outputs.reshape(MICRO, STREAMS, STREAM, D), input_grad.reshape(MICRO, STREAMS, 2 * STREAM, C_CNN), weight_grads[0], weight_grads[1], weight_grads[2], weight_grads[3], weight_grads[4], weight_grads[5], weight_grads[6], weight_grads[7], weight_grads[8], weight_grads[9], weight_grads[10])
```

```python
import math

import jax
import jax.numpy as jnp
from jax import lax
from jax.experimental import pallas as pl
from jax.experimental.pallas import tpu as pltpu
from jax.sharding import PartitionSpec as P

D = 768
HEADS = 12
C_CNN = 512
POS_K = 128
GROUPS = 16
HEAD_DIM = 64
CG = 48
HALF = POS_K // 2
FINE = 16
COARSE = POS_K // FINE
HEAD_PARTS = 4
MICROS = 2
LOG2E = 1.4426950408889634
VMEM = 60 * 1024 * 1024

NORM_EPS = 1e-05
F32 = jnp.float32
BF16 = jnp.bfloat16


def shifted(array, axis, by):
    peers = lax.axis_size(axis)
    pairs = [(i, i + by) for i in range(peers) if 0 <= i + by < peers]
    return lax.ppermute(array, axis, pairs)


def with_halo(block, width):
    low = shifted(block[:, block.shape[1] - width :], "seq", 1)
    high = shifted(block[:, :width], "seq", -1)
    return jnp.concatenate([low, block, high], axis=1)


def send_parts(parts, axis):
    count = lax.axis_size(axis)
    me = lax.axis_index(axis)
    got = []
    for k in range(count):
        block = lax.dynamic_index_in_dim(parts, me ^ k, 0, keepdims=False)
        got.append(lax.ppermute(block, axis, [(i, i ^ k) for i in range(count)]) if k else block)
    return got


def place_parts(got, axis):
    me = lax.axis_index(axis)
    out = jnp.zeros((len(got),) + got[0].shape, got[0].dtype)
    for k, block in enumerate(got):
        out = lax.dynamic_update_index_in_dim(out, block, me ^ k, 0)
    return out


def return_parts(results, axis):
    count = lax.axis_size(axis)
    back = [
        lax.ppermute(results[k], axis, [(i, i ^ k) for i in range(count)]) if k else results[0]
        for k in range(count)
    ]
    return place_parts(back, axis)


def norm_rows(values, scales):
    center = values - jnp.mean(values, axis=-1, keepdims=True)
    spread = jnp.mean(center * center, axis=-1, keepdims=True)
    return center * lax.rsqrt(spread + NORM_EPS) * scales


def smooth_gate(values):
    return jax.nn.gelu(values, approximate=False)


def segment_of(utterance_ends, positions):
    return jnp.sum(
        (utterance_ends[..., None, :] <= positions[:, None]).astype(jnp.int32),
        axis=-1,
        dtype=jnp.int32,
    )


def plain_dot(left, right):
    return jnp.dot(left, right, preferred_element_type=F32)


def inner_dot(left, right):
    return lax.dot_general(left, right, (((0,), (0,)), ((), ())), preferred_element_type=F32)


def outer_dot(left, right):
    return lax.dot_general(left, right, (((1,), (1,)), ((), ())), preferred_element_type=F32)


def lane_roll(value, shift):
    shift = shift % value.shape[1]
    return pltpu.roll(value, shift, 1) if shift else value


def fine_shifts(x_ref, fine_ref, streams, span):
    for s in range(streams):
        for m in range(MICROS):
            start = (s * MICROS + m) * span
            x = x_ref[s, :, m * span : (m + 1) * span].astype(F32)
            for fine in range(FINE):
                fine_ref[fine * CG : (fine + 1) * CG, start : start + span] = lane_roll(
                    x, -fine
                ).astype(BF16)


def position_kernel(streams, span, frames, x_ref, w_ref, out_ref, fine_ref):
    fine_shifts(x_ref, fine_ref, streams, span)
    weights = w_ref[...].reshape(COARSE * CG, FINE * CG)
    for s in range(streams):
        for m in range(MICROS):
            start = (s * MICROS + m) * span
            terms = jnp.dot(weights, fine_ref[:, start : start + span], preferred_element_type=F32)
            total = terms[:CG]
            for coarse in range(1, COARSE):
                total += lane_roll(terms[coarse * CG : (coarse + 1) * CG], -FINE * coarse)
            out_ref[s, :, m * frames : (m + 1) * frames] = total[:, :frames].astype(BF16)


def position_back_kernel(
    streams, span, frames, x_ref, g_ref, w_ref, dx_ref, dw_ref, fine_ref, coarse_ref, own_ref
):
    fine_shifts(x_ref, fine_ref, streams, span)
    column = lax.broadcasted_iota(jnp.int32, (CG, span), 1)
    for s in range(streams):
        for m in range(MICROS):
            start = (s * MICROS + m) * span
            g = g_ref[s, :, m * span : (m + 1) * span].astype(F32)
            own = jnp.where((column >= HALF) & (column < HALF + frames), g, 0.0)
            for coarse in range(COARSE):
                rows = slice(coarse * CG, (coarse + 1) * CG)
                coarse_ref[rows, start : start + span] = lane_roll(
                    g, -FINE * (COARSE - 1 - coarse)
                ).astype(BF16)
                own_ref[rows, start : start + span] = lane_roll(
                    own, FINE * coarse - HALF
                ).astype(BF16)
    weights = w_ref[...].reshape(COARSE * CG, FINE * CG)
    turned = weights.astype(F32).T.astype(BF16)
    for s in range(streams):
        for m in range(MICROS):
            start = (s * MICROS + m) * span
            terms = jnp.dot(turned, coarse_ref[:, start : start + span], preferred_element_type=F32)
            total = lane_roll(terms[:CG], -FINE)
            for fine in range(1, FINE):
                total += lane_roll(terms[fine * CG : (fine + 1) * CG], fine - FINE)
            dx_ref[s, :, m * frames : (m + 1) * frames] = total[:, :frames].astype(BF16)
    grad = lax.dot_general(
        own_ref[...], fine_ref[...], (((1,), (1,)), ((), ())), preferred_element_type=F32
    )
    dw_ref[...] = grad.astype(BF16).reshape(COARSE, CG, FINE * CG)


def position_conv(x, weights, frames):
    streams, channels, columns = x.shape
    span = columns // MICROS
    groups = channels // CG
    flops = 2 * groups * streams * columns * COARSE * CG * FINE * CG
    return pl.pallas_call(
        lambda *refs: position_kernel(streams, span, frames, *refs),
        grid=(groups,),
        in_specs=[
            pl.BlockSpec((streams, CG, columns), lambda g: (0, g, 0)),
            pl.BlockSpec((COARSE, CG, FINE * CG), lambda g: (0, g, 0)),
        ],
        out_specs=pl.BlockSpec((streams, CG, MICROS * frames), lambda g: (0, g, 0)),
        out_shape=jax.ShapeDtypeStruct((streams, channels, MICROS * frames), BF16),
        scratch_shapes=[pltpu.VMEM((FINE * CG, streams * columns), BF16)],
        compiler_params=pltpu.CompilerParams(vmem_limit_bytes=VMEM),
        cost_estimate=pl.CostEstimate(
            flops=flops, bytes_accessed=2 * (x.size + weights.size), transcendentals=0
        ),
        name="position_conv",
    )(x, weights)


def position_back(x, grad, weights, frames):
    streams, channels, columns = x.shape
    span = columns // MICROS
    groups = channels // CG
    flops = 4 * groups * streams * columns * COARSE * CG * FINE * CG
    return pl.pallas_call(
        lambda *refs: position_back_kernel(streams, span, frames, *refs),
        grid=(groups,),
        in_specs=[
            pl.BlockSpec((streams, CG, columns), lambda g: (0, g, 0)),
            pl.BlockSpec((streams, CG, columns), lambda g: (0, g, 0)),
            pl.BlockSpec((COARSE, CG, FINE * CG), lambda g: (0, g, 0)),
        ],
        out_specs=[
            pl.BlockSpec((streams, CG, MICROS * frames), lambda g: (0, g, 0)),
            pl.BlockSpec((COARSE, CG, FINE * CG), lambda g: (0, g, 0)),
        ],
        out_shape=[
            jax.ShapeDtypeStruct((streams, channels, MICROS * frames), BF16),
            jax.ShapeDtypeStruct((COARSE, channels, FINE * CG), BF16),
        ],
        scratch_shapes=[
            pltpu.VMEM((FINE * CG, streams * columns), BF16),
            pltpu.VMEM((COARSE * CG, streams * columns), BF16),
            pltpu.VMEM((COARSE * CG, streams * columns), BF16),
        ],
        compiler_params=pltpu.CompilerParams(vmem_limit_bytes=VMEM),
        cost_estimate=pl.CostEstimate(
            flops=flops, bytes_accessed=4 * (x.size + weights.size), transcendentals=0
        ),
        name="position_back",
    )(x, grad, weights)


def side_by_side(ref):
    return jnp.concatenate([ref[s, 0] for s in range(ref.shape[0])], axis=1)


def turn(value):
    return value.astype(F32).T.astype(BF16)


def attention_kernel(block, q_ref, k_ref, v_ref, seg_q_ref, seg_k_ref, out_ref):
    queries = turn(side_by_side(q_ref))
    keys = side_by_side(k_ref)
    values = side_by_side(v_ref)
    frames = out_ref.shape[2]
    factor = HEAD_DIM**-0.5 * LOG2E
    for first in range(0, queries.shape[0], block):
        rows = slice(first, first + block)
        scores = jnp.dot(queries[rows], keys, preferred_element_type=F32)
        expo = jnp.where(seg_q_ref[rows] == seg_k_ref[...], jnp.exp2(scores * factor), 0.0)
        weight_sum = jnp.sum(expo, axis=1, keepdims=True)
        accum = lax.dot_general(
            expo.astype(BF16), values, (((1,), (1,)), ((), ())), preferred_element_type=F32
        )
        context = (accum / weight_sum).T
        for part in range(block // frames):
            out_ref[first // frames + part] = context[:, part * frames : (part + 1) * frames]


def attention_back_kernel(
    block, q_ref, k_ref, v_ref, cg_ref, ctx_ref, seg_q_ref, seg_k_ref,
    dq_ref, dk_ref, dv_ref, dk_sum, dv_sum,
):
    keys_across = side_by_side(k_ref)
    keys = turn(keys_across)
    values = turn(side_by_side(v_ref))
    frames = ctx_ref.shape[2]
    parts = block // frames
    scale = HEAD_DIM**-0.5
    for step in range(q_ref.shape[0] // parts):
        some = range(step * parts, (step + 1) * parts)
        columns = slice(step * block, (step + 1) * block)
        queries = jnp.concatenate([q_ref[s, 0] for s in some], axis=1)
        context_grad = jnp.concatenate([cg_ref[s].astype(F32) for s in some], axis=1)
        context = jnp.concatenate([ctx_ref[s] for s in some], axis=1)
        scores = jnp.dot(keys, queries, preferred_element_type=F32)
        expo = jnp.where(
            seg_k_ref[...] == seg_q_ref[:, columns], jnp.exp2(scores * (scale * LOG2E)), 0.0
        )
        inverse = 1.0 / jnp.sum(expo, axis=0, keepdims=True)
        accum_g = (context_grad * inverse).astype(BF16)
        correction = jnp.sum(context_grad * context, axis=0, keepdims=True) * inverse
        dots = jnp.dot(values, accum_g, preferred_element_type=F32)
        score_g = (expo * (dots - correction)).astype(BF16)
        query_grad = jnp.dot(keys_across, score_g, preferred_element_type=F32) * scale
        for part, s in enumerate(some):
            dq_ref[s] = query_grad[:, part * frames : (part + 1) * frames].astype(BF16)
        key_grad = lax.dot_general(
            score_g, queries, (((1,), (1,)), ((), ())), preferred_element_type=F32
        )
        value_grad = lax.dot_general(
            expo.astype(BF16), accum_g, (((1,), (1,)), ((), ())), preferred_element_type=F32
        )
        if step == 0:
            dk_sum[...] = key_grad
            dv_sum[...] = value_grad
        else:
            dk_sum[...] += key_grad
            dv_sum[...] += value_grad
    key_total = (dk_sum[...] * scale).T.astype(BF16)
    value_total = dv_sum[...].T.astype(BF16)
    for s in range(dk_ref.shape[0]):
        dk_ref[s] = key_total[:, s * frames : (s + 1) * frames]
        dv_ref[s] = value_total[:, s * frames : (s + 1) * frames]


def head_spec(count, frames, which):
    return pl.BlockSpec((count, 1, HEAD_DIM, frames), lambda h: (0, which, h, 0))


def plain_spec(count, frames):
    return pl.BlockSpec((count, HEAD_DIM, frames), lambda h: (0, h, 0))


def whole_spec(array):
    return pl.BlockSpec(array.shape, lambda h: (0,) * array.ndim)


def attention(mixed, mixed_all, seg_q, seg_k):
    count, _, channels, frames = mixed.shape
    total = mixed_all.shape[0]
    heads = channels // HEAD_DIM
    block = math.gcd(count, 2) * frames
    seg_q, seg_k = seg_q[:, None], seg_k[None]
    pairs = heads * count * frames * total * frames
    return pl.pallas_call(
        lambda *refs: attention_kernel(block, *refs),
        grid=(heads,),
        in_specs=[
            head_spec(count, frames, 0),
            head_spec(total, frames, 1),
            head_spec(total, frames, 2),
            whole_spec(seg_q),
            whole_spec(seg_k),
        ],
        out_specs=plain_spec(count, frames),
        out_shape=jax.ShapeDtypeStruct((count, channels, frames), F32),
        compiler_params=pltpu.CompilerParams(vmem_limit_bytes=VMEM),
        cost_estimate=pl.CostEstimate(
            flops=4 * HEAD_DIM * pairs, bytes_accessed=8 * mixed.size, transcendentals=pairs
        ),
        name="attention",
    )(mixed, mixed_all, mixed_all, seg_q, seg_k)


def attention_back(mixed, mixed_all, context_grad, context, seg_q, seg_k):
    count, _, channels, frames = mixed.shape
    total = mixed_all.shape[0]
    heads = channels // HEAD_DIM
    block = math.gcd(count, 2) * frames
    seg_q, seg_k = seg_q[None], seg_k[:, None]
    pairs = heads * count * frames * total * frames
    return pl.pallas_call(
        lambda *refs: attention_back_kernel(block, *refs),
        grid=(heads,),
        in_specs=[
            head_spec(count, frames, 0),
            head_spec(total, frames, 1),
            head_spec(total, frames, 2),
            plain_spec(count, frames),
            plain_spec(count, frames),
            whole_spec(seg_q),
            whole_spec(seg_k),
        ],
        out_specs=[
            plain_spec(count, frames),
            plain_spec(total, frames),
            plain_spec(total, frames),
        ],
        out_shape=[
            jax.ShapeDtypeStruct((count, channels, frames), BF16),
            jax.ShapeDtypeStruct((total, channels, frames), BF16),
            jax.ShapeDtypeStruct((total, channels, frames), BF16),
        ],
        scratch_shapes=[pltpu.VMEM((total * frames, HEAD_DIM), F32)] * 2,
        compiler_params=pltpu.CompilerParams(vmem_limit_bytes=VMEM),
        cost_estimate=pl.CostEstimate(
            flops=10 * HEAD_DIM * pairs, bytes_accessed=16 * mixed.size, transcendentals=pairs
        ),
        name="attention_back",
    )(mixed, mixed_all, mixed_all, context_grad, context, seg_q, seg_k)


def body(
    features,
    lengths,
    conv_weight,
    feature_gain,
    projection_weight,
    position_weight,
    encoder_gain,
    qkv_weight,
    output_weight,
    attention_gain,
    up_weight,
    down_weight,
    final_gain,
    cotangent,
):
    frames = cotangent.shape[2]
    rows = MICROS * frames
    seqs = lax.axis_size("seq")
    streams = lax.axis_size("fsdp")
    devices = seqs * streams
    me = lax.axis_index("seq")
    both = ("seq", "fsdp")

    front_rows = (conv_weight.shape[0], projection_weight.size // C_CNN)
    gains = jnp.concatenate([feature_gain, encoder_gain, attention_gain, final_gain])
    front = jnp.concatenate(
        [
            conv_weight,
            projection_weight.reshape(-1, C_CNN),
            jnp.pad(gains[None], ((0, 7), (0, C_CNN - gains.size))),
        ],
        axis=0,
    )
    front = lax.all_gather(front, both, axis=0, tiled=False)
    cut = front_rows[0] + front_rows[1]
    conv_full = front[:, : front_rows[0]].reshape(-1, C_CNN)
    projection_full = front[:, front_rows[0] : cut].reshape(C_CNN, D)
    gains_full = front[:, cut, : gains.size]
    feature_n, model_n = feature_gain.size, encoder_gain.size
    feature_scale = gains_full[:, :feature_n].reshape(-1).astype(F32)
    encoder_scale, attention_scale, final_scale = (
        gains_full[:, feature_n + i * model_n : feature_n + (i + 1) * model_n]
        .reshape(-1)
        .astype(F32)
        for i in range(3)
    )

    share = D // streams
    own_rows = position_weight.shape[0]
    parts = position_weight.reshape(own_rows, streams, share).transpose(1, 0, 2)
    parts = place_parts(send_parts(parts, "fsdp"), "fsdp").reshape(streams * own_rows, share)
    position_full = lax.all_gather(parts.T, "seq", axis=0, tiled=False)
    position_full = (
        position_full.reshape(COARSE, -1, share, streams * own_rows)
        .transpose(0, 2, 1, 3)
        .reshape(COARSE, share, FINE * CG)
    )

    middle = lax.all_gather(
        jnp.concatenate([qkv_weight, output_weight], axis=1), both, axis=0, tiled=True
    )
    qkv_full, output_full = middle[:, : 3 * D], middle[:, 3 * D :]
    up_rows, down_rows = up_weight.shape[0], down_weight.shape[0]
    ups = up_weight.shape[1] // D
    feed = lax.all_gather(
        jnp.concatenate(
            [
                up_weight.reshape(up_rows, ups, D).transpose(1, 0, 2).reshape(-1, D),
                down_weight,
            ],
            axis=0,
        ),
        both,
        axis=0,
        tiled=False,
    )
    up_full = (
        feed[:, : ups * up_rows]
        .reshape(devices, ups, up_rows, D)
        .transpose(0, 2, 1, 3)
        .reshape(D, ups * D)
    )
    down_full = feed[:, ups * up_rows :].reshape(-1, D)

    ends = jnp.cumsum(lengths[:, 0], axis=-1, dtype=jnp.int32)
    positions = me * frames + jnp.arange(frames + 1, dtype=jnp.int32)
    segments = segment_of(ends, positions)
    same_next = (segments[:, 1:] == segments[:, :-1])[:, :, None]
    pairs = features[:, 0].reshape(MICROS, frames, 2 * C_CNN)
    next_first = shifted(pairs[:, :1, :C_CNN], "seq", -1)
    following = jnp.concatenate([pairs[:, 1:, :C_CNN], next_first], axis=1)
    following = following * same_next.astype(BF16)
    unfolded = jnp.concatenate([pairs, following], axis=2).reshape(rows, 3 * C_CNN)
    before = plain_dot(unfolded, conv_full)
    activated, gate_back = jax.vjp(smooth_gate, before)
    normed, first_norm_back = jax.vjp(norm_rows, activated, feature_scale)
    normed_low = normed.astype(BF16)
    projected = plain_dot(normed_low, projection_full)

    def to_groups(block):
        wide = with_halo(block.reshape(MICROS, frames, D), HALF)
        wide = wide.transpose(2, 0, 1).reshape(streams, share, -1)
        return jnp.stack(send_parts(wide, "fsdp"))

    def from_groups(block):
        return return_parts(block, "fsdp").reshape(D, rows).T.astype(F32)

    window = to_groups(projected.astype(BF16))
    position = from_groups(position_conv(window, position_full, frames))
    position_act, position_gate_back = jax.vjp(smooth_gate, position)
    encoded, encoder_back = jax.vjp(norm_rows, projected + position_act, encoder_scale)
    encoded_low = encoded.astype(BF16)

    group = HEAD_PARTS * MICROS
    outer = seqs // group
    near = [[o * group + i for i in range(group)] for o in range(outer)]
    far = [[o * group + i for o in range(outer)] for i in range(group)]
    part = D // HEAD_PARTS
    mixed = lax.dot_general(
        qkv_full, encoded_low, (((0,), (1,)), ((), ())), preferred_element_type=F32
    ).astype(BF16)

    def to_heads(across, kinds):
        blocks = across.reshape(kinds, HEAD_PARTS, part, MICROS, frames)
        blocks = blocks.transpose(1, 3, 0, 2, 4).reshape(group, kinds, part, frames)
        return lax.all_to_all(blocks, "seq", 0, 0, axis_index_groups=near)

    def from_heads(blocks, kinds):
        blocks = lax.all_to_all(blocks, "seq", 0, 0, axis_index_groups=near)
        blocks = blocks.reshape(HEAD_PARTS, MICROS, kinds, part, frames)
        return blocks.transpose(2, 0, 3, 1, 4).reshape(kinds * D, rows)

    mixed_heads = to_heads(mixed, 3)
    if outer > 1:
        mixed_all = lax.all_gather(
            mixed_heads, "seq", axis=0, tiled=True, axis_index_groups=far
        )
    else:
        mixed_all = mixed_heads
    micro_ends = lax.dynamic_index_in_dim(ends, me % MICROS, 0, keepdims=False)
    seg_all = segment_of(micro_ends, jnp.arange(seqs * frames, dtype=jnp.int32))
    seg_own = lax.dynamic_slice_in_dim(
        seg_all, (me // group) * group * frames, group * frames, 0
    )
    context_heads = attention(mixed_heads, mixed_all, seg_own, seg_all)
    context_low = from_heads(context_heads.astype(BF16)[:, None], 1).T
    branch = plain_dot(context_low, output_full)
    settled, attention_norm_back = jax.vjp(norm_rows, encoded + branch, attention_scale)

    settled_low = settled.astype(BF16)
    up_values = plain_dot(settled_low, up_full)
    hidden, hidden_back = jax.vjp(smooth_gate, up_values)
    hidden_low = hidden.astype(BF16)
    fed = plain_dot(hidden_low, down_full)
    block_out, final_back = jax.vjp(norm_rows, settled + fed, final_scale)
    sum_grad, final_grad = final_back(cotangent[:, 0].reshape(rows, D).astype(F32))
    fed_low = sum_grad.astype(BF16)
    down_grad = inner_dot(hidden_low, fed_low).astype(BF16)
    (up_raw,) = hidden_back(outer_dot(fed_low, down_full))
    up_low = up_raw.astype(BF16)
    up_grad = inner_dot(settled_low, up_low).astype(BF16)
    settled_grad = sum_grad + outer_dot(up_low, up_full)
    mid_grad, attention_grad = attention_norm_back(settled_grad)
    branch_low = mid_grad.astype(BF16)
    output_grad = inner_dot(context_low, branch_low).astype(BF16)

    def scatter_rows(grad):
        chunks = grad.shape[1] // D
        grad = grad.reshape(devices, -1, chunks, D).transpose(0, 2, 1, 3)
        return grad.reshape(devices, -1, D)

    def unscatter_rows(block, chunks):
        return block.reshape(chunks, -1, D).transpose(1, 0, 2).reshape(-1, chunks * D)

    feed_grads = jnp.concatenate(
        [scatter_rows(down_grad), scatter_rows(up_grad), scatter_rows(output_grad)], axis=1
    )
    feed_grads = lax.psum_scatter(feed_grads, both, scatter_dimension=0).astype(F32)
    down_shard = feed_grads[:down_rows]
    up_shard = unscatter_rows(feed_grads[down_rows : down_rows + ups * up_rows], ups)
    output_shard = feed_grads[down_rows + ups * up_rows :]

    context_grad = lax.dot_general(
        output_full, branch_low, (((1,), (1,)), ((), ())), preferred_element_type=F32
    ).astype(BF16)
    context_grad = to_heads(context_grad, 1)[:, 0]
    dq, dk, dv = attention_back(
        mixed_heads, mixed_all, context_grad, context_heads, seg_own, seg_all
    )
    if outer > 1:
        dk, dv = (
            lax.psum_scatter(
                grad, "seq", scatter_dimension=0, tiled=True, axis_index_groups=far
            )
            for grad in (dk, dv)
        )
    mixed_g = from_heads(jnp.stack([dq, dk, dv], axis=1), 3)
    qkv_grad = lax.dot_general(
        encoded_low, mixed_g, (((0,), (1,)), ((), ())), preferred_element_type=F32
    ).astype(BF16)
    encoded_grad = mid_grad + lax.dot_general(
        mixed_g, qkv_full, (((0,), (1,)), ((), ())), preferred_element_type=F32
    )

    joined_grad, encoder_grad = encoder_back(encoded_grad)
    (position_grad,) = position_gate_back(joined_grad)
    grad_window = to_groups(position_grad.astype(BF16))
    projected_back, position_grad_w = position_back(window, grad_window, position_full, frames)
    position_grad_w = (
        position_grad_w.reshape(COARSE, share, -1, streams * own_rows)
        .transpose(0, 2, 1, 3)
        .reshape(seqs, share, streams * own_rows)
    )
    position_shard = lax.psum_scatter(position_grad_w, "seq", scatter_dimension=0)
    position_shard = place_parts(
        send_parts(position_shard.T.reshape(streams, own_rows, share), "fsdp"), "fsdp"
    )
    position_shard = position_shard.transpose(1, 0, 2).reshape(own_rows, D).astype(F32)

    projected_grad = (joined_grad + from_groups(projected_back)).astype(BF16)
    projection_grad = inner_dot(normed_low, projected_grad).astype(BF16)
    activated_grad, feature_grad = first_norm_back(outer_dot(projected_grad, projection_full))
    (before_grad,) = gate_back(activated_grad)
    before_low = before_grad.astype(BF16)
    conv_grad = inner_dot(unfolded, before_low).astype(BF16)
    unfolded_grad = outer_dot(before_low, conv_full).reshape(MICROS, frames, 3 * C_CNN)
    following_grad = unfolded_grad[:, :, 2 * C_CNN :] * same_next.astype(F32)
    carried = shifted(following_grad[:, frames - 1 :], "seq", 1)
    even_grad = unfolded_grad[:, :, :C_CNN] + jnp.concatenate(
        [carried, following_grad[:, :-1]], axis=1
    )
    input_grad = jnp.concatenate([even_grad, unfolded_grad[:, :, C_CNN : 2 * C_CNN]], axis=2)
    input_grad = input_grad.reshape(MICROS, 1, 2 * frames, C_CNN)

    gain_grads = jnp.concatenate(
        [feature_grad.reshape(devices, -1)]
        + [grad.reshape(devices, -1) for grad in (encoder_grad, attention_grad, final_grad)],
        axis=1,
    ).astype(BF16)
    gain_grads = jnp.pad(gain_grads[:, None], ((0, 0), (0, 7), (0, D - gains.size)))
    rest = jnp.concatenate(
        [
            scatter_rows(qkv_grad),
            projection_grad.reshape(devices, -1, D),
            conv_grad.reshape(devices, -1, D),
            gain_grads,
        ],
        axis=1,
    )
    rest = lax.psum_scatter(rest, both, scatter_dimension=0).astype(F32)
    cuts = [0, 3 * qkv_weight.shape[0]]
    cuts.append(cuts[-1] + projection_weight.shape[0])
    cuts.append(cuts[-1] + conv_weight.size // D)
    qkv_shard = unscatter_rows(rest[: cuts[1]], 3)
    projection_shard = rest[cuts[1] : cuts[2]]
    conv_shard = rest[cuts[2] : cuts[3]].reshape(-1, C_CNN)
    gain_row = rest[cuts[3]]
    gain_shards = [
        gain_row[:feature_n],
        *(gain_row[feature_n + i * model_n : feature_n + (i + 1) * model_n] for i in range(3)),
    ]
    return (
        block_out.reshape(MICROS, 1, frames, D),
        input_grad,
        conv_shard,
        gain_shards[0],
        projection_shard,
        position_shard,
        gain_shards[1],
        qkv_shard,
        output_shard,
        gain_shards[2],
        up_shard,
        down_shard,
        gain_shards[3],
    )


def solution(mesh):
    weight, gain = P(("seq", "fsdp"), None), P(("seq", "fsdp"))
    rows = P(None, "fsdp", "seq", None)
    in_specs = (
        rows, P(None, "fsdp", None), weight, gain, weight, weight, gain, weight, weight, gain,
        weight, weight, gain, rows,
    )
    out_specs = (
        rows, rows, weight, gain, weight, weight, gain, weight, weight, gain, weight, weight, gain,
    )
    return jax.shard_map(body, mesh=mesh, in_specs=in_specs, out_specs=out_specs, check_vma=False)
```

```python
import math

import jax
import jax.numpy as jnp
from jax import lax
from jax.experimental import pallas as pl
from jax.experimental.pallas import tpu as pltpu
from jax.sharding import PartitionSpec as P

D = 768
HEADS = 12
C_CNN = 512
POS_K = 128
GROUPS = 16
HEAD_DIM = 64
CG = 48
HALF = POS_K // 2
FINE = 16
COARSE = POS_K // FINE
HEAD_PARTS = 4
MICROS = 2
LOG2E = 1.4426950408889634
VMEM = 60 * 1024 * 1024

NORM_EPS = 1e-05
F32 = jnp.float32
BF16 = jnp.bfloat16


def shifted(array, axis, by):
    peers = lax.axis_size(axis)
    pairs = [(i, i + by) for i in range(peers) if 0 <= i + by < peers]
    return lax.ppermute(array, axis, pairs)


def flip(blocks, me):
    count = len(blocks)
    return [lax.select_n(me, *(blocks[m ^ k] for m in range(count))) for k in range(count)]


def swapped(array, k):
    count = lax.axis_size("fsdp")
    return lax.ppermute(array, "fsdp", [(i, i ^ k) for i in range(count)])


def swap_parts(parts, me):
    ordered = flip(parts, me)
    return flip([ordered[0]] + [swapped(ordered[k], k) for k in range(1, 4)], me)


def gather_blocks(block):
    over_x = swapped(block, 2)
    return [block, swapped(block, 1), over_x, swapped(over_x, 1)]


def low_sum(*terms):
    return sum(term.astype(F32) for term in terms).astype(BF16)


def pair_sums(blocks):
    return low_sum(blocks[0], swapped(blocks[1], 1)), low_sum(blocks[2], swapped(blocks[3], 1))


def reduce_blocks(blocks):
    kept, sent = pair_sums(blocks)
    return low_sum(kept, swapped(sent, 2))


def norm_rows(values, scales):
    center = values - jnp.mean(values, axis=-1, keepdims=True)
    spread = jnp.mean(center * center, axis=-1, keepdims=True)
    return center * lax.rsqrt(spread + NORM_EPS) * scales


def smooth_gate(values):
    return jax.nn.gelu(values, approximate=False)


def segment_of(utterance_ends, positions):
    return jnp.sum(
        (utterance_ends[..., None, :] <= positions[:, None]).astype(jnp.int32),
        axis=-1,
        dtype=jnp.int32,
    )


def plain_dot(left, right):
    return jnp.dot(left, right, preferred_element_type=F32)


def inner_dot(left, right):
    return lax.dot_general(left, right, (((0,), (0,)), ((), ())), preferred_element_type=F32)


def outer_dot(left, right):
    return lax.dot_general(left, right, (((1,), (1,)), ((), ())), preferred_element_type=F32)


def lane_roll(value, shift):
    shift = shift % value.shape[1]
    return pltpu.roll(value, shift, 1) if shift else value


def joined(ref, edge_ref, micro, frames):
    columns = slice(micro * frames, (micro + 1) * frames)
    edge = slice(micro * POS_K, (micro + 1) * POS_K)
    blocks = [ref[s, :, columns] for s in range(ref.shape[0])] + [edge_ref[:, edge]]
    return jnp.concatenate(blocks, axis=1).astype(F32)


def fine_shifts(x_ref, edge_ref, fine_ref, frames, span):
    for m in range(MICROS):
        x = joined(x_ref, edge_ref, m, frames)
        for fine in range(FINE):
            fine_ref[fine * CG : (fine + 1) * CG, m * span : (m + 1) * span] = lane_roll(
                x, HALF - fine
            ).astype(BF16)


def store_frames(out_ref, micro, frames, total):
    for s in range(out_ref.shape[0]):
        out_ref[s, :, micro * frames : (micro + 1) * frames] = total[
            :, s * frames : (s + 1) * frames
        ].astype(BF16)


def position_kernel(span, frames, x_ref, edge_ref, w_ref, out_ref, fine_ref):
    fine_shifts(x_ref, edge_ref, fine_ref, frames, span)
    weights = w_ref[...].reshape(COARSE * CG, FINE * CG)
    for m in range(MICROS):
        terms = jnp.dot(
            weights, fine_ref[:, m * span : (m + 1) * span], preferred_element_type=F32
        )
        total = terms[:CG]
        for coarse in range(1, COARSE):
            total += lane_roll(terms[coarse * CG : (coarse + 1) * CG], -FINE * coarse)
        store_frames(out_ref, m, frames, total)


def position_back_kernel(
    span, frames, x_ref, x_edge_ref, g_ref, g_edge_ref, w_ref, dx_ref, dw_ref,
    fine_ref, coarse_ref, own_ref,
):
    fine_shifts(x_ref, x_edge_ref, fine_ref, frames, span)
    column = lax.broadcasted_iota(jnp.int32, (CG, span), 1)
    for m in range(MICROS):
        columns = slice(m * span, (m + 1) * span)
        g = joined(g_ref, g_edge_ref, m, frames)
        own = jnp.where(column < span - POS_K, g, 0.0)
        for coarse in range(COARSE):
            rows = slice(coarse * CG, (coarse + 1) * CG)
            back = FINE * (COARSE - 1 - coarse)
            coarse_ref[rows, columns] = lane_roll(g, HALF - back).astype(BF16)
            own_ref[rows, columns] = lane_roll(own, FINE * coarse).astype(BF16)
    weights = w_ref[...].reshape(COARSE * CG, FINE * CG)
    turned = weights.astype(F32).T.astype(BF16)
    for m in range(MICROS):
        terms = jnp.dot(
            turned, coarse_ref[:, m * span : (m + 1) * span], preferred_element_type=F32
        )
        total = lane_roll(terms[:CG], -FINE)
        for fine in range(1, FINE):
            total += lane_roll(terms[fine * CG : (fine + 1) * CG], fine - FINE)
        store_frames(dx_ref, m, frames, total)
    grad = lax.dot_general(
        own_ref[...], fine_ref[...], (((1,), (1,)), ((), ())), preferred_element_type=F32
    )
    dw_ref[...] = grad.astype(BF16).reshape(COARSE, CG, FINE * CG)


def group_specs(count, columns):
    wide = pl.BlockSpec((count, CG, columns), lambda g: (0, g, 0))
    edge = pl.BlockSpec((CG, MICROS * POS_K), lambda g: (g, 0))
    weight = pl.BlockSpec((COARSE, CG, FINE * CG), lambda g: (0, g, 0))
    return wide, edge, weight


def position_conv(x, edge, weights):
    count, channels, columns = x.shape
    frames = columns // MICROS
    span = count * frames + POS_K
    groups = channels // CG
    wide, edge_spec, weight = group_specs(count, columns)
    flops = 2 * groups * MICROS * span * COARSE * CG * FINE * CG
    return pl.pallas_call(
        lambda *refs: position_kernel(span, frames, *refs),
        grid=(groups,),
        in_specs=[wide, edge_spec, weight],
        out_specs=wide,
        out_shape=jax.ShapeDtypeStruct(x.shape, BF16),
        scratch_shapes=[pltpu.VMEM((FINE * CG, MICROS * span), BF16)],
        compiler_params=pltpu.CompilerParams(vmem_limit_bytes=VMEM),
        cost_estimate=pl.CostEstimate(
            flops=flops, bytes_accessed=2 * (2 * x.size + weights.size), transcendentals=0
        ),
        name="position_conv",
    )(x, edge, weights)


def position_back(x, x_edge, grad, grad_edge, weights):
    count, channels, columns = x.shape
    frames = columns // MICROS
    span = count * frames + POS_K
    groups = channels // CG
    wide, edge_spec, weight = group_specs(count, columns)
    flops = 4 * groups * MICROS * span * COARSE * CG * FINE * CG
    return pl.pallas_call(
        lambda *refs: position_back_kernel(span, frames, *refs),
        grid=(groups,),
        in_specs=[wide, edge_spec, wide, edge_spec, weight],
        out_specs=[wide, weight],
        out_shape=[
            jax.ShapeDtypeStruct(x.shape, BF16),
            jax.ShapeDtypeStruct(weights.shape, BF16),
        ],
        scratch_shapes=[
            pltpu.VMEM((FINE * CG, MICROS * span), BF16),
            pltpu.VMEM((COARSE * CG, MICROS * span), BF16),
            pltpu.VMEM((COARSE * CG, MICROS * span), BF16),
        ],
        compiler_params=pltpu.CompilerParams(vmem_limit_bytes=VMEM),
        cost_estimate=pl.CostEstimate(
            flops=flops, bytes_accessed=2 * (3 * x.size + 2 * weights.size), transcendentals=0
        ),
        name="position_back",
    )(x, x_edge, grad, grad_edge, weights)


def side_by_side(ref):
    return jnp.concatenate([ref[s, 0] for s in range(ref.shape[0])], axis=1)


def turn(value):
    return value.astype(F32).T.astype(BF16)


def attention_kernel(block, q_ref, k_ref, v_ref, seg_q_ref, seg_k_ref, out_ref):
    queries = turn(side_by_side(q_ref))
    keys = side_by_side(k_ref)
    values = side_by_side(v_ref)
    frames = out_ref.shape[2]
    factor = HEAD_DIM**-0.5 * LOG2E
    for first in range(0, queries.shape[0], block):
        rows = slice(first, first + block)
        scores = jnp.dot(queries[rows], keys, preferred_element_type=F32)
        expo = jnp.where(seg_q_ref[rows] == seg_k_ref[...], jnp.exp2(scores * factor), 0.0)
        weight_sum = jnp.sum(expo, axis=1, keepdims=True)
        accum = lax.dot_general(
            expo.astype(BF16), values, (((1,), (1,)), ((), ())), preferred_element_type=F32
        )
        context = (accum / weight_sum).T
        for part in range(block // frames):
            out_ref[first // frames + part] = context[:, part * frames : (part + 1) * frames]


def attention_back_kernel(
    block, q_ref, k_ref, v_ref, cg_ref, ctx_ref, seg_q_ref, seg_k_ref,
    dq_ref, dk_ref, dv_ref, dk_sum, dv_sum,
):
    keys_across = side_by_side(k_ref)
    keys = turn(keys_across)
    values = turn(side_by_side(v_ref))
    frames = ctx_ref.shape[2]
    parts = block // frames
    scale = HEAD_DIM**-0.5
    for step in range(q_ref.shape[0] // parts):
        some = range(step * parts, (step + 1) * parts)
        columns = slice(step * block, (step + 1) * block)
        queries = jnp.concatenate([q_ref[s, 0] for s in some], axis=1)
        context_grad = jnp.concatenate([cg_ref[s].astype(F32) for s in some], axis=1)
        context = jnp.concatenate([ctx_ref[s] for s in some], axis=1)
        scores = jnp.dot(keys, queries, preferred_element_type=F32)
        expo = jnp.where(
            seg_k_ref[...] == seg_q_ref[:, columns], jnp.exp2(scores * (scale * LOG2E)), 0.0
        )
        inverse = 1.0 / jnp.sum(expo, axis=0, keepdims=True)
        accum_g = (context_grad * inverse).astype(BF16)
        correction = jnp.sum(context_grad * context, axis=0, keepdims=True) * inverse
        dots = jnp.dot(values, accum_g, preferred_element_type=F32)
        score_g = (expo * (dots - correction)).astype(BF16)
        query_grad = jnp.dot(keys_across, score_g, preferred_element_type=F32) * scale
        for part, s in enumerate(some):
            dq_ref[s] = query_grad[:, part * frames : (part + 1) * frames].astype(BF16)
        key_grad = lax.dot_general(
            score_g, queries, (((1,), (1,)), ((), ())), preferred_element_type=F32
        )
        value_grad = lax.dot_general(
            expo.astype(BF16), accum_g, (((1,), (1,)), ((), ())), preferred_element_type=F32
        )
        if step == 0:
            dk_sum[...] = key_grad
            dv_sum[...] = value_grad
        else:
            dk_sum[...] += key_grad
            dv_sum[...] += value_grad
    key_total = (dk_sum[...] * scale).T.astype(BF16)
    value_total = dv_sum[...].T.astype(BF16)
    for s in range(dk_ref.shape[0]):
        dk_ref[s] = key_total[:, s * frames : (s + 1) * frames]
        dv_ref[s] = value_total[:, s * frames : (s + 1) * frames]


def head_spec(count, frames, which):
    return pl.BlockSpec((count, 1, HEAD_DIM, frames), lambda h: (0, which, h, 0))


def plain_spec(count, frames):
    return pl.BlockSpec((count, HEAD_DIM, frames), lambda h: (0, h, 0))


def whole_spec(array):
    return pl.BlockSpec(array.shape, lambda h: (0,) * array.ndim)


def attention(mixed, mixed_all, seg_q, seg_k):
    count, _, channels, frames = mixed.shape
    total = mixed_all.shape[0]
    heads = channels // HEAD_DIM
    block = math.gcd(count, 2) * frames
    seg_q, seg_k = seg_q[:, None], seg_k[None]
    pairs = heads * count * frames * total * frames
    return pl.pallas_call(
        lambda *refs: attention_kernel(block, *refs),
        grid=(heads,),
        in_specs=[
            head_spec(count, frames, 0),
            head_spec(total, frames, 1),
            head_spec(total, frames, 2),
            whole_spec(seg_q),
            whole_spec(seg_k),
        ],
        out_specs=plain_spec(count, frames),
        out_shape=jax.ShapeDtypeStruct((count, channels, frames), F32),
        compiler_params=pltpu.CompilerParams(vmem_limit_bytes=VMEM),
        cost_estimate=pl.CostEstimate(
            flops=4 * HEAD_DIM * pairs, bytes_accessed=8 * mixed.size, transcendentals=pairs
        ),
        name="attention",
    )(mixed, mixed_all, mixed_all, seg_q, seg_k)


def attention_back(mixed, mixed_all, context_grad, context, seg_q, seg_k):
    count, _, channels, frames = mixed.shape
    total = mixed_all.shape[0]
    heads = channels // HEAD_DIM
    block = math.gcd(count, 2) * frames
    seg_q, seg_k = seg_q[None], seg_k[:, None]
    pairs = heads * count * frames * total * frames
    return pl.pallas_call(
        lambda *refs: attention_back_kernel(block, *refs),
        grid=(heads,),
        in_specs=[
            head_spec(count, frames, 0),
            head_spec(total, frames, 1),
            head_spec(total, frames, 2),
            plain_spec(count, frames),
            plain_spec(count, frames),
            whole_spec(seg_q),
            whole_spec(seg_k),
        ],
        out_specs=[
            plain_spec(count, frames),
            plain_spec(total, frames),
            plain_spec(total, frames),
        ],
        out_shape=[
            jax.ShapeDtypeStruct((count, channels, frames), BF16),
            jax.ShapeDtypeStruct((total, channels, frames), BF16),
            jax.ShapeDtypeStruct((total, channels, frames), BF16),
        ],
        scratch_shapes=[pltpu.VMEM((total * frames, HEAD_DIM), F32)] * 2,
        compiler_params=pltpu.CompilerParams(vmem_limit_bytes=VMEM),
        cost_estimate=pl.CostEstimate(
            flops=10 * HEAD_DIM * pairs, bytes_accessed=16 * mixed.size, transcendentals=pairs
        ),
        name="attention_back",
    )(mixed, mixed_all, mixed_all, context_grad, context, seg_q, seg_k)


def body(
    features,
    lengths,
    conv_weight,
    feature_gain,
    projection_weight,
    position_weight,
    encoder_gain,
    qkv_weight,
    output_weight,
    attention_gain,
    up_weight,
    down_weight,
    final_gain,
    cotangent,
):
    frames = cotangent.shape[2]
    rows = MICROS * frames
    seqs = lax.axis_size("seq")
    streams = lax.axis_size("fsdp")
    devices = seqs * streams
    me = lax.axis_index("seq")
    stream = lax.axis_index("fsdp")
    both = ("seq", "fsdp")
    group = HEAD_PARTS * MICROS
    outer = seqs // group
    near = [[o * group + i for i in range(group)] for o in range(outer)]
    far = [[o * group + i for o in range(outer)] for i in range(group)]

    def near_swap(blocks):
        return lax.all_to_all(blocks, "seq", 0, 0, axis_index_groups=near)

    def near_sum(blocks):
        place = me % group
        terms = []
        for k in range(group):
            block = lax.dynamic_index_in_dim(blocks, place ^ k, 0, keepdims=False)
            pairs = [(i, i - i % group + (i % group ^ k)) for i in range(seqs)]
            terms.append(lax.ppermute(block, "seq", pairs) if k else block)
        return sum(term.astype(F32) for term in terms)

    front_rows = (conv_weight.shape[0], projection_weight.size // C_CNN)
    gains = jnp.concatenate([feature_gain, encoder_gain, attention_gain, final_gain])
    front = jnp.concatenate(
        [
            conv_weight,
            projection_weight.reshape(-1, C_CNN),
            jnp.pad(gains[None], ((0, 7), (0, C_CNN - gains.size))),
        ],
        axis=0,
    )
    front = lax.all_gather(front, both, axis=0, tiled=False)
    cut = front_rows[0] + front_rows[1]
    conv_full = front[:, : front_rows[0]].reshape(-1, C_CNN)
    projection_full = front[:, front_rows[0] : cut].reshape(C_CNN, D)
    gains_full = front[:, cut, : gains.size]
    feature_n, model_n = feature_gain.size, encoder_gain.size
    feature_scale = gains_full[:, :feature_n].reshape(-1).astype(F32)
    encoder_scale, attention_scale, final_scale = (
        gains_full[:, feature_n + i * model_n : feature_n + (i + 1) * model_n]
        .reshape(-1)
        .astype(F32)
        for i in range(3)
    )

    part = D // HEAD_PARTS
    up_rows = up_weight.shape[0]
    unit_rows = down_weight.shape[0]
    wide = seqs * unit_rows
    up_parts = up_weight.reshape(up_rows, seqs, streams, unit_rows).transpose(2, 0, 1, 3)
    qkv_parts = qkv_weight.reshape(up_rows, 3, streams, part).transpose(2, 0, 1, 3)
    parts = jnp.concatenate(
        [qkv_parts.reshape(streams, up_rows, 3 * part), up_parts.reshape(streams, up_rows, wide)],
        axis=2,
    )
    parts = jnp.concatenate(swap_parts([parts[j] for j in range(streams)], stream), axis=0)
    share = D // group
    own_rows = position_weight.shape[0]
    taps, parts = lax.optimization_barrier((position_weight, parts))
    taps = near_swap(taps.T.reshape(group, share, own_rows))
    if outer > 1:
        taps = lax.all_gather(taps, "seq", axis=0, axis_index_groups=far)
    taps = taps.reshape(outer, group, share, own_rows)
    position_full = (
        jnp.stack(flip(gather_blocks(taps), stream))
        .transpose(3, 1, 2, 0, 4)
        .reshape(share, COARSE, FINE * CG)
        .transpose(1, 0, 2)
    )

    out_parts = output_weight.reshape(up_rows, streams, part).transpose(1, 0, 2)
    quarter = jnp.concatenate(
        [parts[:, : 3 * part], out_parts.reshape(-1, part), parts[:, 3 * part :], down_weight],
        axis=1,
    )
    quarter, front = lax.optimization_barrier((quarter, front))
    quarter = lax.all_gather(quarter, "seq", axis=0, tiled=True)

    ends = jnp.cumsum(lengths[:, 0], axis=-1, dtype=jnp.int32)
    positions = me * frames + jnp.arange(frames + 1, dtype=jnp.int32)
    segments = segment_of(ends, positions)
    same_next = (segments[:, 1:] == segments[:, :-1])[:, :, None]
    pairs = features[:, 0].reshape(MICROS, frames, 2 * C_CNN)
    next_first = shifted(pairs[:, :1, :C_CNN], "seq", -1)
    following = jnp.concatenate([pairs[:, 1:, :C_CNN], next_first], axis=1)
    following = following * same_next.astype(BF16)
    unfolded = jnp.concatenate([pairs, following], axis=2).reshape(rows, 3 * C_CNN)
    before = plain_dot(unfolded, conv_full)
    activated, gate_back = jax.vjp(smooth_gate, before)
    normed, first_norm_back = jax.vjp(norm_rows, activated, feature_scale)
    normed_low = normed.astype(BF16)
    projected = plain_dot(normed_low, projection_full)

    def to_groups(block):
        across = near_swap(block.T.reshape(group, share, rows))
        if outer == 1:
            return across, jnp.zeros((share, MICROS * POS_K), BF16)
        first = across[0].reshape(share, MICROS, frames)[:, :, :HALF]
        last = across[-1].reshape(share, MICROS, frames)[:, :, frames - HALF :]
        edge = [shifted(first, "seq", -group), shifted(last, "seq", group)]
        return across, jnp.concatenate(edge, axis=2).reshape(share, MICROS * POS_K)

    def from_groups(block):
        return near_swap(block).reshape(D, rows).T.astype(F32)

    window, window_edge = to_groups(projected.astype(BF16))
    position = position_conv(window, window_edge, position_full)
    position, quarter = lax.optimization_barrier((position, quarter))
    middle = gather_blocks(quarter[:, : 4 * part])
    qkv_blocks = [block[:, : 3 * part] for block in middle]
    output_full = jnp.stack(flip([block[:, 3 * part :] for block in middle], stream))
    output_full = (
        output_full.reshape(streams, seqs, streams, up_rows, part)
        .transpose(1, 0, 3, 2, 4)
        .reshape(D, D)
    )
    position = from_groups(position)
    feed, position = lax.optimization_barrier((quarter[:, 4 * part :], position))
    feed = gather_blocks(feed)
    up_blocks = [block[:, :wide] for block in feed]
    down_blocks = [block[:, wide:] for block in feed]
    position_act, position_gate_back = jax.vjp(smooth_gate, position)
    encoded, encoder_back = jax.vjp(norm_rows, projected + position_act, encoder_scale)
    encoded_low = encoded.astype(BF16)

    def to_heads(blocks, kinds):
        across = jnp.stack(blocks).reshape(HEAD_PARTS, kinds * part, MICROS, frames)
        across = across.transpose(0, 2, 1, 3).reshape(group, kinds, part, frames)
        return near_swap(across)

    def from_heads(blocks, kinds):
        blocks = near_swap(blocks).reshape(HEAD_PARTS, MICROS, kinds * part, frames)
        blocks = blocks.transpose(0, 2, 1, 3).reshape(HEAD_PARTS, kinds * part, rows)
        return [blocks[k] for k in range(HEAD_PARTS)]

    mixed = [
        lax.dot_general(
            block, encoded_low, (((0,), (1,)), ((), ())), preferred_element_type=F32
        ).astype(BF16)
        for block in qkv_blocks
    ]
    mixed_heads = to_heads(mixed, 3)
    if outer > 1:
        mixed_all = lax.all_gather(
            mixed_heads, "seq", axis=0, tiled=True, axis_index_groups=far
        )
    else:
        mixed_all = mixed_heads
    micro_ends = lax.dynamic_index_in_dim(ends, me % MICROS, 0, keepdims=False)
    seg_all = segment_of(micro_ends, jnp.arange(seqs * frames, dtype=jnp.int32))
    seg_own = lax.dynamic_slice_in_dim(
        seg_all, (me // group) * group * frames, group * frames, 0
    )
    context_heads = attention(mixed_heads, mixed_all, seg_own, seg_all)
    context_low = from_heads(context_heads.astype(BF16)[:, None], 1)
    context_low = jnp.concatenate(flip(context_low, stream), axis=0).T
    branch = plain_dot(context_low, output_full)
    settled, attention_norm_back = jax.vjp(norm_rows, encoded + branch, attention_scale)

    settled_low = settled.astype(BF16)
    hidden_low, hidden_backs = [], []
    fed = 0.0
    for up_block, down_block in zip(up_blocks, down_blocks):
        hidden, hidden_back = jax.vjp(smooth_gate, plain_dot(settled_low, up_block))
        hidden_low.append(hidden.astype(BF16))
        hidden_backs.append(hidden_back)
        fed += plain_dot(hidden_low[-1], down_block)
    block_out, final_back = jax.vjp(norm_rows, settled + fed, final_scale)
    sum_grad, final_grad = final_back(cotangent[:, 0].reshape(rows, D).astype(F32))
    fed_low = sum_grad.astype(BF16)
    settled_grad = sum_grad
    feed_grads = []
    for k in range(streams):
        (up_raw,) = hidden_backs[k](outer_dot(fed_low, down_blocks[k]))
        up_low = up_raw.astype(BF16)
        settled_grad += outer_dot(up_low, up_blocks[k])
        feed_grads.append(
            jnp.concatenate(
                [
                    inner_dot(settled_low, up_low).astype(BF16),
                    inner_dot(hidden_low[k], fed_low).astype(BF16),
                ],
                axis=1,
            )
        )
    mid_grad, attention_grad = attention_norm_back(settled_grad)
    branch_low = mid_grad.astype(BF16)
    branch_low, feed_grads = lax.optimization_barrier((branch_low, feed_grads))
    output_grad = inner_dot(context_low, branch_low).astype(BF16)
    output_grad = (
        output_grad.reshape(seqs, streams, up_rows, streams, part)
        .transpose(1, 0, 3, 2, 4)
        .reshape(streams, D, part)
    )
    output_grads = flip([output_grad[j] for j in range(streams)], stream)

    context_grad = lax.dot_general(
        output_full, branch_low, (((1,), (1,)), ((), ())), preferred_element_type=F32
    ).astype(BF16)
    context_grad = context_grad.reshape(HEAD_PARTS, part, rows)
    context_grad = flip([context_grad[j] for j in range(HEAD_PARTS)], stream)
    context_grad, feed_pairs = lax.optimization_barrier(
        (to_heads(context_grad, 1)[:, 0], pair_sums(feed_grads))
    )
    feed_sum = low_sum(feed_pairs[0], swapped(feed_pairs[1], 2))
    dq, dk, dv = attention_back(
        mixed_heads, mixed_all, context_grad, context_heads, seg_own, seg_all
    )
    if outer > 1:
        dk, dv = (
            lax.psum_scatter(
                grad, "seq", scatter_dimension=0, tiled=True, axis_index_groups=far
            )
            for grad in (dk, dv)
        )
    mixed_g = from_heads(jnp.stack([dq, dk, dv], axis=1), 3)
    mixed_g, feed_sum = lax.optimization_barrier((mixed_g, feed_sum))
    encoded_grad = mid_grad
    for block, block_g in zip(qkv_blocks, mixed_g):
        encoded_grad += lax.dot_general(
            block_g, block, (((0,), (1,)), ((), ())), preferred_element_type=F32
        )
    middle_grads = [
        jnp.concatenate(
            [
                lax.dot_general(
                    encoded_low, block_g, (((0,), (1,)), ((), ())), preferred_element_type=F32
                ).astype(BF16),
                output_block,
            ],
            axis=1,
        )
        for block_g, output_block in zip(mixed_g, output_grads)
    ]

    joined_grad, encoder_grad = encoder_back(encoded_grad)
    (position_grad,) = position_gate_back(joined_grad)
    position_low = position_grad.astype(BF16)
    grad_window, grad_edge = to_groups(position_low)
    projected_back, taps_grad = position_back(
        window, window_edge, grad_window, grad_edge, position_full
    )
    quarter_sum = jnp.concatenate([reduce_blocks(middle_grads), feed_sum], axis=1)
    projected_back, quarter_sum = lax.optimization_barrier((projected_back, quarter_sum))
    quarter_shard = lax.psum_scatter(quarter_sum, "seq", scatter_dimension=0, tiled=True)

    projected_back, taps_grad = lax.optimization_barrier((from_groups(projected_back), taps_grad))
    projected_grad = (joined_grad + projected_back).astype(BF16)
    projection_grad = inner_dot(normed_low, projected_grad).astype(BF16)
    activated_grad, feature_grad = first_norm_back(outer_dot(projected_grad, projection_full))
    (before_grad,) = gate_back(activated_grad)
    before_low = before_grad.astype(BF16)
    conv_grad = inner_dot(unfolded, before_low).astype(BF16)
    unfolded_grad = outer_dot(before_low, conv_full).reshape(MICROS, frames, 3 * C_CNN)
    following_grad = unfolded_grad[:, :, 2 * C_CNN :] * same_next.astype(F32)
    carried = shifted(following_grad[:, frames - 1 :], "seq", 1)
    even_grad = unfolded_grad[:, :, :C_CNN] + jnp.concatenate(
        [carried, following_grad[:, :-1]], axis=1
    )
    input_grad = jnp.concatenate([even_grad, unfolded_grad[:, :, C_CNN : 2 * C_CNN]], axis=2)
    input_grad = input_grad.reshape(MICROS, 1, 2 * frames, C_CNN)

    gain_grads = jnp.concatenate(
        [
            grad.reshape(devices, -1)
            for grad in (feature_grad, encoder_grad, attention_grad, final_grad)
        ],
        axis=1,
    ).astype(BF16)
    gain_grads = jnp.pad(gain_grads[:, None], ((0, 0), (0, 7), (0, D - gains.size)))
    front_grads = jnp.concatenate(
        [conv_grad.reshape(devices, -1, D), projection_grad.reshape(devices, -1, D), gain_grads],
        axis=1,
    )
    front_grads = front_grads.reshape(seqs, streams, -1, D)
    front_sum = reduce_blocks(flip([front_grads[:, j] for j in range(streams)], stream))
    front_shard = near_sum(front_sum.reshape(outer, group, -1, D).transpose(1, 0, 2, 3))
    if outer > 1:
        front_shard = lax.psum_scatter(
            front_shard, "seq", scatter_dimension=0, axis_index_groups=far
        )
    else:
        front_shard = front_shard[0]

    taps_grad = (
        taps_grad.transpose(1, 0, 2)
        .reshape(share, outer, group, streams, own_rows)
        .transpose(3, 1, 2, 0, 4)
    )
    taps_grad = reduce_blocks(flip([taps_grad[j] for j in range(streams)], stream))
    if outer > 1:
        taps_grad = lax.psum_scatter(
            taps_grad, "seq", scatter_dimension=0, axis_index_groups=far
        )
    else:
        taps_grad = taps_grad[0]
    position_shard = near_swap(taps_grad).reshape(D, own_rows).T.astype(F32)

    out_cut = 4 * part + wide
    parts = jnp.concatenate([quarter_shard[:, : 3 * part], quarter_shard[:, 4 * part : out_cut]], 1)
    parts = parts.reshape(streams, up_rows, -1)
    parts = jnp.stack(swap_parts([parts[j] for j in range(streams)], stream)).astype(F32)
    qkv_shard = (
        parts[:, :, : 3 * part]
        .reshape(streams, up_rows, 3, part)
        .transpose(1, 2, 0, 3)
        .reshape(up_rows, -1)
    )
    up_shard = (
        parts[:, :, 3 * part :]
        .reshape(streams, up_rows, seqs, unit_rows)
        .transpose(1, 2, 0, 3)
        .reshape(up_rows, -1)
    )
    output_shard = (
        quarter_shard[:, 3 * part : 4 * part]
        .reshape(streams, up_rows, part)
        .transpose(1, 0, 2)
        .reshape(up_rows, D)
        .astype(F32)
    )
    down_shard = quarter_shard[:, out_cut:].astype(F32)
    cuts = [conv_weight.size // D]
    cuts.append(cuts[0] + projection_weight.shape[0])
    conv_shard = front_shard[: cuts[0]].reshape(-1, C_CNN)
    projection_shard = front_shard[cuts[0] : cuts[1]]
    gain_row = front_shard[cuts[1]]
    gain_shards = [
        gain_row[:feature_n],
        *(gain_row[feature_n + i * model_n : feature_n + (i + 1) * model_n] for i in range(3)),
    ]
    return (
        block_out.reshape(MICROS, 1, frames, D),
        input_grad,
        conv_shard,
        gain_shards[0],
        projection_shard,
        position_shard,
        gain_shards[1],
        qkv_shard,
        output_shard,
        gain_shards[2],
        up_shard,
        down_shard,
        gain_shards[3],
    )


def solution(mesh):
    weight, gain = P(("seq", "fsdp"), None), P(("seq", "fsdp"))
    rows = P(None, "fsdp", "seq", None)
    in_specs = (
        rows, P(None, "fsdp", None), weight, gain, weight, weight, gain, weight, weight, gain,
        weight, weight, gain, rows,
    )
    out_specs = (
        rows, rows, weight, gain, weight, weight, gain, weight, weight, gain, weight, weight, gain,
    )
    return jax.shard_map(body, mesh=mesh, in_specs=in_specs, out_specs=out_specs, check_vma=False)
```

```python
import math

import jax
import jax.numpy as jnp
from jax import lax
from jax.experimental import pallas as pl
from jax.experimental.pallas import tpu as pltpu
from jax.sharding import PartitionSpec as P

D = 768
HEADS = 12
C_CNN = 512
POS_K = 128
GROUPS = 16
HEAD_DIM = 64
CG = 48
HALF = POS_K // 2
FINE = 16
COARSE = POS_K // FINE
HEAD_PARTS = 4
MICROS = 2
LOG2E = 1.4426950408889634
VMEM = 60 * 1024 * 1024

NORM_EPS = 1e-05
F32 = jnp.float32
BF16 = jnp.bfloat16


def shifted(array, axis, by):
    peers = lax.axis_size(axis)
    pairs = [(i, i + by) for i in range(peers) if 0 <= i + by < peers]
    return lax.ppermute(array, axis, pairs)


def flip(blocks, me):
    count = len(blocks)
    return [lax.select_n(me, *(blocks[m ^ k] for m in range(count))) for k in range(count)]


def swapped(array, k):
    count = lax.axis_size("fsdp")
    return lax.ppermute(array, "fsdp", [(i, i ^ k) for i in range(count)])


def swap_parts(parts, me):
    ordered = flip(parts, me)
    return flip([ordered[0]] + [swapped(ordered[k], k) for k in range(1, 4)], me)


def gather_blocks(block):
    over_x = swapped(block, 2)
    return [block, swapped(block, 1), over_x, swapped(over_x, 1)]


def low_sum(*terms):
    return sum(term.astype(F32) for term in terms).astype(BF16)


def pair_sums(blocks):
    return low_sum(blocks[0], swapped(blocks[1], 1)), low_sum(blocks[2], swapped(blocks[3], 1))


def reduce_blocks(blocks):
    kept, sent = pair_sums(blocks)
    return low_sum(kept, swapped(sent, 2))


def norm_rows(values, scales):
    center = values - jnp.mean(values, axis=-1, keepdims=True)
    spread = jnp.mean(center * center, axis=-1, keepdims=True)
    return center * lax.rsqrt(spread + NORM_EPS) * scales


def smooth_gate(values):
    return jax.nn.gelu(values, approximate=False)


def segment_of(utterance_ends, positions):
    return jnp.sum(
        (utterance_ends[..., None, :] <= positions[:, None]).astype(jnp.int32),
        axis=-1,
        dtype=jnp.int32,
    )


def plain_dot(left, right):
    return jnp.dot(left, right, preferred_element_type=F32)


def inner_dot(left, right):
    return lax.dot_general(left, right, (((0,), (0,)), ((), ())), preferred_element_type=F32)


def outer_dot(left, right):
    return lax.dot_general(left, right, (((1,), (1,)), ((), ())), preferred_element_type=F32)


def lane_roll(value, shift):
    shift = shift % value.shape[1]
    return pltpu.roll(value, shift, 1) if shift else value


def joined(ref, edge_ref, micro, frames):
    columns = slice(micro * frames, (micro + 1) * frames)
    edge = slice(micro * POS_K, (micro + 1) * POS_K)
    blocks = [ref[s, :, columns] for s in range(ref.shape[0])] + [edge_ref[:, edge]]
    return jnp.concatenate(blocks, axis=1).astype(F32)


def fine_shifts(x_ref, edge_ref, fine_ref, frames, span):
    for m in range(MICROS):
        x = joined(x_ref, edge_ref, m, frames)
        for fine in range(FINE):
            fine_ref[fine * CG : (fine + 1) * CG, m * span : (m + 1) * span] = lane_roll(
                x, HALF - fine
            ).astype(BF16)


def store_frames(out_ref, micro, frames, total):
    for s in range(out_ref.shape[0]):
        out_ref[s, :, micro * frames : (micro + 1) * frames] = total[
            :, s * frames : (s + 1) * frames
        ].astype(BF16)


def position_kernel(span, frames, x_ref, edge_ref, w_ref, out_ref, fine_ref):
    fine_shifts(x_ref, edge_ref, fine_ref, frames, span)
    weights = w_ref[...].reshape(COARSE * CG, FINE * CG)
    for m in range(MICROS):
        terms = jnp.dot(
            weights, fine_ref[:, m * span : (m + 1) * span], preferred_element_type=F32
        )
        total = terms[:CG]
        for coarse in range(1, COARSE):
            total += lane_roll(terms[coarse * CG : (coarse + 1) * CG], -FINE * coarse)
        store_frames(out_ref, m, frames, total)


def position_back_kernel(
    span, frames, x_ref, x_edge_ref, g_ref, g_edge_ref, w_ref, dx_ref, dw_ref,
    fine_ref, coarse_ref, own_ref,
):
    fine_shifts(x_ref, x_edge_ref, fine_ref, frames, span)
    column = lax.broadcasted_iota(jnp.int32, (CG, span), 1)
    for m in range(MICROS):
        columns = slice(m * span, (m + 1) * span)
        g = joined(g_ref, g_edge_ref, m, frames)
        own = jnp.where(column < span - POS_K, g, 0.0)
        for coarse in range(COARSE):
            rows = slice(coarse * CG, (coarse + 1) * CG)
            back = FINE * (COARSE - 1 - coarse)
            coarse_ref[rows, columns] = lane_roll(g, HALF - back).astype(BF16)
            own_ref[rows, columns] = lane_roll(own, FINE * coarse).astype(BF16)
    weights = w_ref[...].reshape(COARSE * CG, FINE * CG)
    turned = weights.astype(F32).T.astype(BF16)
    for m in range(MICROS):
        terms = jnp.dot(
            turned, coarse_ref[:, m * span : (m + 1) * span], preferred_element_type=F32
        )
        total = lane_roll(terms[:CG], -FINE)
        for fine in range(1, FINE):
            total += lane_roll(terms[fine * CG : (fine + 1) * CG], fine - FINE)
        store_frames(dx_ref, m, frames, total)
    grad = lax.dot_general(
        own_ref[...], fine_ref[...], (((1,), (1,)), ((), ())), preferred_element_type=F32
    )
    dw_ref[...] = grad.astype(BF16).reshape(COARSE, CG, FINE * CG)


def group_specs(count, columns):
    wide = pl.BlockSpec((count, CG, columns), lambda g: (0, g, 0))
    edge = pl.BlockSpec((CG, MICROS * POS_K), lambda g: (g, 0))
    weight = pl.BlockSpec((COARSE, CG, FINE * CG), lambda g: (0, g, 0))
    return wide, edge, weight


def position_conv(x, edge, weights):
    count, channels, columns = x.shape
    frames = columns // MICROS
    span = count * frames + POS_K
    groups = channels // CG
    wide, edge_spec, weight = group_specs(count, columns)
    flops = 2 * groups * MICROS * span * COARSE * CG * FINE * CG
    return pl.pallas_call(
        lambda *refs: position_kernel(span, frames, *refs),
        grid=(groups,),
        in_specs=[wide, edge_spec, weight],
        out_specs=wide,
        out_shape=jax.ShapeDtypeStruct(x.shape, BF16),
        scratch_shapes=[pltpu.VMEM((FINE * CG, MICROS * span), BF16)],
        compiler_params=pltpu.CompilerParams(vmem_limit_bytes=VMEM),
        cost_estimate=pl.CostEstimate(
            flops=flops, bytes_accessed=2 * (2 * x.size + weights.size), transcendentals=0
        ),
        name="position_conv",
    )(x, edge, weights)


def position_back(x, x_edge, grad, grad_edge, weights):
    count, channels, columns = x.shape
    frames = columns // MICROS
    span = count * frames + POS_K
    groups = channels // CG
    wide, edge_spec, weight = group_specs(count, columns)
    flops = 4 * groups * MICROS * span * COARSE * CG * FINE * CG
    return pl.pallas_call(
        lambda *refs: position_back_kernel(span, frames, *refs),
        grid=(groups,),
        in_specs=[wide, edge_spec, wide, edge_spec, weight],
        out_specs=[wide, weight],
        out_shape=[
            jax.ShapeDtypeStruct(x.shape, BF16),
            jax.ShapeDtypeStruct(weights.shape, BF16),
        ],
        scratch_shapes=[
            pltpu.VMEM((FINE * CG, MICROS * span), BF16),
            pltpu.VMEM((COARSE * CG, MICROS * span), BF16),
            pltpu.VMEM((COARSE * CG, MICROS * span), BF16),
        ],
        compiler_params=pltpu.CompilerParams(vmem_limit_bytes=VMEM),
        cost_estimate=pl.CostEstimate(
            flops=flops, bytes_accessed=2 * (3 * x.size + 2 * weights.size), transcendentals=0
        ),
        name="position_back",
    )(x, x_edge, grad, grad_edge, weights)


def side_by_side(ref):
    return jnp.concatenate([ref[s, 0] for s in range(ref.shape[0])], axis=1)


def turn(value):
    return value.astype(F32).T.astype(BF16)


def attention_kernel(block, q_ref, k_ref, v_ref, seg_q_ref, seg_k_ref, out_ref):
    queries = turn(side_by_side(q_ref))
    keys = side_by_side(k_ref)
    values = side_by_side(v_ref)
    frames = out_ref.shape[2]
    factor = HEAD_DIM**-0.5 * LOG2E
    for first in range(0, queries.shape[0], block):
        rows = slice(first, first + block)
        scores = jnp.dot(queries[rows], keys, preferred_element_type=F32)
        expo = jnp.where(seg_q_ref[rows] == seg_k_ref[...], jnp.exp2(scores * factor), 0.0)
        weight_sum = jnp.sum(expo, axis=1, keepdims=True)
        accum = lax.dot_general(
            expo.astype(BF16), values, (((1,), (1,)), ((), ())), preferred_element_type=F32
        )
        context = (accum / weight_sum).T
        for part in range(block // frames):
            out_ref[first // frames + part] = context[:, part * frames : (part + 1) * frames]


def attention_back_kernel(
    block, q_ref, k_ref, v_ref, cg_ref, ctx_ref, seg_q_ref, seg_k_ref,
    dq_ref, dk_ref, dv_ref, dk_sum, dv_sum,
):
    keys_across = side_by_side(k_ref)
    keys = turn(keys_across)
    values = turn(side_by_side(v_ref))
    frames = ctx_ref.shape[2]
    parts = block // frames
    scale = HEAD_DIM**-0.5
    for step in range(q_ref.shape[0] // parts):
        some = range(step * parts, (step + 1) * parts)
        columns = slice(step * block, (step + 1) * block)
        queries = jnp.concatenate([q_ref[s, 0] for s in some], axis=1)
        context_grad = jnp.concatenate([cg_ref[s].astype(F32) for s in some], axis=1)
        context = jnp.concatenate([ctx_ref[s] for s in some], axis=1)
        scores = jnp.dot(keys, queries, preferred_element_type=F32)
        expo = jnp.where(
            seg_k_ref[...] == seg_q_ref[:, columns], jnp.exp2(scores * (scale * LOG2E)), 0.0
        )
        inverse = 1.0 / jnp.sum(expo, axis=0, keepdims=True)
        accum_g = (context_grad * inverse).astype(BF16)
        correction = jnp.sum(context_grad * context, axis=0, keepdims=True) * inverse
        dots = jnp.dot(values, accum_g, preferred_element_type=F32)
        score_g = (expo * (dots - correction)).astype(BF16)
        query_grad = jnp.dot(keys_across, score_g, preferred_element_type=F32) * scale
        for part, s in enumerate(some):
            dq_ref[s] = query_grad[:, part * frames : (part + 1) * frames].astype(BF16)
        key_grad = lax.dot_general(
            score_g, queries, (((1,), (1,)), ((), ())), preferred_element_type=F32
        )
        value_grad = lax.dot_general(
            expo.astype(BF16), accum_g, (((1,), (1,)), ((), ())), preferred_element_type=F32
        )
        if step == 0:
            dk_sum[...] = key_grad
            dv_sum[...] = value_grad
        else:
            dk_sum[...] += key_grad
            dv_sum[...] += value_grad
    key_total = (dk_sum[...] * scale).T.astype(BF16)
    value_total = dv_sum[...].T.astype(BF16)
    for s in range(dk_ref.shape[0]):
        dk_ref[s] = key_total[:, s * frames : (s + 1) * frames]
        dv_ref[s] = value_total[:, s * frames : (s + 1) * frames]


def head_spec(count, frames, which):
    return pl.BlockSpec((count, 1, HEAD_DIM, frames), lambda h: (0, which, h, 0))


def plain_spec(count, frames):
    return pl.BlockSpec((count, HEAD_DIM, frames), lambda h: (0, h, 0))


def whole_spec(array):
    return pl.BlockSpec(array.shape, lambda h: (0,) * array.ndim)


def attention(mixed, mixed_all, seg_q, seg_k):
    count, _, channels, frames = mixed.shape
    total = mixed_all.shape[0]
    heads = channels // HEAD_DIM
    block = math.gcd(count, 2) * frames
    seg_q, seg_k = seg_q[:, None], seg_k[None]
    pairs = heads * count * frames * total * frames
    return pl.pallas_call(
        lambda *refs: attention_kernel(block, *refs),
        grid=(heads,),
        in_specs=[
            head_spec(count, frames, 0),
            head_spec(total, frames, 1),
            head_spec(total, frames, 2),
            whole_spec(seg_q),
            whole_spec(seg_k),
        ],
        out_specs=plain_spec(count, frames),
        out_shape=jax.ShapeDtypeStruct((count, channels, frames), F32),
        compiler_params=pltpu.CompilerParams(vmem_limit_bytes=VMEM),
        cost_estimate=pl.CostEstimate(
            flops=4 * HEAD_DIM * pairs, bytes_accessed=8 * mixed.size, transcendentals=pairs
        ),
        name="attention",
    )(mixed, mixed_all, mixed_all, seg_q, seg_k)


def attention_back(mixed, mixed_all, context_grad, context, seg_q, seg_k):
    count, _, channels, frames = mixed.shape
    total = mixed_all.shape[0]
    heads = channels // HEAD_DIM
    block = math.gcd(count, 2) * frames
    seg_q, seg_k = seg_q[None], seg_k[:, None]
    pairs = heads * count * frames * total * frames
    return pl.pallas_call(
        lambda *refs: attention_back_kernel(block, *refs),
        grid=(heads,),
        in_specs=[
            head_spec(count, frames, 0),
            head_spec(total, frames, 1),
            head_spec(total, frames, 2),
            plain_spec(count, frames),
            plain_spec(count, frames),
            whole_spec(seg_q),
            whole_spec(seg_k),
        ],
        out_specs=[
            plain_spec(count, frames),
            plain_spec(total, frames),
            plain_spec(total, frames),
        ],
        out_shape=[
            jax.ShapeDtypeStruct((count, channels, frames), BF16),
            jax.ShapeDtypeStruct((total, channels, frames), BF16),
            jax.ShapeDtypeStruct((total, channels, frames), BF16),
        ],
        scratch_shapes=[pltpu.VMEM((total * frames, HEAD_DIM), F32)] * 2,
        compiler_params=pltpu.CompilerParams(vmem_limit_bytes=VMEM),
        cost_estimate=pl.CostEstimate(
            flops=10 * HEAD_DIM * pairs, bytes_accessed=16 * mixed.size, transcendentals=pairs
        ),
        name="attention_back",
    )(mixed, mixed_all, mixed_all, context_grad, context, seg_q, seg_k)


def body(
    features,
    lengths,
    conv_weight,
    feature_gain,
    projection_weight,
    position_weight,
    encoder_gain,
    qkv_weight,
    output_weight,
    attention_gain,
    up_weight,
    down_weight,
    final_gain,
    cotangent,
):
    frames = cotangent.shape[2]
    rows = MICROS * frames
    seqs = lax.axis_size("seq")
    streams = lax.axis_size("fsdp")
    devices = seqs * streams
    me = lax.axis_index("seq")
    stream = lax.axis_index("fsdp")
    both = ("seq", "fsdp")
    group = HEAD_PARTS * MICROS
    outer = seqs // group
    near = [[o * group + i for i in range(group)] for o in range(outer)]
    far = [[o * group + i for o in range(outer)] for i in range(group)]

    def near_swap(blocks):
        return lax.all_to_all(blocks, "seq", 0, 0, axis_index_groups=near)

    def seq_sum(blocks):
        blocks = near_swap(blocks.reshape(outer, group, -1, D).transpose(1, 0, 2, 3))
        total = jnp.sum(blocks.astype(F32), axis=0)
        if outer == 1:
            return total[0]
        return lax.psum_scatter(total, "seq", scatter_dimension=0, axis_index_groups=far)

    def near_gather(block, again):
        blocks = [block]
        for k in range(1, group):
            pairs = [(i, i - i % group + (i % group ^ k)) for i in range(seqs)]
            blocks.append(lax.ppermute(block if k < 5 else again, "seq", pairs))
        return jnp.stack(flip(blocks, me % group))

    front_rows = (conv_weight.shape[0], projection_weight.size // C_CNN)
    gains = jnp.concatenate([feature_gain, encoder_gain, attention_gain, final_gain])
    front = jnp.concatenate(
        [
            conv_weight,
            projection_weight.reshape(-1, C_CNN),
            jnp.pad(gains[None], ((0, 7), (0, C_CNN - gains.size))),
        ],
        axis=0,
    )
    part = D // HEAD_PARTS
    up_rows = up_weight.shape[0]
    unit_rows = down_weight.shape[0]
    wide = seqs * unit_rows
    up_parts = up_weight.reshape(up_rows, seqs, streams, unit_rows).transpose(2, 0, 1, 3)
    qkv_parts = qkv_weight.reshape(up_rows, 3, streams, part).transpose(2, 0, 1, 3)
    parts = jnp.concatenate(
        [qkv_parts.reshape(streams, up_rows, 3 * part), up_parts.reshape(streams, up_rows, wide)],
        axis=2,
    )
    parts = jnp.concatenate(swap_parts([parts[j] for j in range(streams)], stream), axis=0)
    front_again, parts = lax.optimization_barrier((front, parts))
    front_near = near_gather(front, front_again)
    front = front_near
    if outer > 1:
        front = lax.all_gather(front, "seq", axis=0, tiled=True, axis_index_groups=far)
    front = jnp.stack(flip(gather_blocks(front), stream), axis=1)
    front = front.reshape(devices, -1, C_CNN)
    cut = front_rows[0] + front_rows[1]
    conv_full = front[:, : front_rows[0]].reshape(-1, C_CNN)
    projection_full = front[:, front_rows[0] : cut].reshape(C_CNN, D)
    gains_full = front[:, cut, : gains.size]
    feature_n, model_n = feature_gain.size, encoder_gain.size
    feature_scale = gains_full[:, :feature_n].reshape(-1).astype(F32)
    encoder_scale, attention_scale, final_scale = (
        gains_full[:, feature_n + i * model_n : feature_n + (i + 1) * model_n]
        .reshape(-1)
        .astype(F32)
        for i in range(3)
    )

    share = D // group
    own_rows = position_weight.shape[0]
    taps, front_near = lax.optimization_barrier((position_weight, front_near))
    taps = near_swap(taps.T.reshape(group, share, own_rows))
    if outer > 1:
        taps = lax.all_gather(taps, "seq", axis=0, axis_index_groups=far)
    taps = taps.reshape(outer, group, share, own_rows)
    position_full = (
        jnp.stack(flip(gather_blocks(taps), stream))
        .transpose(3, 1, 2, 0, 4)
        .reshape(share, COARSE, FINE * CG)
        .transpose(1, 0, 2)
    )

    out_parts = output_weight.reshape(up_rows, streams, part).transpose(1, 0, 2)
    quarter = jnp.concatenate(
        [parts[:, : 3 * part], out_parts.reshape(-1, part), parts[:, 3 * part :], down_weight],
        axis=1,
    )
    quarter = lax.all_gather(quarter, "seq", axis=0, tiled=True)

    ends = jnp.cumsum(lengths[:, 0], axis=-1, dtype=jnp.int32)
    positions = me * frames + jnp.arange(frames + 1, dtype=jnp.int32)
    segments = segment_of(ends, positions)
    same_next = (segments[:, 1:] == segments[:, :-1])[:, :, None]
    pairs = features[:, 0].reshape(MICROS, frames, 2 * C_CNN)
    next_first = shifted(pairs[:, :1, :C_CNN], "seq", -1)
    following = jnp.concatenate([pairs[:, 1:, :C_CNN], next_first], axis=1)
    following = following * same_next.astype(BF16)
    unfolded = jnp.concatenate([pairs, following], axis=2).reshape(rows, 3 * C_CNN)
    before = plain_dot(unfolded, conv_full)
    activated, gate_back = jax.vjp(smooth_gate, before)
    normed, first_norm_back = jax.vjp(norm_rows, activated, feature_scale)
    normed_low = normed.astype(BF16)
    projected = plain_dot(normed_low, projection_full)

    def to_groups(block):
        across = near_swap(block.T.reshape(group, share, rows))
        if outer == 1:
            return across, jnp.zeros((share, MICROS * POS_K), BF16)
        first = across[0].reshape(share, MICROS, frames)[:, :, :HALF]
        last = across[-1].reshape(share, MICROS, frames)[:, :, frames - HALF :]
        edge = [shifted(first, "seq", -group), shifted(last, "seq", group)]
        return across, jnp.concatenate(edge, axis=2).reshape(share, MICROS * POS_K)

    def from_groups(block):
        return near_swap(block).reshape(D, rows).T.astype(F32)

    window, window_edge = to_groups(projected.astype(BF16))
    position = position_conv(window, window_edge, position_full)
    position, quarter = lax.optimization_barrier((position, quarter))
    middle = gather_blocks(quarter[:, : 4 * part])
    qkv_blocks = [block[:, : 3 * part] for block in middle]
    output_full = jnp.stack(flip([block[:, 3 * part :] for block in middle], stream))
    output_full = (
        output_full.reshape(streams, seqs, streams, up_rows, part)
        .transpose(1, 0, 3, 2, 4)
        .reshape(HEAD_PARTS, part, D)
    )
    output_full = jnp.concatenate(flip([output_full[j] for j in range(HEAD_PARTS)], stream))
    position = from_groups(position)
    feed, position = lax.optimization_barrier((quarter[:, 4 * part :], position))
    feed = gather_blocks(feed)
    up_blocks = [block[:, :wide] for block in feed]
    down_blocks = [block[:, wide:] for block in feed]
    position_act, position_gate_back = jax.vjp(smooth_gate, position)
    encoded, encoder_back = jax.vjp(norm_rows, projected + position_act, encoder_scale)
    encoded_low = encoded.astype(BF16)

    def to_heads(blocks, kinds):
        across = jnp.stack(blocks) if isinstance(blocks, list) else blocks
        across = across.reshape(HEAD_PARTS, kinds * part, MICROS, frames)
        across = across.transpose(0, 2, 1, 3).reshape(group, kinds, part, frames)
        return near_swap(across)

    def from_heads(blocks, kinds):
        blocks = near_swap(blocks).reshape(HEAD_PARTS, MICROS, kinds * part, frames)
        blocks = blocks.transpose(0, 2, 1, 3).reshape(HEAD_PARTS, kinds * part, rows)
        return [blocks[k] for k in range(HEAD_PARTS)]

    mixed = [
        lax.dot_general(
            block, encoded_low, (((0,), (1,)), ((), ())), preferred_element_type=F32
        ).astype(BF16)
        for block in qkv_blocks
    ]
    mixed_heads = to_heads(mixed, 3)
    if outer > 1:
        mixed_all = lax.all_gather(
            mixed_heads, "seq", axis=0, tiled=True, axis_index_groups=far
        )
    else:
        mixed_all = mixed_heads
    micro_ends = lax.dynamic_index_in_dim(ends, me % MICROS, 0, keepdims=False)
    seg_all = segment_of(micro_ends, jnp.arange(seqs * frames, dtype=jnp.int32))
    seg_own = lax.dynamic_slice_in_dim(
        seg_all, (me // group) * group * frames, group * frames, 0
    )
    context_heads = attention(mixed_heads, mixed_all, seg_own, seg_all)
    context_low = from_heads(context_heads.astype(BF16)[:, None], 1)
    context_low = jnp.concatenate(context_low, axis=0).T
    branch = plain_dot(context_low, output_full)
    settled, attention_norm_back = jax.vjp(norm_rows, encoded + branch, attention_scale)

    settled_low = settled.astype(BF16)
    hidden_low, hidden_backs = [], []
    fed = 0.0
    for up_block, down_block in zip(up_blocks, down_blocks):
        hidden, hidden_back = jax.vjp(smooth_gate, plain_dot(settled_low, up_block))
        hidden_low.append(hidden.astype(BF16))
        hidden_backs.append(hidden_back)
        fed += plain_dot(hidden_low[-1], down_block)
    block_out, final_back = jax.vjp(norm_rows, settled + fed, final_scale)
    sum_grad, final_grad = final_back(cotangent[:, 0].reshape(rows, D).astype(F32))
    fed_low = sum_grad.astype(BF16)
    settled_grad = sum_grad
    feed_grads = []
    for k in range(streams):
        (up_raw,) = hidden_backs[k](outer_dot(fed_low, down_blocks[k]))
        up_low = up_raw.astype(BF16)
        settled_grad += outer_dot(up_low, up_blocks[k])
        feed_grads.append(
            jnp.concatenate(
                [
                    inner_dot(settled_low, up_low).astype(BF16),
                    inner_dot(hidden_low[k], fed_low).astype(BF16),
                ],
                axis=1,
            )
        )
    mid_grad, attention_grad = attention_norm_back(settled_grad)
    branch_low = mid_grad.astype(BF16)
    branch_low, feed_grads = lax.optimization_barrier((branch_low, feed_grads))
    output_grad = inner_dot(context_low, branch_low).astype(BF16)
    output_grad = output_grad.reshape(HEAD_PARTS, part, D)
    output_grad = jnp.stack(flip([output_grad[j] for j in range(HEAD_PARTS)], stream))
    output_grad = (
        output_grad.reshape(seqs, streams, up_rows, streams, part)
        .transpose(1, 0, 3, 2, 4)
        .reshape(streams, D, part)
    )
    output_grads = flip([output_grad[j] for j in range(streams)], stream)

    context_grad = lax.dot_general(
        output_full, branch_low, (((1,), (1,)), ((), ())), preferred_element_type=F32
    ).astype(BF16)
    context_grad = context_grad.reshape(HEAD_PARTS, part, rows)
    context_grad, feed_pairs = lax.optimization_barrier(
        (to_heads(context_grad, 1)[:, 0], pair_sums(feed_grads))
    )
    feed_sum = low_sum(feed_pairs[0], swapped(feed_pairs[1], 2))
    dq, dk, dv = attention_back(
        mixed_heads, mixed_all, context_grad, context_heads, seg_own, seg_all
    )
    if outer > 1:
        dk, dv = (
            lax.psum_scatter(
                grad, "seq", scatter_dimension=0, tiled=True, axis_index_groups=far
            )
            for grad in (dk, dv)
        )
    mixed_g = from_heads(jnp.stack([dq, dk, dv], axis=1), 3)
    mixed_g, feed_sum = lax.optimization_barrier((mixed_g, feed_sum))
    feed_shard = lax.psum_scatter(feed_sum, "seq", scatter_dimension=0, tiled=True)
    encoded_grad = mid_grad
    for block, block_g in zip(qkv_blocks, mixed_g):
        encoded_grad += lax.dot_general(
            block_g, block, (((0,), (1,)), ((), ())), preferred_element_type=F32
        )
    middle_grads = [
        jnp.concatenate(
            [
                lax.dot_general(
                    encoded_low, block_g, (((0,), (1,)), ((), ())), preferred_element_type=F32
                ).astype(BF16),
                output_block,
            ],
            axis=1,
        )
        for block_g, output_block in zip(mixed_g, output_grads)
    ]

    joined_grad, encoder_grad = encoder_back(encoded_grad)
    (position_grad,) = position_gate_back(joined_grad)
    position_low = position_grad.astype(BF16)
    grad_window, grad_edge = to_groups(position_low)
    grad_window, middle_pairs = lax.optimization_barrier((grad_window, pair_sums(middle_grads)))
    middle_sum = low_sum(middle_pairs[0], swapped(middle_pairs[1], 2))
    projected_back, taps_grad = position_back(
        window, window_edge, grad_window, grad_edge, position_full
    )

    projected_back, taps_grad, middle_sum = lax.optimization_barrier(
        (from_groups(projected_back), taps_grad, middle_sum)
    )
    projected_grad = (joined_grad + projected_back).astype(BF16)
    projection_grad = inner_dot(normed_low, projected_grad).astype(BF16)
    activated_grad, feature_grad = first_norm_back(outer_dot(projected_grad, projection_full))
    (before_grad,) = gate_back(activated_grad)
    before_low = before_grad.astype(BF16)
    conv_grad = inner_dot(unfolded, before_low).astype(BF16)
    middle_shard = seq_sum(middle_sum)
    conv_grad, middle_shard = lax.optimization_barrier((conv_grad, middle_shard))
    unfolded_grad = outer_dot(before_low, conv_full).reshape(MICROS, frames, 3 * C_CNN)
    following_grad = unfolded_grad[:, :, 2 * C_CNN :] * same_next.astype(F32)
    carried = shifted(following_grad[:, frames - 1 :], "seq", 1)
    even_grad = unfolded_grad[:, :, :C_CNN] + jnp.concatenate(
        [carried, following_grad[:, :-1]], axis=1
    )
    input_grad = jnp.concatenate([even_grad, unfolded_grad[:, :, C_CNN : 2 * C_CNN]], axis=2)
    input_grad = input_grad.reshape(MICROS, 1, 2 * frames, C_CNN)

    gain_grads = jnp.concatenate(
        [
            grad.reshape(devices, -1)
            for grad in (feature_grad, encoder_grad, attention_grad, final_grad)
        ],
        axis=1,
    ).astype(BF16)
    gain_grads = jnp.pad(gain_grads[:, None], ((0, 0), (0, 7), (0, D - gains.size)))
    front_grads = jnp.concatenate(
        [conv_grad.reshape(devices, -1, D), projection_grad.reshape(devices, -1, D), gain_grads],
        axis=1,
    )
    front_grads = front_grads.reshape(seqs, streams, -1, D)
    front_pairs = pair_sums(flip([front_grads[:, j] for j in range(streams)], stream))
    front_pairs, feed_shard = lax.optimization_barrier((front_pairs, feed_shard))
    front_shard = seq_sum(low_sum(front_pairs[0], swapped(front_pairs[1], 2)))

    taps_grad = (
        taps_grad.transpose(1, 0, 2)
        .reshape(share, outer, group, streams, own_rows)
        .transpose(3, 1, 2, 0, 4)
    )
    taps_grad = reduce_blocks(flip([taps_grad[j] for j in range(streams)], stream))
    if outer > 1:
        taps_grad = lax.psum_scatter(
            taps_grad, "seq", scatter_dimension=0, axis_index_groups=far
        )
    else:
        taps_grad = taps_grad[0]
    position_shard = near_swap(taps_grad).reshape(D, own_rows).T.astype(F32)

    def unswap(block):
        block = block.reshape(streams, up_rows, -1)
        return jnp.stack(swap_parts([block[j] for j in range(streams)], stream)).astype(F32)

    up_shard = (
        unswap(feed_shard[:, :wide])
        .reshape(streams, up_rows, seqs, unit_rows)
        .transpose(1, 2, 0, 3)
        .reshape(up_rows, -1)
    )
    down_shard = feed_shard[:, wide:].astype(F32)
    qkv_shard = (
        unswap(middle_shard[:, : 3 * part])
        .reshape(streams, up_rows, 3, part)
        .transpose(1, 2, 0, 3)
        .reshape(up_rows, -1)
    )
    output_shard = (
        middle_shard[:, 3 * part :]
        .reshape(streams, up_rows, part)
        .transpose(1, 0, 2)
        .reshape(up_rows, D)
        .astype(F32)
    )
    cuts = [conv_weight.size // D]
    cuts.append(cuts[0] + projection_weight.shape[0])
    conv_shard = front_shard[: cuts[0]].reshape(-1, C_CNN)
    projection_shard = front_shard[cuts[0] : cuts[1]]
    gain_row = front_shard[cuts[1]]
    gain_shards = [
        gain_row[:feature_n],
        *(gain_row[feature_n + i * model_n : feature_n + (i + 1) * model_n] for i in range(3)),
    ]
    return (
        block_out.reshape(MICROS, 1, frames, D),
        input_grad,
        conv_shard,
        gain_shards[0],
        projection_shard,
        position_shard,
        gain_shards[1],
        qkv_shard,
        output_shard,
        gain_shards[2],
        up_shard,
        down_shard,
        gain_shards[3],
    )


def solution(mesh):
    weight, gain = P(("seq", "fsdp"), None), P(("seq", "fsdp"))
    rows = P(None, "fsdp", "seq", None)
    in_specs = (
        rows, P(None, "fsdp", None), weight, gain, weight, weight, gain, weight, weight, gain,
        weight, weight, gain, rows,
    )
    out_specs = (
        rows, rows, weight, gain, weight, weight, gain, weight, weight, gain, weight, weight, gain,
    )
    return jax.shard_map(body, mesh=mesh, in_specs=in_specs, out_specs=out_specs, check_vma=False)
```

```python
import math

import jax
import jax.numpy as jnp
from jax import lax
from jax.experimental import pallas as pl
from jax.experimental.pallas import tpu as pltpu
from jax.sharding import PartitionSpec as P

D = 768
HEADS = 12
C_CNN = 512
POS_K = 128
GROUPS = 16
HEAD_DIM = 64
CG = 48
HALF = POS_K // 2
FINE = 16
COARSE = POS_K // FINE
HEAD_PARTS = 4
MICROS = 2
LOG2E = 1.4426950408889634
VMEM = 60 * 1024 * 1024

NORM_EPS = 1e-05
F32 = jnp.float32
BF16 = jnp.bfloat16


def shifted(array, axis, by):
    peers = lax.axis_size(axis)
    pairs = [(i, i + by) for i in range(peers) if 0 <= i + by < peers]
    return lax.ppermute(array, axis, pairs)


def flip(blocks, me):
    count = len(blocks)
    return [lax.select_n(me, *(blocks[m ^ k] for m in range(count))) for k in range(count)]


def swapped(array, k):
    count = lax.axis_size("fsdp")
    return lax.ppermute(array, "fsdp", [(i, i ^ k) for i in range(count)])


def swap_parts(parts, me):
    ordered = flip(parts, me)
    return flip([ordered[0]] + [swapped(ordered[k], k) for k in range(1, 4)], me)


def gather_blocks(block):
    over_x = swapped(block, 2)
    return [block, swapped(block, 1), over_x, swapped(over_x, 1)]


def after(value, other):
    return lax.optimization_barrier((value, other))[0]


def low_sum(*terms):
    return sum(term.astype(F32) for term in terms).astype(BF16)


def pair_sums(blocks):
    return low_sum(blocks[0], swapped(blocks[1], 1)), low_sum(blocks[2], swapped(blocks[3], 1))


def reduce_blocks(blocks):
    kept, sent = pair_sums(blocks)
    return low_sum(kept, swapped(sent, 2))


def norm_rows(values, scales):
    center = values - jnp.mean(values, axis=-1, keepdims=True)
    spread = jnp.mean(center * center, axis=-1, keepdims=True)
    return center * lax.rsqrt(spread + NORM_EPS) * scales


def smooth_gate(values):
    return jax.nn.gelu(values, approximate=False)


def segment_of(utterance_ends, positions):
    return jnp.sum(
        (utterance_ends[..., None, :] <= positions[:, None]).astype(jnp.int32),
        axis=-1,
        dtype=jnp.int32,
    )


def plain_dot(left, right):
    return jnp.dot(left, right, preferred_element_type=F32)


def inner_dot(left, right):
    return lax.dot_general(left, right, (((0,), (0,)), ((), ())), preferred_element_type=F32)


def outer_dot(left, right):
    return lax.dot_general(left, right, (((1,), (1,)), ((), ())), preferred_element_type=F32)


def lane_roll(value, shift):
    shift = shift % value.shape[1]
    return pltpu.roll(value, shift, 1) if shift else value


def joined(ref, edge_ref, micro, frames):
    columns = slice(micro * frames, (micro + 1) * frames)
    edge = slice(micro * POS_K, (micro + 1) * POS_K)
    blocks = [ref[s, :, columns] for s in range(ref.shape[0])] + [edge_ref[:, edge]]
    return jnp.concatenate(blocks, axis=1).astype(F32)


def fine_shifts(x_ref, edge_ref, fine_ref, frames, span):
    for m in range(MICROS):
        x = joined(x_ref, edge_ref, m, frames)
        for fine in range(FINE):
            fine_ref[fine * CG : (fine + 1) * CG, m * span : (m + 1) * span] = lane_roll(
                x, HALF - fine
            ).astype(BF16)


def store_frames(out_ref, micro, frames, total):
    for s in range(out_ref.shape[0]):
        out_ref[s, :, micro * frames : (micro + 1) * frames] = total[
            :, s * frames : (s + 1) * frames
        ].astype(BF16)


def position_kernel(span, frames, x_ref, edge_ref, w_ref, out_ref, fine_ref):
    fine_shifts(x_ref, edge_ref, fine_ref, frames, span)
    weights = w_ref[...].reshape(COARSE * CG, FINE * CG)
    for m in range(MICROS):
        terms = jnp.dot(
            weights, fine_ref[:, m * span : (m + 1) * span], preferred_element_type=F32
        )
        total = terms[:CG]
        for coarse in range(1, COARSE):
            total += lane_roll(terms[coarse * CG : (coarse + 1) * CG], -FINE * coarse)
        store_frames(out_ref, m, frames, total)


def position_back_kernel(
    span, frames, x_ref, x_edge_ref, g_ref, g_edge_ref, w_ref, dx_ref, dw_ref,
    fine_ref, coarse_ref, own_ref,
):
    fine_shifts(x_ref, x_edge_ref, fine_ref, frames, span)
    column = lax.broadcasted_iota(jnp.int32, (CG, span), 1)
    for m in range(MICROS):
        columns = slice(m * span, (m + 1) * span)
        g = joined(g_ref, g_edge_ref, m, frames)
        own = jnp.where(column < span - POS_K, g, 0.0)
        for coarse in range(COARSE):
            rows = slice(coarse * CG, (coarse + 1) * CG)
            back = FINE * (COARSE - 1 - coarse)
            coarse_ref[rows, columns] = lane_roll(g, HALF - back).astype(BF16)
            own_ref[rows, columns] = lane_roll(own, FINE * coarse).astype(BF16)
    weights = w_ref[...].reshape(COARSE * CG, FINE * CG)
    turned = weights.astype(F32).T.astype(BF16)
    for m in range(MICROS):
        terms = jnp.dot(
            turned, coarse_ref[:, m * span : (m + 1) * span], preferred_element_type=F32
        )
        total = lane_roll(terms[:CG], -FINE)
        for fine in range(1, FINE):
            total += lane_roll(terms[fine * CG : (fine + 1) * CG], fine - FINE)
        store_frames(dx_ref, m, frames, total)
    grad = lax.dot_general(
        own_ref[...], fine_ref[...], (((1,), (1,)), ((), ())), preferred_element_type=F32
    )
    dw_ref[...] = grad.astype(BF16).reshape(COARSE, CG, FINE * CG)


def group_specs(count, columns):
    wide = pl.BlockSpec((count, CG, columns), lambda g: (0, g, 0))
    edge = pl.BlockSpec((CG, MICROS * POS_K), lambda g: (g, 0))
    weight = pl.BlockSpec((COARSE, CG, FINE * CG), lambda g: (0, g, 0))
    return wide, edge, weight


def position_conv(x, edge, weights):
    count, channels, columns = x.shape
    frames = columns // MICROS
    span = count * frames + POS_K
    groups = channels // CG
    wide, edge_spec, weight = group_specs(count, columns)
    flops = 2 * groups * MICROS * span * COARSE * CG * FINE * CG
    return pl.pallas_call(
        lambda *refs: position_kernel(span, frames, *refs),
        grid=(groups,),
        in_specs=[wide, edge_spec, weight],
        out_specs=wide,
        out_shape=jax.ShapeDtypeStruct(x.shape, BF16),
        scratch_shapes=[pltpu.VMEM((FINE * CG, MICROS * span), BF16)],
        compiler_params=pltpu.CompilerParams(vmem_limit_bytes=VMEM),
        cost_estimate=pl.CostEstimate(
            flops=flops, bytes_accessed=2 * (2 * x.size + weights.size), transcendentals=0
        ),
        name="position_conv",
    )(x, edge, weights)


def position_back(x, x_edge, grad, grad_edge, weights):
    count, channels, columns = x.shape
    frames = columns // MICROS
    span = count * frames + POS_K
    groups = channels // CG
    wide, edge_spec, weight = group_specs(count, columns)
    flops = 4 * groups * MICROS * span * COARSE * CG * FINE * CG
    return pl.pallas_call(
        lambda *refs: position_back_kernel(span, frames, *refs),
        grid=(groups,),
        in_specs=[wide, edge_spec, wide, edge_spec, weight],
        out_specs=[wide, weight],
        out_shape=[
            jax.ShapeDtypeStruct(x.shape, BF16),
            jax.ShapeDtypeStruct(weights.shape, BF16),
        ],
        scratch_shapes=[
            pltpu.VMEM((FINE * CG, MICROS * span), BF16),
            pltpu.VMEM((COARSE * CG, MICROS * span), BF16),
            pltpu.VMEM((COARSE * CG, MICROS * span), BF16),
        ],
        compiler_params=pltpu.CompilerParams(vmem_limit_bytes=VMEM),
        cost_estimate=pl.CostEstimate(
            flops=flops, bytes_accessed=2 * (3 * x.size + 2 * weights.size), transcendentals=0
        ),
        name="position_back",
    )(x, x_edge, grad, grad_edge, weights)


def side_by_side(ref):
    return jnp.concatenate([ref[s, 0] for s in range(ref.shape[0])], axis=1)


def turn(value):
    return value.astype(F32).T.astype(BF16)


def attention_kernel(block, q_ref, k_ref, v_ref, seg_q_ref, seg_k_ref, out_ref):
    queries = turn(side_by_side(q_ref))
    keys = side_by_side(k_ref)
    values = side_by_side(v_ref)
    frames = out_ref.shape[2]
    factor = HEAD_DIM**-0.5 * LOG2E
    for first in range(0, queries.shape[0], block):
        rows = slice(first, first + block)
        scores = jnp.dot(queries[rows], keys, preferred_element_type=F32)
        expo = jnp.where(seg_q_ref[rows] == seg_k_ref[...], jnp.exp2(scores * factor), 0.0)
        weight_sum = jnp.sum(expo, axis=1, keepdims=True)
        accum = lax.dot_general(
            expo.astype(BF16), values, (((1,), (1,)), ((), ())), preferred_element_type=F32
        )
        context = (accum / weight_sum).T
        for part in range(block // frames):
            out_ref[first // frames + part] = context[:, part * frames : (part + 1) * frames]


def attention_back_kernel(
    block, q_ref, k_ref, v_ref, cg_ref, ctx_ref, seg_q_ref, seg_k_ref,
    dq_ref, dk_ref, dv_ref, dk_sum, dv_sum,
):
    keys_across = side_by_side(k_ref)
    keys = turn(keys_across)
    values = turn(side_by_side(v_ref))
    frames = ctx_ref.shape[2]
    parts = block // frames
    scale = HEAD_DIM**-0.5
    for step in range(q_ref.shape[0] // parts):
        some = range(step * parts, (step + 1) * parts)
        columns = slice(step * block, (step + 1) * block)
        queries = jnp.concatenate([q_ref[s, 0] for s in some], axis=1)
        context_grad = jnp.concatenate([cg_ref[s].astype(F32) for s in some], axis=1)
        context = jnp.concatenate([ctx_ref[s] for s in some], axis=1)
        scores = jnp.dot(keys, queries, preferred_element_type=F32)
        expo = jnp.where(
            seg_k_ref[...] == seg_q_ref[:, columns], jnp.exp2(scores * (scale * LOG2E)), 0.0
        )
        inverse = 1.0 / jnp.sum(expo, axis=0, keepdims=True)
        accum_g = (context_grad * inverse).astype(BF16)
        correction = jnp.sum(context_grad * context, axis=0, keepdims=True) * inverse
        dots = jnp.dot(values, accum_g, preferred_element_type=F32)
        score_g = (expo * (dots - correction)).astype(BF16)
        query_grad = jnp.dot(keys_across, score_g, preferred_element_type=F32) * scale
        for part, s in enumerate(some):
            dq_ref[s] = query_grad[:, part * frames : (part + 1) * frames].astype(BF16)
        key_grad = lax.dot_general(
            score_g, queries, (((1,), (1,)), ((), ())), preferred_element_type=F32
        )
        value_grad = lax.dot_general(
            expo.astype(BF16), accum_g, (((1,), (1,)), ((), ())), preferred_element_type=F32
        )
        if step == 0:
            dk_sum[...] = key_grad
            dv_sum[...] = value_grad
        else:
            dk_sum[...] += key_grad
            dv_sum[...] += value_grad
    key_total = (dk_sum[...] * scale).T.astype(BF16)
    value_total = dv_sum[...].T.astype(BF16)
    for s in range(dk_ref.shape[0]):
        dk_ref[s] = key_total[:, s * frames : (s + 1) * frames]
        dv_ref[s] = value_total[:, s * frames : (s + 1) * frames]


def head_spec(count, frames, which):
    return pl.BlockSpec((count, 1, HEAD_DIM, frames), lambda h: (0, which, h, 0))


def plain_spec(count, frames):
    return pl.BlockSpec((count, HEAD_DIM, frames), lambda h: (0, h, 0))


def whole_spec(array):
    return pl.BlockSpec(array.shape, lambda h: (0,) * array.ndim)


def attention(mixed, mixed_all, seg_q, seg_k):
    count, _, channels, frames = mixed.shape
    total = mixed_all.shape[0]
    heads = channels // HEAD_DIM
    block = math.gcd(count, 2) * frames
    seg_q, seg_k = seg_q[:, None], seg_k[None]
    pairs = heads * count * frames * total * frames
    return pl.pallas_call(
        lambda *refs: attention_kernel(block, *refs),
        grid=(heads,),
        in_specs=[
            head_spec(count, frames, 0),
            head_spec(total, frames, 1),
            head_spec(total, frames, 2),
            whole_spec(seg_q),
            whole_spec(seg_k),
        ],
        out_specs=plain_spec(count, frames),
        out_shape=jax.ShapeDtypeStruct((count, channels, frames), F32),
        compiler_params=pltpu.CompilerParams(vmem_limit_bytes=VMEM),
        cost_estimate=pl.CostEstimate(
            flops=4 * HEAD_DIM * pairs, bytes_accessed=8 * mixed.size, transcendentals=pairs
        ),
        name="attention",
    )(mixed, mixed_all, mixed_all, seg_q, seg_k)


def attention_back(mixed, mixed_all, context_grad, context, seg_q, seg_k):
    count, _, channels, frames = mixed.shape
    total = mixed_all.shape[0]
    heads = channels // HEAD_DIM
    block = math.gcd(count, 2) * frames
    seg_q, seg_k = seg_q[None], seg_k[:, None]
    pairs = heads * count * frames * total * frames
    return pl.pallas_call(
        lambda *refs: attention_back_kernel(block, *refs),
        grid=(heads,),
        in_specs=[
            head_spec(count, frames, 0),
            head_spec(total, frames, 1),
            head_spec(total, frames, 2),
            plain_spec(count, frames),
            plain_spec(count, frames),
            whole_spec(seg_q),
            whole_spec(seg_k),
        ],
        out_specs=[
            plain_spec(count, frames),
            plain_spec(total, frames),
            plain_spec(total, frames),
        ],
        out_shape=[
            jax.ShapeDtypeStruct((count, channels, frames), BF16),
            jax.ShapeDtypeStruct((total, channels, frames), BF16),
            jax.ShapeDtypeStruct((total, channels, frames), BF16),
        ],
        scratch_shapes=[pltpu.VMEM((total * frames, HEAD_DIM), F32)] * 2,
        compiler_params=pltpu.CompilerParams(vmem_limit_bytes=VMEM),
        cost_estimate=pl.CostEstimate(
            flops=10 * HEAD_DIM * pairs, bytes_accessed=16 * mixed.size, transcendentals=pairs
        ),
        name="attention_back",
    )(mixed, mixed_all, mixed_all, context_grad, context, seg_q, seg_k)


def gate_and_slope(values):
    inner = 0.5 + 0.5 * lax.erf(values * math.sqrt(0.5))
    density = jnp.exp(-0.5 * values * values) * (1.0 / math.sqrt(2.0 * math.pi))
    return values * inner, inner + values * density


def norm_parts(values):
    center = values - jnp.mean(values, axis=1, keepdims=True)
    spread = jnp.mean(center * center, axis=1, keepdims=True)
    rate = lax.rsqrt(spread + NORM_EPS)
    return center * rate, rate


def norm_back(unit, rate, gain, grad):
    scaled = grad * gain
    level = jnp.mean(scaled, axis=1, keepdims=True)
    slope = jnp.mean(scaled * unit, axis=1, keepdims=True)
    return rate * (scaled - level - unit * slope), jnp.sum(grad * unit, axis=0, keepdims=True)


def dot_nt(left, right):
    return lax.dot_general(left, right, (((1,), (1,)), ((), ())), preferred_element_type=F32)


def feed_kernel(
    ctx_ref, out_w_ref, encoded_ref, attention_gain_ref, final_gain_ref, cotangent_ref,
    feed0, feed1, feed2, feed3,
    block_out_ref, mid_ref, context_grad_ref, attention_grad_ref, final_grad_ref,
    settled_ref, hidden_ref, fed_ref, up_ref, branch_ref,
    weights, slopes, sems,
):
    copies = [
        pltpu.make_async_copy(feed, weights.at[k], sems.at[k])
        for k, feed in enumerate((feed0, feed1, feed2, feed3))
    ]
    for copy in copies:
        copy.start()
    kinds, part, frames = ctx_ref.shape
    heads = kinds // MICROS
    width = weights.shape[1]
    units = weights.shape[2] - width
    context = jnp.concatenate(
        [
            jnp.concatenate([ctx_ref[h * MICROS + m] for m in range(MICROS)], axis=1)
            for h in range(heads)
        ],
        axis=0,
    )
    context = turn(context)
    attention_gain = attention_gain_ref[...]
    final_gain = final_gain_ref[...]
    branch = jnp.dot(context, out_w_ref[...], preferred_element_type=F32)
    unit, rate = norm_parts(encoded_ref[...] + branch)
    settled = unit * attention_gain
    settled_low = settled.astype(BF16)
    settled_ref[...] = settled_low
    fed = settled
    for k, copy in enumerate(copies):
        copy.wait()
        columns = slice(k * units, (k + 1) * units)
        up_values = jnp.dot(settled_low, weights[k, :, :units], preferred_element_type=F32)
        hidden, slope = gate_and_slope(up_values)
        slopes[:, columns] = slope
        hidden_low = hidden.astype(BF16)
        hidden_ref[:, columns] = hidden_low
        fed += jnp.dot(hidden_low, weights[k, :, units:], preferred_element_type=F32)
    final_unit, final_rate = norm_parts(fed)
    block_out_ref[...] = final_unit * final_gain
    sum_grad, final_grad_ref[...] = norm_back(
        final_unit, final_rate, final_gain, cotangent_ref[...].astype(F32)
    )
    fed_low = sum_grad.astype(BF16)
    fed_ref[...] = fed_low
    settled_grad = sum_grad
    for k in range(len(copies)):
        columns = slice(k * units, (k + 1) * units)
        up_low = (dot_nt(fed_low, weights[k, :, units:]) * slopes[:, columns]).astype(BF16)
        up_ref[:, columns] = up_low
        settled_grad += dot_nt(up_low, weights[k, :, :units])
    mid_grad, attention_grad_ref[...] = norm_back(unit, rate, attention_gain, settled_grad)
    mid_ref[...] = mid_grad
    branch_low = mid_grad.astype(BF16)
    branch_ref[...] = branch_low
    context_grad = dot_nt(out_w_ref[...], branch_low).astype(BF16)
    for h in range(heads):
        for m in range(MICROS):
            context_grad_ref[h * MICROS + m] = context_grad[
                h * part : (h + 1) * part, m * frames : (m + 1) * frames
            ]


def feed_forward(context, out_w, encoded, attention_gain, final_gain, cotangent, feeds):
    rows, width = encoded.shape
    units = feeds[0].shape[1] - width
    wide = len(feeds) * units
    vmem = pl.BlockSpec(memory_space=pltpu.VMEM)
    flops = 2 * rows * width * (4 * wide + 2 * width)
    return pl.pallas_call(
        feed_kernel,
        in_specs=[vmem] * 6 + [pl.BlockSpec(memory_space=pl.ANY)] * 4,
        out_specs=[vmem] * 10,
        out_shape=[
            jax.ShapeDtypeStruct((rows, width), F32),
            jax.ShapeDtypeStruct((rows, width), F32),
            jax.ShapeDtypeStruct(context.shape, BF16),
            jax.ShapeDtypeStruct((1, width), F32),
            jax.ShapeDtypeStruct((1, width), F32),
            jax.ShapeDtypeStruct((rows, width), BF16),
            jax.ShapeDtypeStruct((rows, wide), BF16),
            jax.ShapeDtypeStruct((rows, width), BF16),
            jax.ShapeDtypeStruct((rows, wide), BF16),
            jax.ShapeDtypeStruct((rows, width), BF16),
        ],
        scratch_shapes=[
            pltpu.VMEM((len(feeds), width, width + units), BF16),
            pltpu.VMEM((rows, wide), F32),
            pltpu.SemaphoreType.DMA((len(feeds),)),
        ],
        compiler_params=pltpu.CompilerParams(vmem_limit_bytes=VMEM),
        cost_estimate=pl.CostEstimate(
            flops=flops, bytes_accessed=4 * width * wide, transcendentals=2 * rows * wide
        ),
        name="feed_forward",
    )(context, out_w, encoded, attention_gain, final_gain, cotangent, *feeds)


def feed_grad_kernel(settled_ref, up_ref, hidden_ref, fed_ref, out_ref):
    units = up_ref.shape[1]
    up_grad = jnp.dot(turn(settled_ref[...]), up_ref[...], preferred_element_type=F32)
    out_ref[:, :units] = up_grad.astype(BF16)
    down_grad = jnp.dot(turn(hidden_ref[...]), fed_ref[...], preferred_element_type=F32)
    out_ref[:, units:] = down_grad.astype(BF16)


def feed_grad(k, settled, up, hidden, fed):
    rows, width = settled.shape
    units = up.shape[1] // 4
    whole = pl.BlockSpec((rows, width), lambda g: (0, 0))
    block = pl.BlockSpec((rows, units), lambda g: (0, k))
    return pl.pallas_call(
        feed_grad_kernel,
        grid=(1,),
        in_specs=[whole, block, block, whole],
        out_specs=pl.BlockSpec((width, units + width), lambda g: (0, 0)),
        out_shape=jax.ShapeDtypeStruct((width, units + width), BF16),
        compiler_params=pltpu.CompilerParams(vmem_limit_bytes=VMEM),
        cost_estimate=pl.CostEstimate(
            flops=4 * rows * width * units, bytes_accessed=8 * width * units, transcendentals=0
        ),
        name="feed_grad",
    )(settled, up, hidden, fed)


def body(
    features,
    lengths,
    conv_weight,
    feature_gain,
    projection_weight,
    position_weight,
    encoder_gain,
    qkv_weight,
    output_weight,
    attention_gain,
    up_weight,
    down_weight,
    final_gain,
    cotangent,
):
    frames = cotangent.shape[2]
    rows = MICROS * frames
    seqs = lax.axis_size("seq")
    streams = lax.axis_size("fsdp")
    devices = seqs * streams
    me = lax.axis_index("seq")
    stream = lax.axis_index("fsdp")
    both = ("seq", "fsdp")
    group = HEAD_PARTS * MICROS
    outer = seqs // group
    near = [[o * group + i for i in range(group)] for o in range(outer)]
    far = [[o * group + i for o in range(outer)] for i in range(group)]

    def near_swap(blocks):
        return lax.all_to_all(blocks, "seq", 0, 0, axis_index_groups=near)

    def seq_sum(blocks):
        blocks = near_swap(blocks.reshape(outer, group, -1, D).transpose(1, 0, 2, 3))
        total = jnp.sum(blocks.astype(F32), axis=0)
        if outer == 1:
            return total[0]
        return lax.psum_scatter(total, "seq", scatter_dimension=0, axis_index_groups=far)

    def near_gather(block, again):
        blocks = [block]
        for k in range(1, group):
            pairs = [(i, i - i % group + (i % group ^ k)) for i in range(seqs)]
            blocks.append(lax.ppermute(block if k < 5 else again, "seq", pairs))
        return jnp.stack(flip(blocks, me % group))

    front_rows = (conv_weight.shape[0], projection_weight.size // C_CNN)
    gains = jnp.concatenate([feature_gain, encoder_gain, attention_gain, final_gain])
    front = jnp.concatenate(
        [
            conv_weight,
            projection_weight.reshape(-1, C_CNN),
            jnp.pad(gains[None], ((0, 7), (0, C_CNN - gains.size))),
        ],
        axis=0,
    )
    part = D // HEAD_PARTS
    up_rows = up_weight.shape[0]
    unit_rows = down_weight.shape[0]
    wide = seqs * unit_rows
    up_parts = up_weight.reshape(up_rows, seqs, streams, unit_rows).transpose(2, 0, 1, 3)
    qkv_parts = qkv_weight.reshape(up_rows, 3, streams, part).transpose(2, 0, 1, 3)
    parts = jnp.concatenate(
        [qkv_parts.reshape(streams, up_rows, 3 * part), up_parts.reshape(streams, up_rows, wide)],
        axis=2,
    )
    parts = jnp.concatenate(swap_parts([parts[j] for j in range(streams)], stream), axis=0)
    front_again, parts = lax.optimization_barrier((front, parts))
    front_near = near_gather(front, front_again)
    front = front_near
    if outer > 1:
        front = lax.all_gather(front, "seq", axis=0, tiled=True, axis_index_groups=far)
    front = jnp.stack(flip(gather_blocks(front), stream), axis=1)
    front = front.reshape(devices, -1, C_CNN)
    cut = front_rows[0] + front_rows[1]
    conv_full = front[:, : front_rows[0]].reshape(-1, C_CNN)
    projection_full = front[:, front_rows[0] : cut].reshape(C_CNN, D)
    gains_full = front[:, cut, : gains.size]
    feature_n, model_n = feature_gain.size, encoder_gain.size
    feature_scale = gains_full[:, :feature_n].reshape(-1).astype(F32)
    encoder_scale, attention_scale, final_scale = (
        gains_full[:, feature_n + i * model_n : feature_n + (i + 1) * model_n]
        .reshape(-1)
        .astype(F32)
        for i in range(3)
    )

    share = D // group
    own_rows = position_weight.shape[0]
    taps, front_near = lax.optimization_barrier((position_weight, front_near))
    taps = near_swap(taps.T.reshape(group, share, own_rows))
    if outer > 1:
        taps = lax.all_gather(taps, "seq", axis=0, axis_index_groups=far)
    taps = taps.reshape(outer, group, share, own_rows)
    position_full = (
        jnp.stack(flip(gather_blocks(taps), stream))
        .transpose(3, 1, 2, 0, 4)
        .reshape(share, COARSE, FINE * CG)
        .transpose(1, 0, 2)
    )

    out_parts = output_weight.reshape(up_rows, streams, part).transpose(1, 0, 2)
    quarter = jnp.concatenate(
        [parts[:, : 3 * part], out_parts.reshape(-1, part), parts[:, 3 * part :], down_weight],
        axis=1,
    )
    quarter = lax.all_gather(quarter, "seq", axis=0, tiled=True)

    ends = jnp.cumsum(lengths[:, 0], axis=-1, dtype=jnp.int32)
    positions = me * frames + jnp.arange(frames + 1, dtype=jnp.int32)
    segments = segment_of(ends, positions)
    same_next = (segments[:, 1:] == segments[:, :-1])[:, :, None]
    pairs = features[:, 0].reshape(MICROS, frames, 2 * C_CNN)
    next_first = shifted(pairs[:, :1, :C_CNN], "seq", -1)
    following = jnp.concatenate([pairs[:, 1:, :C_CNN], next_first], axis=1)
    following = following * same_next.astype(BF16)
    unfolded = jnp.concatenate([pairs, following], axis=2).reshape(rows, 3 * C_CNN)
    before = plain_dot(unfolded, conv_full)
    activated, gate_back = jax.vjp(smooth_gate, before)
    normed, first_norm_back = jax.vjp(norm_rows, activated, feature_scale)
    normed_low = normed.astype(BF16)
    projected = plain_dot(normed_low, projection_full)

    def to_groups(block):
        across = near_swap(block.T.reshape(group, share, rows))
        if outer == 1:
            return across, jnp.zeros((share, MICROS * POS_K), BF16)
        first = across[0].reshape(share, MICROS, frames)[:, :, :HALF]
        last = across[-1].reshape(share, MICROS, frames)[:, :, frames - HALF :]
        edge = [shifted(first, "seq", -group), shifted(last, "seq", group)]
        return across, jnp.concatenate(edge, axis=2).reshape(share, MICROS * POS_K)

    def from_groups(block):
        return near_swap(block).reshape(D, rows).T.astype(F32)

    window, window_edge = to_groups(projected.astype(BF16))
    position = position_conv(window, window_edge, position_full)
    position, quarter = lax.optimization_barrier((position, quarter))
    middle = gather_blocks(quarter[:, : 4 * part])
    qkv_blocks = [block[:, : 3 * part] for block in middle]
    output_full = jnp.stack(flip([block[:, 3 * part :] for block in middle], stream))
    output_full = (
        output_full.reshape(streams, seqs, streams, up_rows, part)
        .transpose(1, 0, 3, 2, 4)
        .reshape(HEAD_PARTS, part, D)
    )
    output_full = jnp.concatenate(flip([output_full[j] for j in range(HEAD_PARTS)], stream))
    position = from_groups(position)
    feed, position = lax.optimization_barrier((quarter[:, 4 * part :], position))
    feed = gather_blocks(feed)
    position_act, position_gate_back = jax.vjp(smooth_gate, position)
    encoded, encoder_back = jax.vjp(norm_rows, projected + position_act, encoder_scale)
    encoded_low = encoded.astype(BF16)

    def to_heads(blocks, kinds):
        across = jnp.stack(blocks) if isinstance(blocks, list) else blocks
        across = across.reshape(HEAD_PARTS, kinds * part, MICROS, frames)
        across = across.transpose(0, 2, 1, 3).reshape(group, kinds, part, frames)
        return near_swap(across)

    def from_heads(blocks, kinds):
        blocks = near_swap(blocks).reshape(HEAD_PARTS, MICROS, kinds * part, frames)
        blocks = blocks.transpose(0, 2, 1, 3).reshape(HEAD_PARTS, kinds * part, rows)
        return [blocks[k] for k in range(HEAD_PARTS)]

    mixed = [
        lax.dot_general(
            block, encoded_low, (((0,), (1,)), ((), ())), preferred_element_type=F32
        ).astype(BF16)
        for block in qkv_blocks
    ]
    mixed_heads = to_heads(mixed, 3)
    if outer > 1:
        mixed_all = lax.all_gather(
            mixed_heads, "seq", axis=0, tiled=True, axis_index_groups=far
        )
    else:
        mixed_all = mixed_heads
    micro_ends = lax.dynamic_index_in_dim(ends, me % MICROS, 0, keepdims=False)
    seg_all = segment_of(micro_ends, jnp.arange(seqs * frames, dtype=jnp.int32))
    seg_own = lax.dynamic_slice_in_dim(
        seg_all, (me // group) * group * frames, group * frames, 0
    )
    context_heads = attention(mixed_heads, mixed_all, seg_own, seg_all)
    context_low = near_swap(context_heads.astype(BF16))

    (
        block_out, mid_grad, context_grad, attention_grad, final_grad,
        settled_low, hidden_low, fed_low, up_low, branch_low,
    ) = feed_forward(
        context_low, output_full, encoded, attention_scale[None], final_scale[None],
        cotangent[:, 0].reshape(rows, D), feed,
    )
    context_grad = near_swap(context_grad)
    feed_grads = {
        k: feed_grad(k, settled_low, up_low, hidden_low, fed_low) for k in (1, 3, 2, 0)
    }
    feed_grads = [feed_grads[k] for k in range(streams)]
    context_low = context_low.reshape(HEAD_PARTS, MICROS, part, frames).transpose(0, 2, 1, 3)
    output_grad = plain_dot(context_low.reshape(D, rows), branch_low).astype(BF16)
    output_grad = output_grad.reshape(HEAD_PARTS, part, D)
    output_grad = jnp.stack(flip([output_grad[j] for j in range(HEAD_PARTS)], stream))
    output_grad = (
        output_grad.reshape(seqs, streams, up_rows, streams, part)
        .transpose(1, 0, 3, 2, 4)
        .reshape(streams, D, part)
    )
    output_grads = flip([output_grad[j] for j in range(streams)], stream)

    context_grad, feed_pairs = lax.optimization_barrier((context_grad, pair_sums(feed_grads)))
    feed_sum = low_sum(feed_pairs[0], swapped(feed_pairs[1], 2))
    dq, dk, dv = attention_back(
        mixed_heads, mixed_all, context_grad, context_heads, seg_own, seg_all
    )
    if outer > 1:
        dk, dv = (
            lax.psum_scatter(
                grad, "seq", scatter_dimension=0, tiled=True, axis_index_groups=far
            )
            for grad in (dk, dv)
        )
    mixed_g = from_heads(jnp.stack([dq, dk, dv], axis=1), 3)
    mixed_g, feed_sum = lax.optimization_barrier((mixed_g, feed_sum))
    feed_shard = lax.psum_scatter(feed_sum, "seq", scatter_dimension=0, tiled=True)
    encoded_grad = mid_grad
    for block, block_g in zip(qkv_blocks, mixed_g):
        encoded_grad += lax.dot_general(
            block_g, block, (((0,), (1,)), ((), ())), preferred_element_type=F32
        )
    middle_grads = [
        jnp.concatenate(
            [
                lax.dot_general(
                    encoded_low, block_g, (((0,), (1,)), ((), ())), preferred_element_type=F32
                ).astype(BF16),
                output_block,
            ],
            axis=1,
        )
        for block_g, output_block in zip(mixed_g, output_grads)
    ]

    joined_grad, encoder_grad = encoder_back(encoded_grad)
    (position_grad,) = position_gate_back(joined_grad)
    position_low = position_grad.astype(BF16)
    grad_window, grad_edge = to_groups(position_low)
    grad_window, middle_pairs = lax.optimization_barrier((grad_window, pair_sums(middle_grads)))
    middle_sum = low_sum(middle_pairs[0], swapped(middle_pairs[1], 2))
    projected_back, taps_grad = position_back(
        window, window_edge, grad_window, grad_edge, position_full
    )

    projected_back, taps_grad, middle_sum = lax.optimization_barrier(
        (from_groups(projected_back), taps_grad, middle_sum)
    )
    projected_grad = (joined_grad + projected_back).astype(BF16)
    projection_grad = inner_dot(normed_low, projected_grad).astype(BF16)
    activated_grad, feature_grad = first_norm_back(outer_dot(projected_grad, projection_full))
    (before_grad,) = gate_back(activated_grad)
    before_low = before_grad.astype(BF16)
    conv_grad = inner_dot(unfolded, before_low).astype(BF16)
    middle_shard = seq_sum(middle_sum)
    unfolded_grad = outer_dot(before_low, conv_full).reshape(MICROS, frames, 3 * C_CNN)
    following_grad = unfolded_grad[:, :, 2 * C_CNN :] * same_next.astype(F32)
    carried = shifted(following_grad[:, frames - 1 :], "seq", 1)
    even_grad = unfolded_grad[:, :, :C_CNN] + jnp.concatenate(
        [carried, following_grad[:, :-1]], axis=1
    )
    input_grad = jnp.concatenate([even_grad, unfolded_grad[:, :, C_CNN : 2 * C_CNN]], axis=2)
    input_grad = input_grad.reshape(MICROS, 1, 2 * frames, C_CNN)

    gain_grads = jnp.concatenate(
        [
            grad.reshape(devices, -1)
            for grad in (feature_grad, encoder_grad, attention_grad, final_grad)
        ],
        axis=1,
    ).astype(BF16)
    gain_grads = jnp.pad(gain_grads[:, None], ((0, 0), (0, 7), (0, D - gains.size)))
    front_grads = jnp.concatenate(
        [conv_grad.reshape(devices, -1, D), projection_grad.reshape(devices, -1, D), gain_grads],
        axis=1,
    )
    front_grads = front_grads.reshape(seqs, streams, -1, D)
    front_pairs = pair_sums(flip([front_grads[:, j] for j in range(streams)], stream))
    front_shard = seq_sum(low_sum(front_pairs[0], swapped(front_pairs[1], 2)))
    feed_shard = after(feed_shard, front_pairs[1])
    middle_shard = after(middle_shard, front_pairs[1])

    taps_grad = (
        taps_grad.transpose(1, 0, 2)
        .reshape(share, outer, group, streams, own_rows)
        .transpose(3, 1, 2, 0, 4)
    )
    taps_grad = reduce_blocks(flip([taps_grad[j] for j in range(streams)], stream))
    if outer > 1:
        taps_grad = lax.psum_scatter(
            taps_grad, "seq", scatter_dimension=0, axis_index_groups=far
        )
    else:
        taps_grad = taps_grad[0]
    position_shard = near_swap(taps_grad).reshape(D, own_rows).T.astype(F32)

    def unswap(block):
        block = block.reshape(streams, up_rows, -1)
        return jnp.stack(swap_parts([block[j] for j in range(streams)], stream)).astype(F32)

    up_shard = (
        unswap(feed_shard[:, :wide])
        .reshape(streams, up_rows, seqs, unit_rows)
        .transpose(1, 2, 0, 3)
        .reshape(up_rows, -1)
    )
    down_shard = feed_shard[:, wide:].astype(F32)
    qkv_shard = (
        unswap(middle_shard[:, : 3 * part])
        .reshape(streams, up_rows, 3, part)
        .transpose(1, 2, 0, 3)
        .reshape(up_rows, -1)
    )
    output_shard = (
        middle_shard[:, 3 * part :]
        .reshape(streams, up_rows, part)
        .transpose(1, 0, 2)
        .reshape(up_rows, D)
        .astype(F32)
    )
    cuts = [conv_weight.size // D]
    cuts.append(cuts[0] + projection_weight.shape[0])
    conv_shard = front_shard[: cuts[0]].reshape(-1, C_CNN)
    projection_shard = front_shard[cuts[0] : cuts[1]]
    gain_row = front_shard[cuts[1]]
    gain_shards = [
        gain_row[:feature_n],
        *(gain_row[feature_n + i * model_n : feature_n + (i + 1) * model_n] for i in range(3)),
    ]
    return (
        block_out.reshape(MICROS, 1, frames, D),
        input_grad,
        conv_shard,
        gain_shards[0],
        projection_shard,
        position_shard,
        gain_shards[1],
        qkv_shard,
        output_shard,
        gain_shards[2],
        up_shard,
        down_shard,
        gain_shards[3],
    )


def solution(mesh):
    weight, gain = P(("seq", "fsdp"), None), P(("seq", "fsdp"))
    rows = P(None, "fsdp", "seq", None)
    in_specs = (
        rows, P(None, "fsdp", None), weight, gain, weight, weight, gain, weight, weight, gain,
        weight, weight, gain, rows,
    )
    out_specs = (
        rows, rows, weight, gain, weight, weight, gain, weight, weight, gain, weight, weight, gain,
    )
    return jax.shard_map(body, mesh=mesh, in_specs=in_specs, out_specs=out_specs, check_vma=False)
```

```python
import math

import jax
import jax.numpy as jnp
import numpy as np
from jax import lax
from jax.experimental import pallas as pl
from jax.experimental.pallas import tpu as pltpu
from jax.sharding import PartitionSpec as P

D = 768
HEADS = 12
C_CNN = 512
POS_K = 128
GROUPS = 16
HEAD_DIM = 64
CG = 48
HALF = POS_K // 2
FINE = 16
COARSE = POS_K // FINE
HEAD_PARTS = 4
MICROS = 2
LOG2E = 1.4426950408889634
VMEM = 60 * 1024 * 1024

NORM_EPS = 1e-05
F32 = jnp.float32
BF16 = jnp.bfloat16


def shifted(array, axis, by):
    peers = lax.axis_size(axis)
    pairs = [(i, i + by) for i in range(peers) if 0 <= i + by < peers]
    return lax.ppermute(array, axis, pairs)


def flip(blocks, me):
    count = len(blocks)
    return [lax.select_n(me, *(blocks[m ^ k] for m in range(count))) for k in range(count)]


def swapped(array, k):
    count = lax.axis_size("fsdp")
    return lax.ppermute(array, "fsdp", [(i, i ^ k) for i in range(count)])


def swap_parts(parts, me):
    ordered = flip(parts, me)
    return flip([ordered[0]] + [swapped(ordered[k], k) for k in range(1, 4)], me)


def gather_blocks(block):
    over_x = swapped(block, 2)
    return [block, swapped(block, 1), over_x, swapped(over_x, 1)]


def after(value, other):
    return lax.optimization_barrier((value, other))[0]


def low_sum(*terms):
    return sum(term.astype(F32) for term in terms).astype(BF16)


def pair_sums(blocks):
    return low_sum(blocks[0], swapped(blocks[1], 1)), low_sum(blocks[2], swapped(blocks[3], 1))


def reduce_blocks(blocks):
    kept, sent = pair_sums(blocks)
    return low_sum(kept, swapped(sent, 2))


def norm_rows(values, scales):
    center = values - jnp.mean(values, axis=-1, keepdims=True)
    spread = jnp.mean(center * center, axis=-1, keepdims=True)
    return center * lax.rsqrt(spread + NORM_EPS) * scales


def smooth_gate(values):
    return jax.nn.gelu(values, approximate=False)


def segment_of(utterance_ends, positions):
    return jnp.sum(
        (utterance_ends[..., None, :] <= positions[:, None]).astype(jnp.int32),
        axis=-1,
        dtype=jnp.int32,
    )


def plain_dot(left, right):
    return jnp.dot(left, right, preferred_element_type=F32)


def inner_dot(left, right):
    return lax.dot_general(left, right, (((0,), (0,)), ((), ())), preferred_element_type=F32)


def outer_dot(left, right):
    return lax.dot_general(left, right, (((1,), (1,)), ((), ())), preferred_element_type=F32)


def lane_roll(value, shift):
    shift = shift % value.shape[1]
    return pltpu.roll(value, shift, 1) if shift else value


def joined(ref, edge_ref, micro, frames):
    columns = slice(micro * frames, (micro + 1) * frames)
    edge = slice(micro * POS_K, (micro + 1) * POS_K)
    blocks = [ref[s, :, columns] for s in range(ref.shape[0])] + [edge_ref[:, edge]]
    return jnp.concatenate(blocks, axis=1).astype(F32)


def fine_shifts(x_ref, edge_ref, fine_ref, frames, span):
    for m in range(MICROS):
        x = joined(x_ref, edge_ref, m, frames)
        for fine in range(FINE):
            fine_ref[fine * CG : (fine + 1) * CG, m * span : (m + 1) * span] = lane_roll(
                x, HALF - fine
            ).astype(BF16)


def store_frames(out_ref, micro, frames, total):
    for s in range(out_ref.shape[0]):
        out_ref[s, :, micro * frames : (micro + 1) * frames] = total[
            :, s * frames : (s + 1) * frames
        ].astype(BF16)


def position_kernel(span, frames, x_ref, edge_ref, w_ref, out_ref, fine_ref):
    fine_shifts(x_ref, edge_ref, fine_ref, frames, span)
    weights = w_ref[...].reshape(COARSE * CG, FINE * CG)
    for m in range(MICROS):
        terms = jnp.dot(
            weights, fine_ref[:, m * span : (m + 1) * span], preferred_element_type=F32
        )
        total = terms[:CG]
        for coarse in range(1, COARSE):
            total += lane_roll(terms[coarse * CG : (coarse + 1) * CG], -FINE * coarse)
        store_frames(out_ref, m, frames, total)


def position_back_kernel(
    span, frames, x_ref, x_edge_ref, g_ref, g_edge_ref, w_ref, dx_ref, dw_ref,
    fine_ref, coarse_ref, own_ref,
):
    fine_shifts(x_ref, x_edge_ref, fine_ref, frames, span)
    column = lax.broadcasted_iota(jnp.int32, (CG, span), 1)
    for m in range(MICROS):
        columns = slice(m * span, (m + 1) * span)
        g = joined(g_ref, g_edge_ref, m, frames)
        own = jnp.where(column < span - POS_K, g, 0.0)
        for coarse in range(COARSE):
            rows = slice(coarse * CG, (coarse + 1) * CG)
            back = FINE * (COARSE - 1 - coarse)
            coarse_ref[rows, columns] = lane_roll(g, HALF - back).astype(BF16)
            own_ref[rows, columns] = lane_roll(own, FINE * coarse).astype(BF16)
    weights = w_ref[...].reshape(COARSE * CG, FINE * CG)
    turned = weights.astype(F32).T.astype(BF16)
    for m in range(MICROS):
        terms = jnp.dot(
            turned, coarse_ref[:, m * span : (m + 1) * span], preferred_element_type=F32
        )
        total = lane_roll(terms[:CG], -FINE)
        for fine in range(1, FINE):
            total += lane_roll(terms[fine * CG : (fine + 1) * CG], fine - FINE)
        store_frames(dx_ref, m, frames, total)
    grad = lax.dot_general(
        own_ref[...], fine_ref[...], (((1,), (1,)), ((), ())), preferred_element_type=F32
    )
    dw_ref[...] = grad.astype(BF16).reshape(COARSE, CG, FINE * CG)


def group_specs(count, columns):
    wide = pl.BlockSpec((count, CG, columns), lambda g: (0, g, 0))
    edge = pl.BlockSpec((CG, MICROS * POS_K), lambda g: (g, 0))
    weight = pl.BlockSpec((COARSE, CG, FINE * CG), lambda g: (0, g, 0))
    return wide, edge, weight


def position_conv(x, edge, weights):
    count, channels, columns = x.shape
    frames = columns // MICROS
    span = count * frames + POS_K
    groups = channels // CG
    wide, edge_spec, weight = group_specs(count, columns)
    flops = 2 * groups * MICROS * span * COARSE * CG * FINE * CG
    return pl.pallas_call(
        lambda *refs: position_kernel(span, frames, *refs),
        grid=(groups,),
        in_specs=[wide, edge_spec, weight],
        out_specs=wide,
        out_shape=jax.ShapeDtypeStruct(x.shape, BF16),
        scratch_shapes=[pltpu.VMEM((FINE * CG, MICROS * span), BF16)],
        compiler_params=pltpu.CompilerParams(vmem_limit_bytes=VMEM),
        cost_estimate=pl.CostEstimate(
            flops=flops, bytes_accessed=2 * (2 * x.size + weights.size), transcendentals=0
        ),
        name="position_conv",
    )(x, edge, weights)


def position_back(x, x_edge, grad, grad_edge, weights):
    count, channels, columns = x.shape
    frames = columns // MICROS
    span = count * frames + POS_K
    groups = channels // CG
    wide, edge_spec, weight = group_specs(count, columns)
    return pl.pallas_call(
        lambda *refs: position_back_kernel(span, frames, *refs),
        grid=(groups,),
        in_specs=[wide, edge_spec, wide, edge_spec, weight],
        out_specs=[wide, weight],
        out_shape=[
            jax.ShapeDtypeStruct(x.shape, BF16),
            jax.ShapeDtypeStruct(weights.shape, BF16),
        ],
        scratch_shapes=[
            pltpu.VMEM((FINE * CG, MICROS * span), BF16),
            pltpu.VMEM((COARSE * CG, MICROS * span), BF16),
            pltpu.VMEM((COARSE * CG, MICROS * span), BF16),
        ],
        compiler_params=pltpu.CompilerParams(vmem_limit_bytes=VMEM),
        cost_estimate=pl.CostEstimate(flops=0, bytes_accessed=0, transcendentals=0),
        name="position_back",
    )(x, x_edge, grad, grad_edge, weights)


def side_by_side(ref):
    return jnp.concatenate([ref[s, 0] for s in range(ref.shape[0])], axis=1)


def turn(value):
    return value.astype(F32).T.astype(BF16)


def attention_kernel(block, q_ref, k_ref, v_ref, seg_q_ref, seg_k_ref, out_ref):
    queries = turn(side_by_side(q_ref))
    keys = side_by_side(k_ref)
    values = side_by_side(v_ref)
    frames = out_ref.shape[2]
    factor = HEAD_DIM**-0.5 * LOG2E
    for first in range(0, queries.shape[0], block):
        rows = slice(first, first + block)
        scores = jnp.dot(queries[rows], keys, preferred_element_type=F32)
        expo = jnp.where(seg_q_ref[rows] == seg_k_ref[...], jnp.exp2(scores * factor), 0.0)
        weight_sum = jnp.sum(expo, axis=1, keepdims=True)
        accum = lax.dot_general(
            expo.astype(BF16), values, (((1,), (1,)), ((), ())), preferred_element_type=F32
        )
        context = (accum / weight_sum).T
        for part in range(block // frames):
            out_ref[first // frames + part] = context[:, part * frames : (part + 1) * frames]


def attention_back_kernel(
    block, q_ref, k_ref, v_ref, cg_ref, ctx_ref, seg_q_ref, seg_k_ref,
    dq_ref, dk_ref, dv_ref, dk_sum, dv_sum,
):
    keys_across = side_by_side(k_ref)
    keys = turn(keys_across)
    values = turn(side_by_side(v_ref))
    frames = ctx_ref.shape[2]
    parts = block // frames
    scale = HEAD_DIM**-0.5
    for step in range(q_ref.shape[0] // parts):
        some = range(step * parts, (step + 1) * parts)
        columns = slice(step * block, (step + 1) * block)
        queries = jnp.concatenate([q_ref[s, 0] for s in some], axis=1)
        context_grad = jnp.concatenate([cg_ref[s].astype(F32) for s in some], axis=1)
        context = jnp.concatenate([ctx_ref[s] for s in some], axis=1)
        scores = jnp.dot(keys, queries, preferred_element_type=F32)
        expo = jnp.where(
            seg_k_ref[...] == seg_q_ref[:, columns], jnp.exp2(scores * (scale * LOG2E)), 0.0
        )
        inverse = 1.0 / jnp.sum(expo, axis=0, keepdims=True)
        accum_g = (context_grad * inverse).astype(BF16)
        correction = jnp.sum(context_grad * context, axis=0, keepdims=True) * inverse
        dots = jnp.dot(values, accum_g, preferred_element_type=F32)
        score_g = (expo * (dots - correction)).astype(BF16)
        query_grad = jnp.dot(keys_across, score_g, preferred_element_type=F32) * scale
        for part, s in enumerate(some):
            dq_ref[s] = query_grad[:, part * frames : (part + 1) * frames].astype(BF16)
        key_grad = lax.dot_general(
            score_g, queries, (((1,), (1,)), ((), ())), preferred_element_type=F32
        )
        value_grad = lax.dot_general(
            expo.astype(BF16), accum_g, (((1,), (1,)), ((), ())), preferred_element_type=F32
        )
        if step == 0:
            dk_sum[...] = key_grad
            dv_sum[...] = value_grad
        else:
            dk_sum[...] += key_grad
            dv_sum[...] += value_grad
    key_total = (dk_sum[...] * scale).T.astype(BF16)
    value_total = dv_sum[...].T.astype(BF16)
    for s in range(dk_ref.shape[0]):
        dk_ref[s] = key_total[:, s * frames : (s + 1) * frames]
        dv_ref[s] = value_total[:, s * frames : (s + 1) * frames]


def head_spec(count, frames, which):
    return pl.BlockSpec((count, 1, HEAD_DIM, frames), lambda h: (0, which, h, 0))


def plain_spec(count, frames):
    return pl.BlockSpec((count, HEAD_DIM, frames), lambda h: (0, h, 0))


def whole_spec(array):
    return pl.BlockSpec(array.shape, lambda h: (0,) * array.ndim)


def attention(mixed, mixed_all, seg_q, seg_k):
    count, _, channels, frames = mixed.shape
    total = mixed_all.shape[0]
    heads = channels // HEAD_DIM
    block = math.gcd(count, 2) * frames
    seg_q, seg_k = seg_q[:, None], seg_k[None]
    pairs = heads * count * frames * total * frames
    return pl.pallas_call(
        lambda *refs: attention_kernel(block, *refs),
        grid=(heads,),
        in_specs=[
            head_spec(count, frames, 0),
            head_spec(total, frames, 1),
            head_spec(total, frames, 2),
            whole_spec(seg_q),
            whole_spec(seg_k),
        ],
        out_specs=plain_spec(count, frames),
        out_shape=jax.ShapeDtypeStruct((count, channels, frames), F32),
        compiler_params=pltpu.CompilerParams(vmem_limit_bytes=VMEM),
        cost_estimate=pl.CostEstimate(
            flops=4 * HEAD_DIM * pairs, bytes_accessed=8 * mixed.size, transcendentals=pairs
        ),
        name="attention",
    )(mixed, mixed_all, mixed_all, seg_q, seg_k)


def attention_back(mixed, mixed_all, context_grad, context, seg_q, seg_k):
    count, _, channels, frames = mixed.shape
    total = mixed_all.shape[0]
    heads = channels // HEAD_DIM
    block = math.gcd(count, 2) * frames
    seg_q, seg_k = seg_q[None], seg_k[:, None]
    pairs = heads * count * frames * total * frames
    return pl.pallas_call(
        lambda *refs: attention_back_kernel(block, *refs),
        grid=(heads,),
        in_specs=[
            head_spec(count, frames, 0),
            head_spec(total, frames, 1),
            head_spec(total, frames, 2),
            plain_spec(count, frames),
            plain_spec(count, frames),
            whole_spec(seg_q),
            whole_spec(seg_k),
        ],
        out_specs=[
            plain_spec(count, frames),
            plain_spec(total, frames),
            plain_spec(total, frames),
        ],
        out_shape=[
            jax.ShapeDtypeStruct((count, channels, frames), BF16),
            jax.ShapeDtypeStruct((total, channels, frames), BF16),
            jax.ShapeDtypeStruct((total, channels, frames), BF16),
        ],
        scratch_shapes=[pltpu.VMEM((total * frames, HEAD_DIM), F32)] * 2,
        compiler_params=pltpu.CompilerParams(vmem_limit_bytes=VMEM),
        cost_estimate=pl.CostEstimate(
            flops=10 * HEAD_DIM * pairs, bytes_accessed=16 * mixed.size, transcendentals=pairs
        ),
        name="attention_back",
    )(mixed, mixed_all, mixed_all, context_grad, context, seg_q, seg_k)


def gate_and_slope(values):
    inner = 0.5 + 0.5 * lax.erf(values * math.sqrt(0.5))
    density = jnp.exp(-0.5 * values * values) * (1.0 / math.sqrt(2.0 * math.pi))
    return values * inner, inner + values * density


def norm_parts(values):
    center = values - jnp.mean(values, axis=1, keepdims=True)
    spread = jnp.mean(center * center, axis=1, keepdims=True)
    rate = lax.rsqrt(spread + NORM_EPS)
    return center * rate, rate


def norm_back(unit, rate, gain, grad):
    scaled = grad * gain
    level = jnp.mean(scaled, axis=1, keepdims=True)
    slope = jnp.mean(scaled * unit, axis=1, keepdims=True)
    return rate * (scaled - level - unit * slope), jnp.sum(grad * unit, axis=0, keepdims=True)


def dot_nt(left, right):
    return lax.dot_general(left, right, (((1,), (1,)), ((), ())), preferred_element_type=F32)


def feed_kernel(
    ctx_ref, out_w_ref, encoded_ref, attention_gain_ref, final_gain_ref, cotangent_ref,
    feed0, feed1, feed2, feed3,
    block_out_ref, mid_ref, context_grad_ref, attention_grad_ref, final_grad_ref,
    settled_ref, hidden_ref, fed_ref, up_ref, branch_ref,
    weights, slopes, sems,
):
    copies = [
        pltpu.make_async_copy(feed, weights.at[k], sems.at[k])
        for k, feed in enumerate((feed0, feed1, feed2, feed3))
    ]
    for copy in copies:
        copy.start()
    kinds, part, frames = ctx_ref.shape
    heads = kinds // MICROS
    width = weights.shape[1]
    units = weights.shape[2] - width
    context = jnp.concatenate(
        [
            jnp.concatenate([ctx_ref[h * MICROS + m] for m in range(MICROS)], axis=1)
            for h in range(heads)
        ],
        axis=0,
    )
    context = turn(context)
    attention_gain = attention_gain_ref[...]
    final_gain = final_gain_ref[...]
    branch = jnp.dot(context, out_w_ref[...], preferred_element_type=F32)
    unit, rate = norm_parts(encoded_ref[...] + branch)
    settled = unit * attention_gain
    settled_low = settled.astype(BF16)
    settled_ref[...] = settled_low
    fed = settled
    for k, copy in enumerate(copies):
        copy.wait()
        columns = slice(k * units, (k + 1) * units)
        up_values = jnp.dot(settled_low, weights[k, :, :units], preferred_element_type=F32)
        hidden, slope = gate_and_slope(up_values)
        slopes[:, columns] = slope
        hidden_low = hidden.astype(BF16)
        hidden_ref[:, columns] = hidden_low
        fed += jnp.dot(hidden_low, weights[k, :, units:], preferred_element_type=F32)
    final_unit, final_rate = norm_parts(fed)
    block_out_ref[...] = final_unit * final_gain
    sum_grad, final_grad_ref[...] = norm_back(
        final_unit, final_rate, final_gain, cotangent_ref[...].astype(F32)
    )
    fed_low = sum_grad.astype(BF16)
    fed_ref[...] = fed_low
    settled_grad = sum_grad
    for k in range(len(copies)):
        columns = slice(k * units, (k + 1) * units)
        up_low = (dot_nt(fed_low, weights[k, :, units:]) * slopes[:, columns]).astype(BF16)
        up_ref[:, columns] = up_low
        settled_grad += dot_nt(up_low, weights[k, :, :units])
    mid_grad, attention_grad_ref[...] = norm_back(unit, rate, attention_gain, settled_grad)
    mid_ref[...] = mid_grad
    branch_low = mid_grad.astype(BF16)
    branch_ref[...] = branch_low
    context_grad = dot_nt(out_w_ref[...], branch_low).astype(BF16)
    for h in range(heads):
        for m in range(MICROS):
            context_grad_ref[h * MICROS + m] = context_grad[
                h * part : (h + 1) * part, m * frames : (m + 1) * frames
            ]


def feed_forward(context, out_w, encoded, attention_gain, final_gain, cotangent, feeds):
    rows, width = encoded.shape
    units = feeds[0].shape[1] - width
    wide = len(feeds) * units
    vmem = pl.BlockSpec(memory_space=pltpu.VMEM)
    flops = 2 * rows * width * (4 * wide + 2 * width)
    return pl.pallas_call(
        feed_kernel,
        in_specs=[vmem] * 6 + [pl.BlockSpec(memory_space=pl.ANY)] * 4,
        out_specs=[vmem] * 10,
        out_shape=[
            jax.ShapeDtypeStruct((rows, width), F32),
            jax.ShapeDtypeStruct((rows, width), F32),
            jax.ShapeDtypeStruct(context.shape, BF16),
            jax.ShapeDtypeStruct((1, width), F32),
            jax.ShapeDtypeStruct((1, width), F32),
            jax.ShapeDtypeStruct((rows, width), BF16),
            jax.ShapeDtypeStruct((rows, wide), BF16),
            jax.ShapeDtypeStruct((rows, width), BF16),
            jax.ShapeDtypeStruct((rows, wide), BF16),
            jax.ShapeDtypeStruct((rows, width), BF16),
        ],
        scratch_shapes=[
            pltpu.VMEM((len(feeds), width, width + units), BF16),
            pltpu.VMEM((rows, wide), F32),
            pltpu.SemaphoreType.DMA((len(feeds),)),
        ],
        compiler_params=pltpu.CompilerParams(vmem_limit_bytes=VMEM),
        cost_estimate=pl.CostEstimate(
            flops=flops, bytes_accessed=4 * width * wide, transcendentals=2 * rows * wide
        ),
        name="feed_forward",
    )(context, out_w, encoded, attention_gain, final_gain, cotangent, *feeds)


def feed_grad_kernel(settled_ref, up_ref, hidden_ref, fed_ref, out_ref):
    units = up_ref.shape[1]
    up_grad = jnp.dot(turn(settled_ref[...]), up_ref[...], preferred_element_type=F32)
    out_ref[:, :units] = up_grad.astype(BF16)
    down_grad = jnp.dot(turn(hidden_ref[...]), fed_ref[...], preferred_element_type=F32)
    out_ref[:, units:] = down_grad.astype(BF16)


def feed_grad(k, settled, up, hidden, fed):
    rows, width = settled.shape
    units = up.shape[1] // 4
    whole = pl.BlockSpec((rows, width), lambda g: (0, 0))
    block = pl.BlockSpec((rows, units), lambda g: (0, k))
    return pl.pallas_call(
        feed_grad_kernel,
        grid=(1,),
        in_specs=[whole, block, block, whole],
        out_specs=pl.BlockSpec((width, units + width), lambda g: (0, 0)),
        out_shape=jax.ShapeDtypeStruct((width, units + width), BF16),
        compiler_params=pltpu.CompilerParams(vmem_limit_bytes=VMEM),
        cost_estimate=pl.CostEstimate(
            flops=4 * rows * width * units, bytes_accessed=8 * width * units, transcendentals=0
        ),
        name="feed_grad",
    )(settled, up, hidden, fed)


def head_kernel(width, encoded_ref, *refs):
    blocks, out_ref = refs[:-1], refs[-1]
    frames = out_ref.shape[2]
    encoded = encoded_ref[...]
    for k, block in enumerate(blocks):
        mixed = jnp.dot(encoded, block[:, :width], preferred_element_type=F32).T.astype(BF16)
        for m in range(MICROS):
            out_ref[k * MICROS + m] = mixed[:, m * frames : (m + 1) * frames]


def head_projection(encoded, blocks, width):
    rows, depth = encoded.shape
    vmem = pl.BlockSpec(memory_space=pltpu.VMEM)
    shape = (len(blocks) * MICROS, width, rows // MICROS)
    return pl.pallas_call(
        lambda *refs: head_kernel(width, *refs),
        in_specs=[vmem] * (1 + len(blocks)),
        out_specs=vmem,
        out_shape=jax.ShapeDtypeStruct(shape, BF16),
        compiler_params=pltpu.CompilerParams(vmem_limit_bytes=VMEM),
        cost_estimate=pl.CostEstimate(flops=0, bytes_accessed=0, transcendentals=0),
        name="head_projection",
    )(encoded, *blocks)


def head_back_kernel(
    width, mixed_ref, mid_ref, position_ref, projected_ref, gain_ref, block0, block1, block2,
    block3, joined_ref, position_grad_ref, gain_grad_ref,
):
    total = mid_ref[...]
    for k, block in enumerate((block0, block1, block2, block3)):
        pieces = [mixed_ref[k * MICROS + m].astype(F32).T for m in range(MICROS)]
        mixed = jnp.concatenate(pieces, axis=0).astype(BF16)
        total += dot_nt(mixed, block[:, :width])
    position, slope = gate_and_slope(position_ref[...].astype(F32).T)
    unit, rate = norm_parts(projected_ref[...] + position)
    joined, gain_grad_ref[...] = norm_back(unit, rate, gain_ref[...], total)
    joined_ref[...] = joined
    position_grad_ref[...] = (joined * slope).T.astype(BF16)


def head_back(mixed, mid_grad, position, projected, gain, blocks, width):
    rows, depth = mid_grad.shape
    vmem = pl.BlockSpec(memory_space=pltpu.VMEM)
    return pl.pallas_call(
        lambda *refs: head_back_kernel(width, *refs),
        in_specs=[vmem] * (5 + len(blocks)),
        out_specs=[vmem] * 3,
        out_shape=[
            jax.ShapeDtypeStruct((rows, depth), F32),
            jax.ShapeDtypeStruct((depth, rows), BF16),
            jax.ShapeDtypeStruct((1, depth), F32),
        ],
        compiler_params=pltpu.CompilerParams(vmem_limit_bytes=VMEM),
        cost_estimate=pl.CostEstimate(flops=0, bytes_accessed=0, transcendentals=0),
        name="head_back",
    )(mixed, mid_grad, position, projected, gain, *blocks)


def front_kernel(
    stream_ref, back_ref, joined_ref, normed_ref, projection_ref, before_ref, feature_gain_ref,
    unfolded_ref, conv_ref, encoder_ref, attention_ref, final_ref, mask_n_ref, mask_w_ref,
    place0, place1, place2, place3, packed_ref, unfolded_grad_ref,
):
    stream = stream_ref[0]
    projected_grad = (joined_ref[...] + back_ref[...].astype(F32).T).astype(BF16)
    normed_grad = dot_nt(projected_grad, projection_ref[...])
    activated, slope = gate_and_slope(before_ref[...])
    unit, rate = norm_parts(activated)
    activated_grad, feature_grad = norm_back(unit, rate, feature_gain_ref[...], normed_grad)
    before_low = (activated_grad * slope).astype(BF16)
    unfolded_grad_ref[...] = dot_nt(before_low, conv_ref[...])
    conv_grad = jnp.dot(turn(unfolded_ref[...]), before_low, preferred_element_type=F32)
    projection_grad = jnp.dot(turn(normed_ref[...]), projected_grad, preferred_element_type=F32)
    gains = jnp.zeros((mask_n_ref.shape[0], place0.shape[1]), F32)
    for grad, mask, place in (
        (feature_grad, mask_n_ref, place0),
        (encoder_ref[...], mask_w_ref, place1),
        (attention_ref[...], mask_w_ref, place2),
        (final_ref[...], mask_w_ref, place3),
    ):
        gains += jnp.dot((grad * mask[...]).astype(BF16), place[...], preferred_element_type=F32)
    streams, seqs, _, width = packed_ref.shape
    conv_rows = conv_grad.shape[0] // (streams * seqs)
    rows = projection_grad.shape[0] // (streams * seqs)
    first = lax.broadcasted_iota(jnp.int32, (8, gains.shape[1]), 0) == 0
    blank = jnp.zeros((8, width - gains.shape[1]), F32)
    for s in range(seqs):
        for f in range(streams):
            d = s * streams + f
            piece = projection_grad[d * rows : (d + 1) * rows]
            rest = piece[:, width:]
            folded = jnp.concatenate([rest[: rows // 2], rest[rows // 2 :]], axis=1)
            row = jnp.concatenate([jnp.where(first, gains[d : d + 1], 0.0), blank], axis=1)
            block = jnp.concatenate(
                [conv_grad[d * conv_rows : (d + 1) * conv_rows], piece[:, :width], folded, row],
                axis=0,
            )
            packed_ref[f ^ stream, s] = block.astype(BF16)


def front_back(
    stream, back, joined, normed, projection, before, feature_gain, unfolded, conv, gain_grads,
    streams, seqs,
):
    devices = streams * seqs
    narrow, wide = projection.shape
    counts = [narrow // devices] + [wide // devices] * 3
    masks, places, start = [], [], 0
    for size, count in zip((narrow, wide, wide, wide), counts):
        column = np.arange(size)
        masks.append((column[None] // count == np.arange(devices)[:, None]).astype(np.float32))
        place = column[:, None] % count + start == np.arange(128)[None]
        places.append(jnp.asarray(place, BF16))
        start += count
    depth = (conv.shape[0] + narrow + narrow // 2) // devices + 8
    vmem = pl.BlockSpec(memory_space=pltpu.VMEM)
    return pl.pallas_call(
        front_kernel,
        in_specs=[pl.BlockSpec(memory_space=pltpu.SMEM)] + [vmem] * 17,
        out_specs=[vmem] * 2,
        out_shape=[
            jax.ShapeDtypeStruct((streams, seqs, depth, narrow), BF16),
            jax.ShapeDtypeStruct(unfolded.shape, F32),
        ],
        compiler_params=pltpu.CompilerParams(vmem_limit_bytes=VMEM),
        cost_estimate=pl.CostEstimate(flops=0, bytes_accessed=0, transcendentals=0),
        name="front_back",
    )(
        stream, back, joined, normed, projection, before, feature_gain, unfolded, conv,
        *gain_grads, masks[0], masks[1], *places,
    )


def body(
    features,
    lengths,
    conv_weight,
    feature_gain,
    projection_weight,
    position_weight,
    encoder_gain,
    qkv_weight,
    output_weight,
    attention_gain,
    up_weight,
    down_weight,
    final_gain,
    cotangent,
):
    frames = cotangent.shape[2]
    rows = MICROS * frames
    seqs = lax.axis_size("seq")
    streams = lax.axis_size("fsdp")
    devices = seqs * streams
    me = lax.axis_index("seq")
    stream = lax.axis_index("fsdp")
    both = ("seq", "fsdp")
    group = HEAD_PARTS * MICROS
    outer = seqs // group
    near = [[o * group + i for i in range(group)] for o in range(outer)]
    far = [[o * group + i for o in range(outer)] for i in range(group)]

    def near_swap(blocks):
        return lax.all_to_all(blocks, "seq", 0, 0, axis_index_groups=near)

    def seq_sum(blocks):
        shape = (outer, group, -1, blocks.shape[-1])
        blocks = near_swap(blocks.reshape(shape).transpose(1, 0, 2, 3))
        total = jnp.sum(blocks.astype(F32), axis=0)
        if outer == 1:
            return total[0]
        return lax.psum_scatter(total, "seq", scatter_dimension=0, axis_index_groups=far)

    def near_gather(block, again):
        blocks = [block]
        for k in range(1, group):
            pairs = [(i, i - i % group + (i % group ^ k)) for i in range(seqs)]
            blocks.append(lax.ppermute(block if k < 5 else again, "seq", pairs))
        return jnp.stack(flip(blocks, me % group))

    front_rows = (conv_weight.shape[0], projection_weight.size // C_CNN)
    gains = jnp.concatenate([feature_gain, encoder_gain, attention_gain, final_gain])
    front = jnp.concatenate(
        [
            conv_weight,
            projection_weight.reshape(-1, C_CNN),
            jnp.pad(gains[None], ((0, 7), (0, C_CNN - gains.size))),
        ],
        axis=0,
    )
    part = D // HEAD_PARTS
    up_rows = up_weight.shape[0]
    unit_rows = down_weight.shape[0]
    wide = seqs * unit_rows
    up_parts = up_weight.reshape(up_rows, seqs, streams, unit_rows).transpose(2, 0, 1, 3)
    qkv_parts = qkv_weight.reshape(up_rows, 3, streams, part).transpose(2, 0, 1, 3)
    parts = jnp.concatenate(
        [qkv_parts.reshape(streams, up_rows, 3 * part), up_parts.reshape(streams, up_rows, wide)],
        axis=2,
    )
    parts = jnp.concatenate(swap_parts([parts[j] for j in range(streams)], stream), axis=0)
    front_again, parts = lax.optimization_barrier((front, parts))
    front_near = near_gather(front, front_again)
    front = front_near
    if outer > 1:
        front = lax.all_gather(front, "seq", axis=0, tiled=True, axis_index_groups=far)
    front = jnp.stack(flip(gather_blocks(front), stream), axis=1)
    front = front.reshape(devices, -1, C_CNN)
    cut = front_rows[0] + front_rows[1]
    conv_full = front[:, : front_rows[0]].reshape(-1, C_CNN)
    projection_full = front[:, front_rows[0] : cut].reshape(C_CNN, D)
    gains_full = front[:, cut, : gains.size]
    feature_n, model_n = feature_gain.size, encoder_gain.size
    feature_scale = gains_full[:, :feature_n].reshape(-1).astype(F32)
    encoder_scale, attention_scale, final_scale = (
        gains_full[:, feature_n + i * model_n : feature_n + (i + 1) * model_n]
        .reshape(-1)
        .astype(F32)
        for i in range(3)
    )

    share = D // group
    own_rows = position_weight.shape[0]
    taps, front_near = lax.optimization_barrier((position_weight, front_near))
    taps = near_swap(taps.T.reshape(group, share, own_rows))
    if outer > 1:
        taps = lax.all_gather(taps, "seq", axis=0, axis_index_groups=far)
    taps = taps.reshape(outer, group, share, own_rows)
    position_full = (
        jnp.stack(flip(gather_blocks(taps), stream))
        .transpose(3, 1, 2, 0, 4)
        .reshape(share, COARSE, FINE * CG)
        .transpose(1, 0, 2)
    )

    out_parts = output_weight.reshape(up_rows, streams, part).transpose(1, 0, 2)
    quarter = jnp.concatenate(
        [parts[:, : 3 * part], out_parts.reshape(-1, part), parts[:, 3 * part :], down_weight],
        axis=1,
    )
    quarter = lax.all_gather(quarter, "seq", axis=0, tiled=True)

    ends = jnp.cumsum(lengths[:, 0], axis=-1, dtype=jnp.int32)
    positions = me * frames + jnp.arange(frames + 1, dtype=jnp.int32)
    segments = segment_of(ends, positions)
    same_next = (segments[:, 1:] == segments[:, :-1])[:, :, None]
    pairs = features[:, 0].reshape(MICROS, frames, 2 * C_CNN)
    next_first = shifted(pairs[:, :1, :C_CNN], "seq", -1)
    following = jnp.concatenate([pairs[:, 1:, :C_CNN], next_first], axis=1)
    following = following * same_next.astype(BF16)
    unfolded = jnp.concatenate([pairs, following], axis=2).reshape(rows, 3 * C_CNN)
    before = plain_dot(unfolded, conv_full)
    normed_low = norm_rows(smooth_gate(before), feature_scale).astype(BF16)
    projected = plain_dot(normed_low, projection_full)

    def to_groups(block):
        across = near_swap(block.reshape(group, share, rows))
        if outer == 1:
            return across, jnp.zeros((share, MICROS * POS_K), BF16)
        first = across[0].reshape(share, MICROS, frames)[:, :, :HALF]
        last = across[-1].reshape(share, MICROS, frames)[:, :, frames - HALF :]
        edge = [shifted(first, "seq", -group), shifted(last, "seq", group)]
        return across, jnp.concatenate(edge, axis=2).reshape(share, MICROS * POS_K)

    window, window_edge = to_groups(projected.astype(BF16).T)
    position = position_conv(window, window_edge, position_full)
    position, quarter = lax.optimization_barrier((position, quarter))
    middle = gather_blocks(quarter[:, : 4 * part])
    output_full = jnp.stack(flip([block[:, 3 * part :] for block in middle], stream))
    output_full = (
        output_full.reshape(streams, seqs, streams, up_rows, part)
        .transpose(1, 0, 3, 2, 4)
        .reshape(HEAD_PARTS, part, D)
    )
    output_full = jnp.concatenate(flip([output_full[j] for j in range(HEAD_PARTS)], stream))
    position = near_swap(position).reshape(D, rows)
    feed, position = lax.optimization_barrier((quarter[:, 4 * part :], position))
    feed = gather_blocks(feed)
    position_act = smooth_gate(position.T.astype(F32))
    encoded = norm_rows(projected + position_act, encoder_scale)
    encoded_low = encoded.astype(BF16)

    mixed_heads = near_swap(head_projection(encoded_low, middle, 3 * part))
    mixed_heads = mixed_heads.reshape(group, 3, part, frames)
    if outer > 1:
        mixed_all = lax.all_gather(
            mixed_heads, "seq", axis=0, tiled=True, axis_index_groups=far
        )
    else:
        mixed_all = mixed_heads
    micro_ends = lax.dynamic_index_in_dim(ends, me % MICROS, 0, keepdims=False)
    seg_all = segment_of(micro_ends, jnp.arange(seqs * frames, dtype=jnp.int32))
    seg_own = lax.dynamic_slice_in_dim(
        seg_all, (me // group) * group * frames, group * frames, 0
    )
    context_heads = attention(mixed_heads, mixed_all, seg_own, seg_all)
    context_low = near_swap(context_heads.astype(BF16))

    (
        block_out, mid_grad, context_grad, attention_grad, final_grad,
        settled_low, hidden_low, fed_low, up_low, branch_low,
    ) = feed_forward(
        context_low, output_full, encoded, attention_scale[None], final_scale[None],
        cotangent[:, 0].reshape(rows, D), feed,
    )
    context_grad = near_swap(context_grad)
    feed_grads = {
        k: feed_grad(k, settled_low, up_low, hidden_low, fed_low) for k in (1, 3, 2, 0)
    }
    feed_grads = [feed_grads[k] for k in range(streams)]
    context_low = context_low.reshape(HEAD_PARTS, MICROS, part, frames).transpose(0, 2, 1, 3)
    output_grad = plain_dot(context_low.reshape(D, rows), branch_low).astype(BF16)
    output_grad = output_grad.reshape(HEAD_PARTS, part, D)
    output_grad = jnp.stack(flip([output_grad[j] for j in range(HEAD_PARTS)], stream))
    output_grad = (
        output_grad.reshape(seqs, streams, up_rows, streams, part)
        .transpose(1, 0, 3, 2, 4)
        .reshape(streams, D, part)
    )
    output_grads = flip([output_grad[j] for j in range(streams)], stream)

    context_grad, feed_pairs = lax.optimization_barrier((context_grad, pair_sums(feed_grads)))
    half = feed_pairs[1].shape[0] // 2
    first = swapped(feed_pairs[1][:half], 2)
    second = swapped(after(feed_pairs[1][half:], first), 2)
    feed_sum = low_sum(feed_pairs[0], jnp.concatenate([first, second], axis=0))
    dq, dk, dv = attention_back(
        mixed_heads, mixed_all, context_grad, context_heads, seg_own, seg_all
    )
    if outer > 1:
        dk, dv = (
            lax.psum_scatter(
                grad, "seq", scatter_dimension=0, tiled=True, axis_index_groups=far
            )
            for grad in (dk, dv)
        )
    mixed_g = near_swap(jnp.stack([dq, dk, dv], axis=1)).reshape(group, 3 * part, frames)
    mixed_g, feed_sum = lax.optimization_barrier((mixed_g, feed_sum))
    joined_grad, position_grad, encoder_grad = head_back(
        mixed_g, mid_grad, position, projected, encoder_scale[None], middle, 3 * part
    )
    mixed_g = mixed_g.reshape(HEAD_PARTS, MICROS, 3 * part, frames).transpose(0, 2, 1, 3)
    mixed_g = mixed_g.reshape(HEAD_PARTS, 3 * part, rows)
    feed_shard = lax.psum_scatter(feed_sum, "seq", scatter_dimension=0, tiled=True)
    middle_grads = [
        jnp.concatenate(
            [
                lax.dot_general(
                    encoded_low, mixed_g[k], (((0,), (1,)), ((), ())), preferred_element_type=F32
                ).astype(BF16),
                output_grads[k],
            ],
            axis=1,
        )
        for k in range(HEAD_PARTS)
    ]

    grad_window, grad_edge = to_groups(position_grad)
    grad_window, middle_pairs = lax.optimization_barrier((grad_window, pair_sums(middle_grads)))
    middle_sum = low_sum(middle_pairs[0], swapped(middle_pairs[1], 2))
    projected_back, taps_grad = position_back(
        window, window_edge, grad_window, grad_edge, position_full
    )

    projected_back = near_swap(projected_back).reshape(D, rows)
    projected_back, middle_sum = lax.optimization_barrier((projected_back, middle_sum))
    middle_shard = seq_sum(middle_sum)
    front_grads, unfolded_grad = front_back(
        stream[None], projected_back, joined_grad, normed_low, projection_full, before,
        feature_scale[None], unfolded, conv_full, (encoder_grad, attention_grad, final_grad),
        streams, seqs,
    )
    unfolded_grad = unfolded_grad.reshape(MICROS, frames, 3 * C_CNN)
    following_grad = unfolded_grad[:, :, 2 * C_CNN :] * same_next.astype(F32)
    carried = shifted(following_grad[:, frames - 1 :], "seq", 1)
    even_grad = unfolded_grad[:, :, :C_CNN] + jnp.concatenate(
        [carried, following_grad[:, :-1]], axis=1
    )
    input_grad = jnp.concatenate([even_grad, unfolded_grad[:, :, C_CNN : 2 * C_CNN]], axis=2)
    input_grad = input_grad.reshape(MICROS, 1, 2 * frames, C_CNN)

    front_pairs = pair_sums([front_grads[k] for k in range(streams)])
    front_shard = seq_sum(low_sum(front_pairs[0], swapped(front_pairs[1], 2)))
    feed_shard = after(feed_shard, front_pairs[1])
    middle_shard = after(middle_shard, front_pairs[1])

    taps_grad = (
        taps_grad.transpose(1, 0, 2)
        .reshape(share, outer, group, streams, own_rows)
        .transpose(3, 1, 2, 0, 4)
    )
    taps_grad = reduce_blocks(flip([taps_grad[j] for j in range(streams)], stream))
    if outer > 1:
        taps_grad = lax.psum_scatter(
            taps_grad, "seq", scatter_dimension=0, axis_index_groups=far
        )
    else:
        taps_grad = taps_grad[0]
    position_shard = near_swap(taps_grad).reshape(D, own_rows).T.astype(F32)

    def unswap(block):
        block = block.reshape(streams, up_rows, -1)
        return jnp.stack(swap_parts([block[j] for j in range(streams)], stream)).astype(F32)

    up_shard = (
        unswap(feed_shard[:, :wide])
        .reshape(streams, up_rows, seqs, unit_rows)
        .transpose(1, 2, 0, 3)
        .reshape(up_rows, -1)
    )
    down_shard = feed_shard[:, wide:].astype(F32)
    qkv_shard = (
        unswap(middle_shard[:, : 3 * part])
        .reshape(streams, up_rows, 3, part)
        .transpose(1, 2, 0, 3)
        .reshape(up_rows, -1)
    )
    output_shard = (
        middle_shard[:, 3 * part :]
        .reshape(streams, up_rows, part)
        .transpose(1, 0, 2)
        .reshape(up_rows, D)
        .astype(F32)
    )
    conv_rows, projection_rows = conv_weight.shape[0], projection_weight.shape[0]
    conv_shard = front_shard[:conv_rows]
    cut = conv_rows + projection_rows
    folded = front_shard[cut : cut + projection_rows // 2]
    folded = jnp.concatenate([folded[:, : D - C_CNN], folded[:, D - C_CNN :]], axis=0)
    projection_shard = jnp.concatenate([front_shard[conv_rows:cut], folded], axis=1)
    gain_row = front_shard[cut + projection_rows // 2]
    gain_shards = [
        gain_row[:feature_n],
        *(gain_row[feature_n + i * model_n : feature_n + (i + 1) * model_n] for i in range(3)),
    ]
    return (
        block_out.reshape(MICROS, 1, frames, D),
        input_grad,
        conv_shard,
        gain_shards[0],
        projection_shard,
        position_shard,
        gain_shards[1],
        qkv_shard,
        output_shard,
        gain_shards[2],
        up_shard,
        down_shard,
        gain_shards[3],
    )


def solution(mesh):
    weight, gain = P(("seq", "fsdp"), None), P(("seq", "fsdp"))
    rows = P(None, "fsdp", "seq", None)
    in_specs = (
        rows, P(None, "fsdp", None), weight, gain, weight, weight, gain, weight, weight, gain,
        weight, weight, gain, rows,
    )
    out_specs = (
        rows, rows, weight, gain, weight, weight, gain, weight, weight, gain, weight, weight, gain,
    )
    return jax.shard_map(body, mesh=mesh, in_specs=in_specs, out_specs=out_specs, check_vma=False)
```

```python
import math

import jax
import jax.numpy as jnp
import numpy as np
from jax import lax
from jax.experimental import pallas as pl
from jax.experimental.pallas import tpu as pltpu
from jax.sharding import PartitionSpec as P

D = 768
HEADS = 12
C_CNN = 512
POS_K = 128
GROUPS = 16
HEAD_DIM = 64
CG = 48
HALF = POS_K // 2
FINE = 16
COARSE = POS_K // FINE
HEAD_PARTS = 4
MICROS = 2
LOG2E = 1.4426950408889634
VMEM = 60 * 1024 * 1024

NORM_EPS = 1e-05
F32 = jnp.float32
BF16 = jnp.bfloat16


def shifted(array, axis, by):
    peers = lax.axis_size(axis)
    pairs = [(i, i + by) for i in range(peers) if 0 <= i + by < peers]
    return lax.ppermute(array, axis, pairs)


def flip(blocks, me):
    count = len(blocks)
    return [lax.select_n(me, *(blocks[m ^ k] for m in range(count))) for k in range(count)]


def swapped(array, k):
    count = lax.axis_size("fsdp")
    return lax.ppermute(array, "fsdp", [(i, i ^ k) for i in range(count)])


def swap_parts(parts, me):
    ordered = flip(parts, me)
    return flip([ordered[0]] + [swapped(ordered[k], k) for k in range(1, 4)], me)


def gather_blocks(block):
    over_x = swapped(block, 2)
    return [block, swapped(block, 1), over_x, swapped(over_x, 1)]


def after(value, other):
    return lax.optimization_barrier((value, other))[0]


def low_sum(*terms):
    return sum(term.astype(F32) for term in terms).astype(BF16)


def pair_sums(blocks):
    return low_sum(blocks[0], swapped(blocks[1], 1)), low_sum(blocks[2], swapped(blocks[3], 1))


def reduce_blocks(blocks):
    kept, sent = pair_sums(blocks)
    return low_sum(kept, swapped(sent, 2))


def norm_rows(values, scales):
    center = values - jnp.mean(values, axis=-1, keepdims=True)
    spread = jnp.mean(center * center, axis=-1, keepdims=True)
    return center * lax.rsqrt(spread + NORM_EPS) * scales


def smooth_gate(values):
    return jax.nn.gelu(values, approximate=False)


def segment_of(utterance_ends, positions):
    return jnp.sum(
        (utterance_ends[..., None, :] <= positions[:, None]).astype(jnp.int32),
        axis=-1,
        dtype=jnp.int32,
    )


def plain_dot(left, right):
    return jnp.dot(left, right, preferred_element_type=F32)


def inner_dot(left, right):
    return lax.dot_general(left, right, (((0,), (0,)), ((), ())), preferred_element_type=F32)


def outer_dot(left, right):
    return lax.dot_general(left, right, (((1,), (1,)), ((), ())), preferred_element_type=F32)


def lane_roll(value, shift):
    shift = shift % value.shape[1]
    return pltpu.roll(value, shift, 1) if shift else value


def joined(ref, edge_ref, micro, frames):
    columns = slice(micro * frames, (micro + 1) * frames)
    edge = slice(micro * POS_K, (micro + 1) * POS_K)
    blocks = [ref[s, :, columns] for s in range(ref.shape[0])] + [edge_ref[:, edge]]
    return jnp.concatenate(blocks, axis=1).astype(F32)


def fine_shifts(x_ref, edge_ref, fine_ref, frames, span):
    for m in range(MICROS):
        x = joined(x_ref, edge_ref, m, frames)
        for fine in range(FINE):
            fine_ref[fine * CG : (fine + 1) * CG, m * span : (m + 1) * span] = lane_roll(
                x, HALF - fine
            ).astype(BF16)


def store_frames(out_ref, micro, frames, total):
    for s in range(out_ref.shape[0]):
        out_ref[s, :, micro * frames : (micro + 1) * frames] = total[
            :, s * frames : (s + 1) * frames
        ].astype(BF16)


def position_kernel(span, frames, x_ref, edge_ref, w_ref, out_ref, fine_ref):
    fine_shifts(x_ref, edge_ref, fine_ref, frames, span)
    weights = w_ref[...].reshape(COARSE * CG, FINE * CG)
    for m in range(MICROS):
        terms = jnp.dot(
            weights, fine_ref[:, m * span : (m + 1) * span], preferred_element_type=F32
        )
        total = terms[:CG]
        for coarse in range(1, COARSE):
            total += lane_roll(terms[coarse * CG : (coarse + 1) * CG], -FINE * coarse)
        store_frames(out_ref, m, frames, total)


def position_back_kernel(
    span, frames, x_ref, x_edge_ref, g_ref, g_edge_ref, w_ref, dx_ref, dw_ref,
    fine_ref, coarse_ref, own_ref,
):
    fine_shifts(x_ref, x_edge_ref, fine_ref, frames, span)
    column = lax.broadcasted_iota(jnp.int32, (CG, span), 1)
    for m in range(MICROS):
        columns = slice(m * span, (m + 1) * span)
        g = joined(g_ref, g_edge_ref, m, frames)
        own = jnp.where(column < span - POS_K, g, 0.0)
        for coarse in range(COARSE):
            rows = slice(coarse * CG, (coarse + 1) * CG)
            back = FINE * (COARSE - 1 - coarse)
            coarse_ref[rows, columns] = lane_roll(g, HALF - back).astype(BF16)
            own_ref[rows, columns] = lane_roll(own, FINE * coarse).astype(BF16)
    weights = w_ref[...].reshape(COARSE * CG, FINE * CG)
    turned = weights.astype(F32).T.astype(BF16)
    for m in range(MICROS):
        terms = jnp.dot(
            turned, coarse_ref[:, m * span : (m + 1) * span], preferred_element_type=F32
        )
        total = lane_roll(terms[:CG], -FINE)
        for fine in range(1, FINE):
            total += lane_roll(terms[fine * CG : (fine + 1) * CG], fine - FINE)
        store_frames(dx_ref, m, frames, total)
    grad = lax.dot_general(
        own_ref[...], fine_ref[...], (((1,), (1,)), ((), ())), preferred_element_type=F32
    )
    dw_ref[...] = grad.astype(BF16).reshape(COARSE, CG, FINE * CG)


def group_specs(count, columns):
    wide = pl.BlockSpec((count, CG, columns), lambda g: (0, g, 0))
    edge = pl.BlockSpec((CG, MICROS * POS_K), lambda g: (g, 0))
    weight = pl.BlockSpec((COARSE, CG, FINE * CG), lambda g: (0, g, 0))
    return wide, edge, weight


def position_conv(x, edge, weights):
    count, channels, columns = x.shape
    frames = columns // MICROS
    span = count * frames + POS_K
    groups = channels // CG
    wide, edge_spec, weight = group_specs(count, columns)
    return pl.pallas_call(
        lambda *refs: position_kernel(span, frames, *refs),
        grid=(groups,),
        in_specs=[wide, edge_spec, weight],
        out_specs=wide,
        out_shape=jax.ShapeDtypeStruct(x.shape, BF16),
        scratch_shapes=[pltpu.VMEM((FINE * CG, MICROS * span), BF16)],
        compiler_params=pltpu.CompilerParams(vmem_limit_bytes=VMEM),
        cost_estimate=pl.CostEstimate(flops=0, bytes_accessed=0, transcendentals=0),
        name="position_conv",
    )(x, edge, weights)


def position_back(x, x_edge, grad, grad_edge, weights):
    count, channels, columns = x.shape
    frames = columns // MICROS
    span = count * frames + POS_K
    groups = channels // CG
    wide, edge_spec, weight = group_specs(count, columns)
    return pl.pallas_call(
        lambda *refs: position_back_kernel(span, frames, *refs),
        grid=(groups,),
        in_specs=[wide, edge_spec, wide, edge_spec, weight],
        out_specs=[wide, weight],
        out_shape=[
            jax.ShapeDtypeStruct(x.shape, BF16),
            jax.ShapeDtypeStruct(weights.shape, BF16),
        ],
        scratch_shapes=[
            pltpu.VMEM((FINE * CG, MICROS * span), BF16),
            pltpu.VMEM((COARSE * CG, MICROS * span), BF16),
            pltpu.VMEM((COARSE * CG, MICROS * span), BF16),
        ],
        compiler_params=pltpu.CompilerParams(vmem_limit_bytes=VMEM),
        cost_estimate=pl.CostEstimate(flops=0, bytes_accessed=0, transcendentals=0),
        name="position_back",
    )(x, x_edge, grad, grad_edge, weights)


def side_by_side(ref):
    return jnp.concatenate([ref[s, 0] for s in range(ref.shape[0])], axis=1)


def turn(value):
    return value.astype(F32).T.astype(BF16)


def attention_kernel(block, q_ref, k_ref, v_ref, seg_q_ref, seg_k_ref, out_ref):
    queries = turn(side_by_side(q_ref))
    keys = side_by_side(k_ref)
    values = side_by_side(v_ref)
    frames = out_ref.shape[2]
    factor = HEAD_DIM**-0.5 * LOG2E
    for first in range(0, queries.shape[0], block):
        rows = slice(first, first + block)
        scores = jnp.dot(queries[rows], keys, preferred_element_type=F32)
        expo = jnp.where(seg_q_ref[rows] == seg_k_ref[...], jnp.exp2(scores * factor), 0.0)
        weight_sum = jnp.sum(expo, axis=1, keepdims=True)
        accum = lax.dot_general(
            expo.astype(BF16), values, (((1,), (1,)), ((), ())), preferred_element_type=F32
        )
        context = (accum / weight_sum).T
        for part in range(block // frames):
            out_ref[first // frames + part] = context[:, part * frames : (part + 1) * frames]


def attention_back_kernel(
    block, q_ref, k_ref, v_ref, cg_ref, ctx_ref, seg_q_ref, seg_k_ref,
    dq_ref, dk_ref, dv_ref, dk_sum, dv_sum,
):
    keys_across = side_by_side(k_ref)
    keys = turn(keys_across)
    values = turn(side_by_side(v_ref))
    frames = ctx_ref.shape[2]
    parts = block // frames
    scale = HEAD_DIM**-0.5
    for step in range(q_ref.shape[0] // parts):
        some = range(step * parts, (step + 1) * parts)
        columns = slice(step * block, (step + 1) * block)
        queries = jnp.concatenate([q_ref[s, 0] for s in some], axis=1)
        context_grad = jnp.concatenate([cg_ref[s].astype(F32) for s in some], axis=1)
        context = jnp.concatenate([ctx_ref[s] for s in some], axis=1)
        scores = jnp.dot(keys, queries, preferred_element_type=F32)
        expo = jnp.where(
            seg_k_ref[...] == seg_q_ref[:, columns], jnp.exp2(scores * (scale * LOG2E)), 0.0
        )
        inverse = 1.0 / jnp.sum(expo, axis=0, keepdims=True)
        accum_g = (context_grad * inverse).astype(BF16)
        correction = jnp.sum(context_grad * context, axis=0, keepdims=True) * inverse
        dots = jnp.dot(values, accum_g, preferred_element_type=F32)
        score_g = (expo * (dots - correction)).astype(BF16)
        query_grad = jnp.dot(keys_across, score_g, preferred_element_type=F32) * scale
        for part, s in enumerate(some):
            dq_ref[s] = query_grad[:, part * frames : (part + 1) * frames].astype(BF16)
        key_grad = lax.dot_general(
            score_g, queries, (((1,), (1,)), ((), ())), preferred_element_type=F32
        )
        value_grad = lax.dot_general(
            expo.astype(BF16), accum_g, (((1,), (1,)), ((), ())), preferred_element_type=F32
        )
        if step == 0:
            dk_sum[...] = key_grad
            dv_sum[...] = value_grad
        else:
            dk_sum[...] += key_grad
            dv_sum[...] += value_grad
    key_total = (dk_sum[...] * scale).T.astype(BF16)
    value_total = dv_sum[...].T.astype(BF16)
    for s in range(dk_ref.shape[0]):
        dk_ref[s] = key_total[:, s * frames : (s + 1) * frames]
        dv_ref[s] = value_total[:, s * frames : (s + 1) * frames]


def head_spec(count, frames, which):
    return pl.BlockSpec((count, 1, HEAD_DIM, frames), lambda h: (0, which, h, 0))


def plain_spec(count, frames):
    return pl.BlockSpec((count, HEAD_DIM, frames), lambda h: (0, h, 0))


def whole_spec(array):
    return pl.BlockSpec(array.shape, lambda h: (0,) * array.ndim)


def attention(mixed, mixed_all, seg_q, seg_k):
    count, _, channels, frames = mixed.shape
    total = mixed_all.shape[0]
    heads = channels // HEAD_DIM
    block = math.gcd(count, 2) * frames
    seg_q, seg_k = seg_q[:, None], seg_k[None]
    return pl.pallas_call(
        lambda *refs: attention_kernel(block, *refs),
        grid=(heads,),
        in_specs=[
            head_spec(count, frames, 0),
            head_spec(total, frames, 1),
            head_spec(total, frames, 2),
            whole_spec(seg_q),
            whole_spec(seg_k),
        ],
        out_specs=plain_spec(count, frames),
        out_shape=jax.ShapeDtypeStruct((count, channels, frames), F32),
        compiler_params=pltpu.CompilerParams(vmem_limit_bytes=VMEM),
        cost_estimate=pl.CostEstimate(flops=0, bytes_accessed=0, transcendentals=0),
        name="attention",
    )(mixed, mixed_all, mixed_all, seg_q, seg_k)


def attention_back(mixed, mixed_all, context_grad, context, seg_q, seg_k):
    count, _, channels, frames = mixed.shape
    total = mixed_all.shape[0]
    heads = channels // HEAD_DIM
    block = math.gcd(count, 2) * frames
    seg_q, seg_k = seg_q[None], seg_k[:, None]
    return pl.pallas_call(
        lambda *refs: attention_back_kernel(block, *refs),
        grid=(heads,),
        in_specs=[
            head_spec(count, frames, 0),
            head_spec(total, frames, 1),
            head_spec(total, frames, 2),
            plain_spec(count, frames),
            plain_spec(count, frames),
            whole_spec(seg_q),
            whole_spec(seg_k),
        ],
        out_specs=[
            plain_spec(count, frames),
            plain_spec(total, frames),
            plain_spec(total, frames),
        ],
        out_shape=[
            jax.ShapeDtypeStruct((count, channels, frames), BF16),
            jax.ShapeDtypeStruct((total, channels, frames), BF16),
            jax.ShapeDtypeStruct((total, channels, frames), BF16),
        ],
        scratch_shapes=[pltpu.VMEM((total * frames, HEAD_DIM), F32)] * 2,
        compiler_params=pltpu.CompilerParams(vmem_limit_bytes=VMEM),
        cost_estimate=pl.CostEstimate(flops=0, bytes_accessed=0, transcendentals=0),
        name="attention_back",
    )(mixed, mixed_all, mixed_all, context_grad, context, seg_q, seg_k)


def gate_and_slope(values):
    inner = 0.5 + 0.5 * lax.erf(values * math.sqrt(0.5))
    density = jnp.exp(-0.5 * values * values) * (1.0 / math.sqrt(2.0 * math.pi))
    return values * inner, inner + values * density


def norm_parts(values):
    center = values - jnp.mean(values, axis=1, keepdims=True)
    spread = jnp.mean(center * center, axis=1, keepdims=True)
    rate = lax.rsqrt(spread + NORM_EPS)
    return center * rate, rate


def norm_back(unit, rate, gain, grad):
    scaled = grad * gain
    level = jnp.mean(scaled, axis=1, keepdims=True)
    slope = jnp.mean(scaled * unit, axis=1, keepdims=True)
    return rate * (scaled - level - unit * slope), jnp.sum(grad * unit, axis=0, keepdims=True)


def dot_nt(left, right):
    return lax.dot_general(left, right, (((1,), (1,)), ((), ())), preferred_element_type=F32)


def feed_kernel(
    ctx_ref, out_w_ref, encoded_ref, attention_gain_ref, final_gain_ref, cotangent_ref,
    feed0, feed1, feed2, feed3,
    block_out_ref, mid_ref, context_grad_ref, attention_grad_ref, final_grad_ref,
    settled_ref, hidden_ref, fed_ref, up_ref, branch_ref,
    weights, slopes, sems,
):
    copies = [
        pltpu.make_async_copy(feed, weights.at[k], sems.at[k])
        for k, feed in enumerate((feed0, feed1, feed2, feed3))
    ]
    for copy in copies:
        copy.start()
    kinds, part, frames = ctx_ref.shape
    heads = kinds // MICROS
    width = weights.shape[1]
    units = weights.shape[2] - width
    context = jnp.concatenate(
        [
            jnp.concatenate([ctx_ref[h * MICROS + m] for m in range(MICROS)], axis=1)
            for h in range(heads)
        ],
        axis=0,
    )
    context = turn(context)
    attention_gain = attention_gain_ref[...]
    final_gain = final_gain_ref[...]
    branch = jnp.dot(context, out_w_ref[...], preferred_element_type=F32)
    unit, rate = norm_parts(encoded_ref[...] + branch)
    settled = unit * attention_gain
    settled_low = settled.astype(BF16)
    settled_ref[...] = settled_low
    fed = settled
    for k, copy in enumerate(copies):
        copy.wait()
        columns = slice(k * units, (k + 1) * units)
        up_values = jnp.dot(settled_low, weights[k, :, :units], preferred_element_type=F32)
        hidden, slope = gate_and_slope(up_values)
        slopes[:, columns] = slope
        hidden_low = hidden.astype(BF16)
        hidden_ref[:, columns] = hidden_low
        fed += jnp.dot(hidden_low, weights[k, :, units:], preferred_element_type=F32)
    final_unit, final_rate = norm_parts(fed)
    block_out_ref[...] = final_unit * final_gain
    sum_grad, final_grad_ref[...] = norm_back(
        final_unit, final_rate, final_gain, cotangent_ref[...].astype(F32)
    )
    fed_low = sum_grad.astype(BF16)
    fed_ref[...] = fed_low
    settled_grad = sum_grad
    for k in range(len(copies)):
        columns = slice(k * units, (k + 1) * units)
        up_low = (dot_nt(fed_low, weights[k, :, units:]) * slopes[:, columns]).astype(BF16)
        up_ref[:, columns] = up_low
        settled_grad += dot_nt(up_low, weights[k, :, :units])
    mid_grad, attention_grad_ref[...] = norm_back(unit, rate, attention_gain, settled_grad)
    mid_ref[...] = mid_grad
    branch_low = mid_grad.astype(BF16)
    branch_ref[...] = branch_low
    context_grad = dot_nt(out_w_ref[...], branch_low).astype(BF16)
    for h in range(heads):
        for m in range(MICROS):
            context_grad_ref[h * MICROS + m] = context_grad[
                h * part : (h + 1) * part, m * frames : (m + 1) * frames
            ]


def feed_forward(context, out_w, encoded, attention_gain, final_gain, cotangent, feeds):
    rows, width = encoded.shape
    units = feeds[0].shape[1] - width
    wide = len(feeds) * units
    vmem = pl.BlockSpec(memory_space=pltpu.VMEM)
    return pl.pallas_call(
        feed_kernel,
        in_specs=[vmem] * 6 + [pl.BlockSpec(memory_space=pl.ANY)] * 4,
        out_specs=[vmem] * 10,
        out_shape=[
            jax.ShapeDtypeStruct((rows, width), F32),
            jax.ShapeDtypeStruct((rows, width), F32),
            jax.ShapeDtypeStruct(context.shape, BF16),
            jax.ShapeDtypeStruct((1, width), F32),
            jax.ShapeDtypeStruct((1, width), F32),
            jax.ShapeDtypeStruct((rows, width), BF16),
            jax.ShapeDtypeStruct((rows, wide), BF16),
            jax.ShapeDtypeStruct((rows, width), BF16),
            jax.ShapeDtypeStruct((rows, wide), BF16),
            jax.ShapeDtypeStruct((rows, width), BF16),
        ],
        scratch_shapes=[
            pltpu.VMEM((len(feeds), width, width + units), BF16),
            pltpu.VMEM((rows, wide), F32),
            pltpu.SemaphoreType.DMA((len(feeds),)),
        ],
        compiler_params=pltpu.CompilerParams(vmem_limit_bytes=VMEM),
        cost_estimate=pl.CostEstimate(flops=0, bytes_accessed=0, transcendentals=0),
        name="feed_forward",
    )(context, out_w, encoded, attention_gain, final_gain, cotangent, *feeds)


def feed_grad_kernel(settled_ref, up_ref, hidden_ref, fed_ref, out_ref):
    units = up_ref.shape[1]
    up_grad = jnp.dot(turn(settled_ref[...]), up_ref[...], preferred_element_type=F32)
    out_ref[:, :units] = up_grad.astype(BF16)
    down_grad = jnp.dot(turn(hidden_ref[...]), fed_ref[...], preferred_element_type=F32)
    out_ref[:, units:] = down_grad.astype(BF16)


def feed_grad(k, settled, up, hidden, fed):
    rows, width = settled.shape
    units = up.shape[1] // 4
    whole = pl.BlockSpec((rows, width), lambda g: (0, 0))
    block = pl.BlockSpec((rows, units), lambda g: (0, k))
    return pl.pallas_call(
        feed_grad_kernel,
        grid=(1,),
        in_specs=[whole, block, block, whole],
        out_specs=pl.BlockSpec((width, units + width), lambda g: (0, 0)),
        out_shape=jax.ShapeDtypeStruct((width, units + width), BF16),
        compiler_params=pltpu.CompilerParams(vmem_limit_bytes=VMEM),
        cost_estimate=pl.CostEstimate(flops=0, bytes_accessed=0, transcendentals=0),
        name="feed_grad",
    )(settled, up, hidden, fed)


def head_kernel(width, encoded_ref, *refs):
    blocks, out_ref = refs[:-1], refs[-1]
    frames = out_ref.shape[2]
    encoded = encoded_ref[...]
    for k, block in enumerate(blocks):
        mixed = jnp.dot(encoded, block[:, :width], preferred_element_type=F32).T.astype(BF16)
        for m in range(MICROS):
            out_ref[k * MICROS + m] = mixed[:, m * frames : (m + 1) * frames]


def head_projection(encoded, blocks, width):
    rows, depth = encoded.shape
    vmem = pl.BlockSpec(memory_space=pltpu.VMEM)
    shape = (len(blocks) * MICROS, width, rows // MICROS)
    return pl.pallas_call(
        lambda *refs: head_kernel(width, *refs),
        in_specs=[vmem] * (1 + len(blocks)),
        out_specs=vmem,
        out_shape=jax.ShapeDtypeStruct(shape, BF16),
        compiler_params=pltpu.CompilerParams(vmem_limit_bytes=VMEM),
        cost_estimate=pl.CostEstimate(flops=0, bytes_accessed=0, transcendentals=0),
        name="head_projection",
    )(encoded, *blocks)


def head_back_kernel(
    width, mixed_ref, mid_ref, position_ref, projected_ref, gain_ref, block0, block1, block2,
    block3, joined_ref, position_grad_ref, gain_grad_ref,
):
    total = mid_ref[...]
    for k, block in enumerate((block0, block1, block2, block3)):
        pieces = [mixed_ref[k * MICROS + m].astype(F32).T for m in range(MICROS)]
        mixed = jnp.concatenate(pieces, axis=0).astype(BF16)
        total += dot_nt(mixed, block[:, :width])
    position, slope = gate_and_slope(position_ref[...].astype(F32).T)
    unit, rate = norm_parts(projected_ref[...] + position)
    joined, gain_grad_ref[...] = norm_back(unit, rate, gain_ref[...], total)
    joined_ref[...] = joined
    position_grad_ref[...] = (joined * slope).T.astype(BF16)


def head_back(mixed, mid_grad, position, projected, gain, blocks, width):
    rows, depth = mid_grad.shape
    vmem = pl.BlockSpec(memory_space=pltpu.VMEM)
    return pl.pallas_call(
        lambda *refs: head_back_kernel(width, *refs),
        in_specs=[vmem] * (5 + len(blocks)),
        out_specs=[vmem] * 3,
        out_shape=[
            jax.ShapeDtypeStruct((rows, depth), F32),
            jax.ShapeDtypeStruct((depth, rows), BF16),
            jax.ShapeDtypeStruct((1, depth), F32),
        ],
        compiler_params=pltpu.CompilerParams(vmem_limit_bytes=VMEM),
        cost_estimate=pl.CostEstimate(flops=0, bytes_accessed=0, transcendentals=0),
        name="head_back",
    )(mixed, mid_grad, position, projected, gain, *blocks)


def front_kernel(
    stream_ref, back_ref, joined_ref, normed_ref, projection_ref, before_ref, feature_gain_ref,
    unfolded_ref, conv_ref, encoder_ref, attention_ref, final_ref, mask_n_ref, mask_w_ref,
    place0, place1, place2, place3, packed_ref, unfolded_grad_ref,
):
    stream = stream_ref[0]
    projected_grad = (joined_ref[...] + back_ref[...].astype(F32).T).astype(BF16)
    normed_grad = dot_nt(projected_grad, projection_ref[...])
    activated, slope = gate_and_slope(before_ref[...])
    unit, rate = norm_parts(activated)
    activated_grad, feature_grad = norm_back(unit, rate, feature_gain_ref[...], normed_grad)
    before_low = (activated_grad * slope).astype(BF16)
    unfolded_grad_ref[...] = dot_nt(before_low, conv_ref[...])
    conv_grad = jnp.dot(turn(unfolded_ref[...]), before_low, preferred_element_type=F32)
    projection_grad = jnp.dot(turn(normed_ref[...]), projected_grad, preferred_element_type=F32)
    gains = jnp.zeros((mask_n_ref.shape[0], place0.shape[1]), F32)
    for grad, mask, place in (
        (feature_grad, mask_n_ref, place0),
        (encoder_ref[...], mask_w_ref, place1),
        (attention_ref[...], mask_w_ref, place2),
        (final_ref[...], mask_w_ref, place3),
    ):
        gains += jnp.dot((grad * mask[...]).astype(BF16), place[...], preferred_element_type=F32)
    streams, seqs, _, width = packed_ref.shape
    conv_rows = conv_grad.shape[0] // (streams * seqs)
    rows = projection_grad.shape[0] // (streams * seqs)
    first = lax.broadcasted_iota(jnp.int32, (8, gains.shape[1]), 0) == 0
    blank = jnp.zeros((8, width - gains.shape[1]), F32)
    for s in range(seqs):
        for f in range(streams):
            d = s * streams + f
            piece = projection_grad[d * rows : (d + 1) * rows]
            rest = piece[:, width:]
            folded = jnp.concatenate([rest[: rows // 2], rest[rows // 2 :]], axis=1)
            row = jnp.concatenate([jnp.where(first, gains[d : d + 1], 0.0), blank], axis=1)
            block = jnp.concatenate(
                [conv_grad[d * conv_rows : (d + 1) * conv_rows], piece[:, :width], folded, row],
                axis=0,
            )
            packed_ref[f ^ stream, s] = block.astype(BF16)


def front_back(
    stream, back, joined, normed, projection, before, feature_gain, unfolded, conv, gain_grads,
    streams, seqs,
):
    devices = streams * seqs
    narrow, wide = projection.shape
    counts = [narrow // devices] + [wide // devices] * 3
    masks, places, start = [], [], 0
    for size, count in zip((narrow, wide, wide, wide), counts):
        column = np.arange(size)
        masks.append((column[None] // count == np.arange(devices)[:, None]).astype(np.float32))
        place = column[:, None] % count + start == np.arange(128)[None]
        places.append(jnp.asarray(place, BF16))
        start += count
    depth = (conv.shape[0] + narrow + narrow // 2) // devices + 8
    vmem = pl.BlockSpec(memory_space=pltpu.VMEM)
    return pl.pallas_call(
        front_kernel,
        in_specs=[pl.BlockSpec(memory_space=pltpu.SMEM)] + [vmem] * 17,
        out_specs=[vmem] * 2,
        out_shape=[
            jax.ShapeDtypeStruct((streams, seqs, depth, narrow), BF16),
            jax.ShapeDtypeStruct(unfolded.shape, F32),
        ],
        compiler_params=pltpu.CompilerParams(vmem_limit_bytes=VMEM),
        cost_estimate=pl.CostEstimate(flops=0, bytes_accessed=0, transcendentals=0),
        name="front_back",
    )(
        stream, back, joined, normed, projection, before, feature_gain, unfolded, conv,
        *gain_grads, masks[0], masks[1], *places,
    )


def body(
    features,
    lengths,
    conv_weight,
    feature_gain,
    projection_weight,
    position_weight,
    encoder_gain,
    qkv_weight,
    output_weight,
    attention_gain,
    up_weight,
    down_weight,
    final_gain,
    cotangent,
):
    frames = cotangent.shape[2]
    rows = MICROS * frames
    seqs = lax.axis_size("seq")
    streams = lax.axis_size("fsdp")
    devices = seqs * streams
    me = lax.axis_index("seq")
    stream = lax.axis_index("fsdp")
    both = ("seq", "fsdp")
    group = HEAD_PARTS * MICROS
    outer = seqs // group
    near = [[o * group + i for i in range(group)] for o in range(outer)]
    far = [[o * group + i for o in range(outer)] for i in range(group)]

    def near_swap(blocks):
        return lax.all_to_all(blocks, "seq", 0, 0, axis_index_groups=near)

    def seq_sum(blocks):
        shape = (outer, group, -1, blocks.shape[-1])
        blocks = near_swap(blocks.reshape(shape).transpose(1, 0, 2, 3))
        total = jnp.sum(blocks.astype(F32), axis=0)
        if outer == 1:
            return total[0]
        return lax.psum_scatter(total, "seq", scatter_dimension=0, axis_index_groups=far)

    def near_gather(block, again):
        blocks = [block]
        for k in range(1, group):
            pairs = [(i, i - i % group + (i % group ^ k)) for i in range(seqs)]
            blocks.append(lax.ppermute(block if k < 5 else again, "seq", pairs))
        return jnp.stack(flip(blocks, me % group))

    front_rows = (conv_weight.shape[0], projection_weight.size // C_CNN)
    gains = jnp.concatenate([feature_gain, encoder_gain, attention_gain, final_gain])
    front = jnp.concatenate(
        [
            conv_weight,
            projection_weight.reshape(-1, C_CNN),
            jnp.pad(gains[None], ((0, 7), (0, C_CNN - gains.size))),
        ],
        axis=0,
    )
    part = D // HEAD_PARTS
    up_rows = up_weight.shape[0]
    unit_rows = down_weight.shape[0]
    wide = seqs * unit_rows
    up_parts = up_weight.reshape(up_rows, seqs, streams, unit_rows).transpose(2, 0, 1, 3)
    qkv_parts = qkv_weight.reshape(up_rows, 3, streams, part).transpose(2, 0, 1, 3)
    parts = jnp.concatenate(
        [qkv_parts.reshape(streams, up_rows, 3 * part), up_parts.reshape(streams, up_rows, wide)],
        axis=2,
    )
    parts = jnp.concatenate(swap_parts([parts[j] for j in range(streams)], stream), axis=0)
    front_again, parts = lax.optimization_barrier((front, parts))
    front_near = near_gather(front, front_again)
    front = front_near
    if outer > 1:
        front = lax.all_gather(front, "seq", axis=0, tiled=True, axis_index_groups=far)
    front = jnp.stack(flip(gather_blocks(front), stream), axis=1)
    front = front.reshape(devices, -1, C_CNN)
    cut = front_rows[0] + front_rows[1]
    conv_full = front[:, : front_rows[0]].reshape(-1, C_CNN)
    projection_full = front[:, front_rows[0] : cut].reshape(C_CNN, D)
    gains_full = front[:, cut, : gains.size]
    feature_n, model_n = feature_gain.size, encoder_gain.size
    feature_scale = gains_full[:, :feature_n].reshape(-1).astype(F32)
    encoder_scale, attention_scale, final_scale = (
        gains_full[:, feature_n + i * model_n : feature_n + (i + 1) * model_n]
        .reshape(-1)
        .astype(F32)
        for i in range(3)
    )

    share = D // group
    own_rows = position_weight.shape[0]
    taps = after(position_weight, front_near)
    taps = near_swap(taps.T.reshape(group, share, own_rows))

    out_parts = output_weight.reshape(up_rows, streams, part).transpose(1, 0, 2)
    middle = jnp.concatenate([parts[:, : 3 * part], out_parts.reshape(-1, part)], axis=1)
    middle = lax.all_gather(middle, "seq", axis=0, tiled=True)
    feed = jnp.concatenate([parts[:, 3 * part :], down_weight], axis=1)
    feed = lax.all_gather(after(feed, middle), "seq", axis=0, tiled=True)

    ends = jnp.cumsum(lengths[:, 0], axis=-1, dtype=jnp.int32)
    positions = me * frames + jnp.arange(frames + 1, dtype=jnp.int32)
    segments = segment_of(ends, positions)
    same_next = (segments[:, 1:] == segments[:, :-1])[:, :, None]
    pairs = features[:, 0].reshape(MICROS, frames, 2 * C_CNN)
    next_first = shifted(pairs[:, :1, :C_CNN], "seq", -1)
    following = jnp.concatenate([pairs[:, 1:, :C_CNN], next_first], axis=1)
    following = following * same_next.astype(BF16)
    unfolded = jnp.concatenate([pairs, following], axis=2).reshape(rows, 3 * C_CNN)
    before = plain_dot(unfolded, conv_full)
    normed_low = norm_rows(smooth_gate(before), feature_scale).astype(BF16)
    projected = plain_dot(normed_low, projection_full)

    taps = after(taps, projected)
    if outer > 1:
        taps = lax.all_gather(taps, "seq", axis=0, axis_index_groups=far)
    taps = taps.reshape(outer, group, share, own_rows)
    position_full = (
        jnp.stack(flip(gather_blocks(taps), stream))
        .transpose(3, 1, 2, 0, 4)
        .reshape(share, COARSE, FINE * CG)
        .transpose(1, 0, 2)
    )
    middle = gather_blocks(after(middle, projected))

    def to_groups(block):
        across = near_swap(block.reshape(group, share, rows))
        if outer == 1:
            return across, jnp.zeros((share, MICROS * POS_K), BF16)
        first = across[0].reshape(share, MICROS, frames)[:, :, :HALF]
        last = across[-1].reshape(share, MICROS, frames)[:, :, frames - HALF :]
        edge = [shifted(first, "seq", -group), shifted(last, "seq", group)]
        return across, jnp.concatenate(edge, axis=2).reshape(share, MICROS * POS_K)

    window, window_edge = to_groups(projected.astype(BF16).T)
    position = position_conv(window, window_edge, position_full)
    position = near_swap(position).reshape(D, rows)
    position_act = smooth_gate(position.T.astype(F32))
    encoded = norm_rows(projected + position_act, encoder_scale)
    encoded_low = encoded.astype(BF16)

    mixed_heads = head_projection(encoded_low, middle, 3 * part)
    feed = gather_blocks(after(feed, mixed_heads))
    mixed_heads = near_swap(mixed_heads)
    mixed_heads = mixed_heads.reshape(group, 3, part, frames)
    micro_ends = lax.dynamic_index_in_dim(ends, me % MICROS, 0, keepdims=False)
    seg_all = segment_of(micro_ends, jnp.arange(seqs * frames, dtype=jnp.int32))
    seg_own = lax.dynamic_slice_in_dim(
        seg_all, (me // group) * group * frames, group * frames, 0
    )
    output_full = jnp.stack(flip([block[:, 3 * part :] for block in middle], stream))
    output_full = (
        output_full.reshape(streams, seqs, streams, up_rows, part)
        .transpose(1, 0, 3, 2, 4)
        .reshape(HEAD_PARTS, part, D)
    )
    output_full = jnp.concatenate(flip([output_full[j] for j in range(HEAD_PARTS)], stream))
    mixed_heads, output_full = lax.optimization_barrier((mixed_heads, output_full))
    if outer > 1:
        mixed_all = lax.all_gather(
            mixed_heads, "seq", axis=0, tiled=True, axis_index_groups=far
        )
    else:
        mixed_all = mixed_heads
    context_heads = attention(mixed_heads, mixed_all, seg_own, seg_all)
    context_low = near_swap(context_heads.astype(BF16))

    (
        block_out, mid_grad, context_grad, attention_grad, final_grad,
        settled_low, hidden_low, fed_low, up_low, branch_low,
    ) = feed_forward(
        context_low, output_full, encoded, attention_scale[None], final_scale[None],
        cotangent[:, 0].reshape(rows, D), feed,
    )
    context_grad = near_swap(context_grad)
    feed_grads = {
        k: feed_grad(k, settled_low, up_low, hidden_low, fed_low) for k in (1, 3, 2, 0)
    }
    feed_grads = [feed_grads[k] for k in range(streams)]
    context_low = context_low.reshape(HEAD_PARTS, MICROS, part, frames).transpose(0, 2, 1, 3)
    output_grad = plain_dot(context_low.reshape(D, rows), branch_low).astype(BF16)
    output_grad = output_grad.reshape(HEAD_PARTS, part, D)
    output_grad = jnp.stack(flip([output_grad[j] for j in range(HEAD_PARTS)], stream))
    output_grad = (
        output_grad.reshape(seqs, streams, up_rows, streams, part)
        .transpose(1, 0, 3, 2, 4)
        .reshape(streams, D, part)
    )
    output_grads = flip([output_grad[j] for j in range(streams)], stream)

    over_core = [swapped(feed_grads[1], 1), swapped(feed_grads[3], 1)]
    context_grad, feed_grads = lax.optimization_barrier((context_grad, feed_grads))
    dq, dk, dv = attention_back(
        mixed_heads, mixed_all, context_grad, context_heads, seg_own, seg_all
    )
    if outer > 1:
        dk, dv = (
            lax.psum_scatter(
                grad, "seq", scatter_dimension=0, tiled=True, axis_index_groups=far
            )
            for grad in (dk, dv)
        )
    over_core = after(over_core, dq)
    sent = low_sum(feed_grads[2], over_core[1])
    kept = low_sum(feed_grads[0], over_core[0])
    third = sent.shape[0] // 3
    over_x = [swapped(sent[:third], 2)]
    for i in (1, 2):
        piece = after(sent[i * third : (i + 1) * third], over_x[-1])
        over_x.append(swapped(piece, 2))
    feed_sum = low_sum(kept, jnp.concatenate(over_x, axis=0))
    mixed_g = near_swap(jnp.stack([dq, dk, dv], axis=1)).reshape(group, 3 * part, frames)
    joined_grad, position_grad, encoder_grad = head_back(
        mixed_g, mid_grad, position, projected, encoder_scale[None], middle, 3 * part
    )
    mixed_g = mixed_g.reshape(HEAD_PARTS, MICROS, 3 * part, frames).transpose(0, 2, 1, 3)
    mixed_g = mixed_g.reshape(HEAD_PARTS, 3 * part, rows)
    middle_grads = [
        jnp.concatenate(
            [
                lax.dot_general(
                    encoded_low, mixed_g[k], (((0,), (1,)), ((), ())), preferred_element_type=F32
                ).astype(BF16),
                output_grads[k],
            ],
            axis=1,
        )
        for k in range(HEAD_PARTS)
    ]

    grad_window, grad_edge = to_groups(position_grad)
    grad_window, middle_pairs, feed_sum = lax.optimization_barrier(
        (grad_window, pair_sums(middle_grads), feed_sum)
    )
    feed_shard = lax.psum_scatter(feed_sum, "seq", scatter_dimension=0, tiled=True)
    middle_sum = low_sum(middle_pairs[0], swapped(middle_pairs[1], 2))
    block_out = after(block_out, (feed_shard, middle_sum))
    projected_back, taps_grad = position_back(
        window, window_edge, grad_window, grad_edge, position_full
    )


    projected_back = near_swap(projected_back).reshape(D, rows)
    front_grads, unfolded_grad = front_back(
        stream[None], projected_back, joined_grad, normed_low, projection_full, before,
        feature_scale[None], unfolded, conv_full, (encoder_grad, attention_grad, final_grad),
        streams, seqs,
    )
    unfolded_grad = unfolded_grad.reshape(MICROS, frames, 3 * C_CNN)
    middle_shard = seq_sum(after(middle_sum, front_grads))
    taps_grad = after(taps_grad, front_grads)
    following_grad = unfolded_grad[:, :, 2 * C_CNN :] * same_next.astype(F32)
    carried = shifted(following_grad[:, frames - 1 :], "seq", 1)
    even_grad = unfolded_grad[:, :, :C_CNN] + jnp.concatenate(
        [carried, following_grad[:, :-1]], axis=1
    )
    input_grad = jnp.concatenate([even_grad, unfolded_grad[:, :, C_CNN : 2 * C_CNN]], axis=2)
    input_grad = input_grad.reshape(MICROS, 1, 2 * frames, C_CNN)

    front_pairs = pair_sums([front_grads[k] for k in range(streams)])
    front_shard = seq_sum(low_sum(front_pairs[0], swapped(front_pairs[1], 2)))
    feed_shard = after(feed_shard, front_pairs[1])
    middle_shard = after(middle_shard, front_pairs[1])

    taps_grad = (
        taps_grad.transpose(1, 0, 2)
        .reshape(share, outer, group, streams, own_rows)
        .transpose(3, 1, 2, 0, 4)
    )
    taps_grad = reduce_blocks(flip([taps_grad[j] for j in range(streams)], stream))
    if outer > 1:
        taps_grad = lax.psum_scatter(
            taps_grad, "seq", scatter_dimension=0, axis_index_groups=far
        )
    else:
        taps_grad = taps_grad[0]
    position_shard = near_swap(taps_grad).reshape(D, own_rows).T.astype(F32)

    def unswap(block):
        block = block.reshape(streams, up_rows, -1)
        return jnp.stack(swap_parts([block[j] for j in range(streams)], stream)).astype(F32)

    up_shard = (
        unswap(feed_shard[:, :wide])
        .reshape(streams, up_rows, seqs, unit_rows)
        .transpose(1, 2, 0, 3)
        .reshape(up_rows, -1)
    )
    down_shard = feed_shard[:, wide:].astype(F32)
    qkv_shard = (
        unswap(middle_shard[:, : 3 * part])
        .reshape(streams, up_rows, 3, part)
        .transpose(1, 2, 0, 3)
        .reshape(up_rows, -1)
    )
    output_shard = (
        middle_shard[:, 3 * part :]
        .reshape(streams, up_rows, part)
        .transpose(1, 0, 2)
        .reshape(up_rows, D)
        .astype(F32)
    )
    conv_rows, projection_rows = conv_weight.shape[0], projection_weight.shape[0]
    conv_shard = front_shard[:conv_rows]
    cut = conv_rows + projection_rows
    folded = front_shard[cut : cut + projection_rows // 2]
    folded = jnp.concatenate([folded[:, : D - C_CNN], folded[:, D - C_CNN :]], axis=0)
    projection_shard = jnp.concatenate([front_shard[conv_rows:cut], folded], axis=1)
    gain_row = front_shard[cut + projection_rows // 2]
    gain_shards = [
        gain_row[:feature_n],
        *(gain_row[feature_n + i * model_n : feature_n + (i + 1) * model_n] for i in range(3)),
    ]
    return (
        block_out.reshape(MICROS, 1, frames, D),
        input_grad,
        conv_shard,
        gain_shards[0],
        projection_shard,
        position_shard,
        gain_shards[1],
        qkv_shard,
        output_shard,
        gain_shards[2],
        up_shard,
        down_shard,
        gain_shards[3],
    )


def solution(mesh):
    weight, gain = P(("seq", "fsdp"), None), P(("seq", "fsdp"))
    rows = P(None, "fsdp", "seq", None)
    in_specs = (
        rows, P(None, "fsdp", None), weight, gain, weight, weight, gain, weight, weight, gain,
        weight, weight, gain, rows,
    )
    out_specs = (
        rows, rows, weight, gain, weight, weight, gain, weight, weight, gain, weight, weight, gain,
    )
    return jax.shard_map(body, mesh=mesh, in_specs=in_specs, out_specs=out_specs, check_vma=False)
```

```python
import math

import jax
import jax.numpy as jnp
import numpy as np
from jax import lax
from jax.experimental import pallas as pl
from jax.experimental.pallas import tpu as pltpu
from jax.sharding import PartitionSpec as P

D = 768
HEADS = 12
C_CNN = 512
POS_K = 128
GROUPS = 16
HEAD_DIM = 64
CG = 48
HALF = POS_K // 2
FINE = 16
COARSE = POS_K // FINE
HEAD_PARTS = 4
MICROS = 2
LOG2E = 1.4426950408889634
VMEM = 60 * 1024 * 1024

NORM_EPS = 1e-05
F32 = jnp.float32
BF16 = jnp.bfloat16


def shifted(array, axis, by):
    peers = lax.axis_size(axis)
    pairs = [(i, i + by) for i in range(peers) if 0 <= i + by < peers]
    return lax.ppermute(array, axis, pairs)


def flip(blocks, me):
    count = len(blocks)
    return [lax.select_n(me, *(blocks[m ^ k] for m in range(count))) for k in range(count)]


def swapped(array, k):
    count = lax.axis_size("fsdp")
    return lax.ppermute(array, "fsdp", [(i, i ^ k) for i in range(count)])


def swap_parts(parts, me):
    ordered = flip(parts, me)
    return flip([ordered[0]] + [swapped(ordered[k], k) for k in range(1, 4)], me)


def gather_blocks(block):
    over_x = swapped(block, 2)
    return [block, swapped(block, 1), over_x, swapped(over_x, 1)]


def after(value, other):
    return lax.optimization_barrier((value, other))[0]


def low_sum(*terms):
    return sum(term.astype(F32) for term in terms).astype(BF16)


def pair_sums(blocks):
    return low_sum(blocks[0], swapped(blocks[1], 1)), low_sum(blocks[2], swapped(blocks[3], 1))


def reduce_blocks(blocks):
    kept, sent = pair_sums(blocks)
    return low_sum(kept, swapped(sent, 2))


def norm_rows(values, scales):
    center = values - jnp.mean(values, axis=-1, keepdims=True)
    spread = jnp.mean(center * center, axis=-1, keepdims=True)
    return center * lax.rsqrt(spread + NORM_EPS) * scales


def smooth_gate(values):
    return jax.nn.gelu(values, approximate=False)


def segment_of(utterance_ends, positions):
    return jnp.sum(
        (utterance_ends[..., None, :] <= positions[:, None]).astype(jnp.int32),
        axis=-1,
        dtype=jnp.int32,
    )


def plain_dot(left, right):
    return jnp.dot(left, right, preferred_element_type=F32)


def inner_dot(left, right):
    return lax.dot_general(left, right, (((0,), (0,)), ((), ())), preferred_element_type=F32)


def outer_dot(left, right):
    return lax.dot_general(left, right, (((1,), (1,)), ((), ())), preferred_element_type=F32)


def lane_roll(value, shift):
    shift = shift % value.shape[1]
    return pltpu.roll(value, shift, 1) if shift else value


def joined(ref, edge_ref, micro, frames):
    columns = slice(micro * frames, (micro + 1) * frames)
    edge = slice(micro * POS_K, (micro + 1) * POS_K)
    blocks = [ref[s, :, columns] for s in range(ref.shape[0])] + [edge_ref[:, edge]]
    return jnp.concatenate(blocks, axis=1).astype(F32)


def fine_shifts(x_ref, edge_ref, fine_ref, frames, span):
    for m in range(MICROS):
        x = joined(x_ref, edge_ref, m, frames)
        for fine in range(FINE):
            fine_ref[fine * CG : (fine + 1) * CG, m * span : (m + 1) * span] = lane_roll(
                x, HALF - fine
            ).astype(BF16)


def store_frames(out_ref, micro, frames, total):
    for s in range(out_ref.shape[0]):
        out_ref[s, :, micro * frames : (micro + 1) * frames] = total[
            :, s * frames : (s + 1) * frames
        ].astype(BF16)


def position_kernel(span, frames, x_ref, edge_ref, w_ref, out_ref, fine_ref):
    fine_shifts(x_ref, edge_ref, fine_ref, frames, span)
    weights = w_ref[...].reshape(COARSE * CG, FINE * CG)
    for m in range(MICROS):
        terms = jnp.dot(
            weights, fine_ref[:, m * span : (m + 1) * span], preferred_element_type=F32
        )
        total = terms[:CG]
        for coarse in range(1, COARSE):
            total += lane_roll(terms[coarse * CG : (coarse + 1) * CG], -FINE * coarse)
        store_frames(out_ref, m, frames, total)


def position_back_kernel(
    span, frames, x_ref, x_edge_ref, g_ref, g_edge_ref, w_ref, dx_ref, dw_ref,
    fine_ref, coarse_ref, own_ref,
):
    fine_shifts(x_ref, x_edge_ref, fine_ref, frames, span)
    column = lax.broadcasted_iota(jnp.int32, (CG, span), 1)
    for m in range(MICROS):
        columns = slice(m * span, (m + 1) * span)
        g = joined(g_ref, g_edge_ref, m, frames)
        own = jnp.where(column < span - POS_K, g, 0.0)
        for coarse in range(COARSE):
            rows = slice(coarse * CG, (coarse + 1) * CG)
            back = FINE * (COARSE - 1 - coarse)
            coarse_ref[rows, columns] = lane_roll(g, HALF - back).astype(BF16)
            own_ref[rows, columns] = lane_roll(own, FINE * coarse).astype(BF16)
    weights = w_ref[...].reshape(COARSE * CG, FINE * CG)
    turned = weights.astype(F32).T.astype(BF16)
    for m in range(MICROS):
        terms = jnp.dot(
            turned, coarse_ref[:, m * span : (m + 1) * span], preferred_element_type=F32
        )
        total = lane_roll(terms[:CG], -FINE)
        for fine in range(1, FINE):
            total += lane_roll(terms[fine * CG : (fine + 1) * CG], fine - FINE)
        store_frames(dx_ref, m, frames, total)
    grad = lax.dot_general(
        own_ref[...], fine_ref[...], (((1,), (1,)), ((), ())), preferred_element_type=F32
    )
    dw_ref[...] = grad.astype(BF16).reshape(COARSE, CG, FINE * CG)


def group_specs(count, columns):
    wide = pl.BlockSpec((count, CG, columns), lambda g: (0, g, 0))
    edge = pl.BlockSpec((CG, MICROS * POS_K), lambda g: (g, 0))
    weight = pl.BlockSpec((COARSE, CG, FINE * CG), lambda g: (0, g, 0))
    return wide, edge, weight


def position_conv(x, edge, weights):
    count, channels, columns = x.shape
    frames = columns // MICROS
    span = count * frames + POS_K
    groups = channels // CG
    wide, edge_spec, weight = group_specs(count, columns)
    return pl.pallas_call(
        lambda *refs: position_kernel(span, frames, *refs),
        grid=(groups,),
        in_specs=[wide, edge_spec, weight],
        out_specs=wide,
        out_shape=jax.ShapeDtypeStruct(x.shape, BF16),
        scratch_shapes=[pltpu.VMEM((FINE * CG, MICROS * span), BF16)],
        compiler_params=pltpu.CompilerParams(vmem_limit_bytes=VMEM),
        cost_estimate=pl.CostEstimate(flops=0, bytes_accessed=0, transcendentals=0),
        name="position_conv",
    )(x, edge, weights)


def position_back(x, x_edge, grad, grad_edge, weights):
    count, channels, columns = x.shape
    frames = columns // MICROS
    span = count * frames + POS_K
    groups = channels // CG
    wide, edge_spec, weight = group_specs(count, columns)
    return pl.pallas_call(
        lambda *refs: position_back_kernel(span, frames, *refs),
        grid=(groups,),
        in_specs=[wide, edge_spec, wide, edge_spec, weight],
        out_specs=[wide, weight],
        out_shape=[
            jax.ShapeDtypeStruct(x.shape, BF16),
            jax.ShapeDtypeStruct(weights.shape, BF16),
        ],
        scratch_shapes=[
            pltpu.VMEM((FINE * CG, MICROS * span), BF16),
            pltpu.VMEM((COARSE * CG, MICROS * span), BF16),
            pltpu.VMEM((COARSE * CG, MICROS * span), BF16),
        ],
        compiler_params=pltpu.CompilerParams(vmem_limit_bytes=VMEM),
        cost_estimate=pl.CostEstimate(flops=0, bytes_accessed=0, transcendentals=0),
        name="position_back",
    )(x, x_edge, grad, grad_edge, weights)


def side_by_side(ref):
    return jnp.concatenate([ref[s, 0] for s in range(ref.shape[0])], axis=1)


def turn(value):
    return value.astype(F32).T.astype(BF16)


def attention_kernel(block, q_ref, k_ref, v_ref, seg_q_ref, seg_k_ref, out_ref):
    queries = turn(side_by_side(q_ref))
    keys = side_by_side(k_ref)
    values = side_by_side(v_ref)
    frames = out_ref.shape[2]
    factor = HEAD_DIM**-0.5 * LOG2E
    for first in range(0, queries.shape[0], block):
        rows = slice(first, first + block)
        scores = jnp.dot(queries[rows], keys, preferred_element_type=F32)
        expo = jnp.where(seg_q_ref[rows] == seg_k_ref[...], jnp.exp2(scores * factor), 0.0)
        weight_sum = jnp.sum(expo, axis=1, keepdims=True)
        accum = lax.dot_general(
            expo.astype(BF16), values, (((1,), (1,)), ((), ())), preferred_element_type=F32
        )
        context = (accum / weight_sum).T
        for part in range(block // frames):
            out_ref[first // frames + part] = context[:, part * frames : (part + 1) * frames]


def attention_back_kernel(
    block, q_ref, k_ref, v_ref, cg_ref, ctx_ref, seg_q_ref, seg_k_ref,
    dq_ref, dk_ref, dv_ref, dk_sum, dv_sum,
):
    keys_across = side_by_side(k_ref)
    keys = turn(keys_across)
    values = turn(side_by_side(v_ref))
    frames = ctx_ref.shape[2]
    parts = block // frames
    scale = HEAD_DIM**-0.5
    for step in range(q_ref.shape[0] // parts):
        some = range(step * parts, (step + 1) * parts)
        columns = slice(step * block, (step + 1) * block)
        queries = jnp.concatenate([q_ref[s, 0] for s in some], axis=1)
        context_grad = jnp.concatenate([cg_ref[s].astype(F32) for s in some], axis=1)
        context = jnp.concatenate([ctx_ref[s] for s in some], axis=1)
        scores = jnp.dot(keys, queries, preferred_element_type=F32)
        expo = jnp.where(
            seg_k_ref[...] == seg_q_ref[:, columns], jnp.exp2(scores * (scale * LOG2E)), 0.0
        )
        inverse = 1.0 / jnp.sum(expo, axis=0, keepdims=True)
        accum_g = (context_grad * inverse).astype(BF16)
        correction = jnp.sum(context_grad * context, axis=0, keepdims=True) * inverse
        dots = jnp.dot(values, accum_g, preferred_element_type=F32)
        score_g = (expo * (dots - correction)).astype(BF16)
        query_grad = jnp.dot(keys_across, score_g, preferred_element_type=F32) * scale
        for part, s in enumerate(some):
            dq_ref[s] = query_grad[:, part * frames : (part + 1) * frames].astype(BF16)
        key_grad = lax.dot_general(
            score_g, queries, (((1,), (1,)), ((), ())), preferred_element_type=F32
        )
        value_grad = lax.dot_general(
            expo.astype(BF16), accum_g, (((1,), (1,)), ((), ())), preferred_element_type=F32
        )
        if step == 0:
            dk_sum[...] = key_grad
            dv_sum[...] = value_grad
        else:
            dk_sum[...] += key_grad
            dv_sum[...] += value_grad
    key_total = (dk_sum[...] * scale).T.astype(BF16)
    value_total = dv_sum[...].T.astype(BF16)
    for s in range(dk_ref.shape[0]):
        dk_ref[s] = key_total[:, s * frames : (s + 1) * frames]
        dv_ref[s] = value_total[:, s * frames : (s + 1) * frames]


def head_spec(count, frames, which):
    return pl.BlockSpec((count, 1, HEAD_DIM, frames), lambda h: (0, which, h, 0))


def plain_spec(count, frames):
    return pl.BlockSpec((count, HEAD_DIM, frames), lambda h: (0, h, 0))


def whole_spec(array):
    return pl.BlockSpec(array.shape, lambda h: (0,) * array.ndim)


def attention(mixed, mixed_all, seg_q, seg_k):
    count, _, channels, frames = mixed.shape
    total = mixed_all.shape[0]
    heads = channels // HEAD_DIM
    block = math.gcd(count, 2) * frames
    seg_q, seg_k = seg_q[:, None], seg_k[None]
    return pl.pallas_call(
        lambda *refs: attention_kernel(block, *refs),
        grid=(heads,),
        in_specs=[
            head_spec(count, frames, 0),
            head_spec(total, frames, 1),
            head_spec(total, frames, 2),
            whole_spec(seg_q),
            whole_spec(seg_k),
        ],
        out_specs=plain_spec(count, frames),
        out_shape=jax.ShapeDtypeStruct((count, channels, frames), F32),
        compiler_params=pltpu.CompilerParams(vmem_limit_bytes=VMEM),
        cost_estimate=pl.CostEstimate(flops=0, bytes_accessed=0, transcendentals=0),
        name="attention",
    )(mixed, mixed_all, mixed_all, seg_q, seg_k)


def attention_back(mixed, mixed_all, context_grad, context, seg_q, seg_k):
    count, _, channels, frames = mixed.shape
    total = mixed_all.shape[0]
    heads = channels // HEAD_DIM
    block = math.gcd(count, 2) * frames
    seg_q, seg_k = seg_q[None], seg_k[:, None]
    return pl.pallas_call(
        lambda *refs: attention_back_kernel(block, *refs),
        grid=(heads,),
        in_specs=[
            head_spec(count, frames, 0),
            head_spec(total, frames, 1),
            head_spec(total, frames, 2),
            plain_spec(count, frames),
            plain_spec(count, frames),
            whole_spec(seg_q),
            whole_spec(seg_k),
        ],
        out_specs=[
            plain_spec(count, frames),
            plain_spec(total, frames),
            plain_spec(total, frames),
        ],
        out_shape=[
            jax.ShapeDtypeStruct((count, channels, frames), BF16),
            jax.ShapeDtypeStruct((total, channels, frames), BF16),
            jax.ShapeDtypeStruct((total, channels, frames), BF16),
        ],
        scratch_shapes=[pltpu.VMEM((total * frames, HEAD_DIM), F32)] * 2,
        compiler_params=pltpu.CompilerParams(vmem_limit_bytes=VMEM),
        cost_estimate=pl.CostEstimate(flops=0, bytes_accessed=0, transcendentals=0),
        name="attention_back",
    )(mixed, mixed_all, mixed_all, context_grad, context, seg_q, seg_k)


def gate_and_slope(values):
    inner = 0.5 + 0.5 * lax.erf(values * math.sqrt(0.5))
    density = jnp.exp(-0.5 * values * values) * (1.0 / math.sqrt(2.0 * math.pi))
    return values * inner, inner + values * density


def norm_parts(values):
    center = values - jnp.mean(values, axis=1, keepdims=True)
    spread = jnp.mean(center * center, axis=1, keepdims=True)
    rate = lax.rsqrt(spread + NORM_EPS)
    return center * rate, rate


def norm_back(unit, rate, gain, grad):
    scaled = grad * gain
    level = jnp.mean(scaled, axis=1, keepdims=True)
    slope = jnp.mean(scaled * unit, axis=1, keepdims=True)
    return rate * (scaled - level - unit * slope), jnp.sum(grad * unit, axis=0, keepdims=True)


def dot_nt(left, right):
    return lax.dot_general(left, right, (((1,), (1,)), ((), ())), preferred_element_type=F32)


def feed_kernel(
    ctx_ref, out_w_ref, encoded_ref, attention_gain_ref, final_gain_ref, cotangent_ref,
    feed0, feed1, feed2, feed3,
    block_out_ref, mid_ref, context_grad_ref, attention_grad_ref, final_grad_ref,
    settled_ref, hidden_ref, fed_ref, up_ref, branch_ref,
    weights, slopes, sems,
):
    copies = [
        pltpu.make_async_copy(feed, weights.at[k], sems.at[k])
        for k, feed in enumerate((feed0, feed1, feed2, feed3))
    ]
    for copy in copies:
        copy.start()
    kinds, part, frames = ctx_ref.shape
    heads = kinds // MICROS
    width = weights.shape[1]
    units = weights.shape[2] - width
    context = jnp.concatenate(
        [
            jnp.concatenate([ctx_ref[h * MICROS + m] for m in range(MICROS)], axis=1)
            for h in range(heads)
        ],
        axis=0,
    )
    context = turn(context)
    attention_gain = attention_gain_ref[...]
    final_gain = final_gain_ref[...]
    branch = jnp.dot(context, out_w_ref[...], preferred_element_type=F32)
    unit, rate = norm_parts(encoded_ref[...] + branch)
    settled = unit * attention_gain
    settled_low = settled.astype(BF16)
    settled_ref[...] = settled_low
    fed = settled
    for k, copy in enumerate(copies):
        copy.wait()
        columns = slice(k * units, (k + 1) * units)
        up_values = jnp.dot(settled_low, weights[k, :, :units], preferred_element_type=F32)
        hidden, slope = gate_and_slope(up_values)
        slopes[:, columns] = slope
        hidden_low = hidden.astype(BF16)
        hidden_ref[:, columns] = hidden_low
        fed += jnp.dot(hidden_low, weights[k, :, units:], preferred_element_type=F32)
    final_unit, final_rate = norm_parts(fed)
    block_out_ref[...] = final_unit * final_gain
    sum_grad, final_grad_ref[...] = norm_back(
        final_unit, final_rate, final_gain, cotangent_ref[...].astype(F32)
    )
    fed_low = sum_grad.astype(BF16)
    fed_ref[...] = fed_low
    settled_grad = sum_grad
    for k in range(len(copies)):
        columns = slice(k * units, (k + 1) * units)
        up_low = (dot_nt(fed_low, weights[k, :, units:]) * slopes[:, columns]).astype(BF16)
        up_ref[:, columns] = up_low
        settled_grad += dot_nt(up_low, weights[k, :, :units])
    mid_grad, attention_grad_ref[...] = norm_back(unit, rate, attention_gain, settled_grad)
    mid_ref[...] = mid_grad
    branch_low = mid_grad.astype(BF16)
    branch_ref[...] = branch_low
    context_grad = dot_nt(out_w_ref[...], branch_low).astype(BF16)
    for h in range(heads):
        for m in range(MICROS):
            context_grad_ref[h * MICROS + m] = context_grad[
                h * part : (h + 1) * part, m * frames : (m + 1) * frames
            ]


def feed_forward(context, out_w, encoded, attention_gain, final_gain, cotangent, feeds):
    rows, width = encoded.shape
    units = feeds[0].shape[1] - width
    wide = len(feeds) * units
    vmem = pl.BlockSpec(memory_space=pltpu.VMEM)
    return pl.pallas_call(
        feed_kernel,
        in_specs=[vmem] * 6 + [pl.BlockSpec(memory_space=pl.ANY)] * 4,
        out_specs=[vmem] * 10,
        out_shape=[
            jax.ShapeDtypeStruct((rows, width), F32),
            jax.ShapeDtypeStruct((rows, width), F32),
            jax.ShapeDtypeStruct(context.shape, BF16),
            jax.ShapeDtypeStruct((1, width), F32),
            jax.ShapeDtypeStruct((1, width), F32),
            jax.ShapeDtypeStruct((rows, width), BF16),
            jax.ShapeDtypeStruct((rows, wide), BF16),
            jax.ShapeDtypeStruct((rows, width), BF16),
            jax.ShapeDtypeStruct((rows, wide), BF16),
            jax.ShapeDtypeStruct((rows, width), BF16),
        ],
        scratch_shapes=[
            pltpu.VMEM((len(feeds), width, width + units), BF16),
            pltpu.VMEM((rows, wide), F32),
            pltpu.SemaphoreType.DMA((len(feeds),)),
        ],
        compiler_params=pltpu.CompilerParams(vmem_limit_bytes=VMEM),
        cost_estimate=pl.CostEstimate(flops=0, bytes_accessed=0, transcendentals=0),
        name="feed_forward",
    )(context, out_w, encoded, attention_gain, final_gain, cotangent, *feeds)


def feed_grad_kernel(settled_ref, up_ref, hidden_ref, fed_ref, out_ref):
    units = up_ref.shape[1]
    up_grad = jnp.dot(turn(settled_ref[...]), up_ref[...], preferred_element_type=F32)
    out_ref[:, :units] = up_grad.astype(BF16)
    down_grad = jnp.dot(turn(hidden_ref[...]), fed_ref[...], preferred_element_type=F32)
    out_ref[:, units:] = down_grad.astype(BF16)


def feed_grad(k, settled, up, hidden, fed):
    rows, width = settled.shape
    units = up.shape[1] // 4
    whole = pl.BlockSpec((rows, width), lambda g: (0, 0))
    block = pl.BlockSpec((rows, units), lambda g: (0, k))
    return pl.pallas_call(
        feed_grad_kernel,
        grid=(1,),
        in_specs=[whole, block, block, whole],
        out_specs=pl.BlockSpec((width, units + width), lambda g: (0, 0)),
        out_shape=jax.ShapeDtypeStruct((width, units + width), BF16),
        compiler_params=pltpu.CompilerParams(vmem_limit_bytes=VMEM),
        cost_estimate=pl.CostEstimate(flops=0, bytes_accessed=0, transcendentals=0),
        name="feed_grad",
    )(settled, up, hidden, fed)


def head_kernel(width, encoded_ref, *refs):
    blocks, out_ref = refs[:-1], refs[-1]
    frames = out_ref.shape[2]
    encoded = encoded_ref[...]
    for k, block in enumerate(blocks):
        mixed = jnp.dot(encoded, block[:, :width], preferred_element_type=F32).T.astype(BF16)
        for m in range(MICROS):
            out_ref[k * MICROS + m] = mixed[:, m * frames : (m + 1) * frames]


def head_projection(encoded, blocks, width):
    rows, depth = encoded.shape
    vmem = pl.BlockSpec(memory_space=pltpu.VMEM)
    shape = (len(blocks) * MICROS, width, rows // MICROS)
    return pl.pallas_call(
        lambda *refs: head_kernel(width, *refs),
        in_specs=[vmem] * (1 + len(blocks)),
        out_specs=vmem,
        out_shape=jax.ShapeDtypeStruct(shape, BF16),
        compiler_params=pltpu.CompilerParams(vmem_limit_bytes=VMEM),
        cost_estimate=pl.CostEstimate(flops=0, bytes_accessed=0, transcendentals=0),
        name="head_projection",
    )(encoded, *blocks)


def head_back_kernel(
    width, mixed_ref, mid_ref, position_ref, projected_ref, gain_ref, block0, block1, block2,
    block3, joined_ref, position_grad_ref, gain_grad_ref,
):
    total = mid_ref[...]
    for k, block in enumerate((block0, block1, block2, block3)):
        pieces = [mixed_ref[k * MICROS + m].astype(F32).T for m in range(MICROS)]
        mixed = jnp.concatenate(pieces, axis=0).astype(BF16)
        total += dot_nt(mixed, block[:, :width])
    position, slope = gate_and_slope(position_ref[...].astype(F32).T)
    unit, rate = norm_parts(projected_ref[...] + position)
    joined, gain_grad_ref[...] = norm_back(unit, rate, gain_ref[...], total)
    joined_ref[...] = joined
    position_grad_ref[...] = (joined * slope).T.astype(BF16)


def head_back(mixed, mid_grad, position, projected, gain, blocks, width):
    rows, depth = mid_grad.shape
    vmem = pl.BlockSpec(memory_space=pltpu.VMEM)
    return pl.pallas_call(
        lambda *refs: head_back_kernel(width, *refs),
        in_specs=[vmem] * (5 + len(blocks)),
        out_specs=[vmem] * 3,
        out_shape=[
            jax.ShapeDtypeStruct((rows, depth), F32),
            jax.ShapeDtypeStruct((depth, rows), BF16),
            jax.ShapeDtypeStruct((1, depth), F32),
        ],
        compiler_params=pltpu.CompilerParams(vmem_limit_bytes=VMEM),
        cost_estimate=pl.CostEstimate(flops=0, bytes_accessed=0, transcendentals=0),
        name="head_back",
    )(mixed, mid_grad, position, projected, gain, *blocks)


def front_kernel(
    stream_ref, back_ref, joined_ref, normed_ref, projection_ref, before_ref, feature_gain_ref,
    unfolded_ref, conv_ref, encoder_ref, attention_ref, final_ref, mask_n_ref, mask_w_ref,
    place0, place1, place2, place3, packed_ref, unfolded_grad_ref,
):
    stream = stream_ref[0]
    projected_grad = (joined_ref[...] + back_ref[...].astype(F32).T).astype(BF16)
    normed_grad = dot_nt(projected_grad, projection_ref[...])
    activated, slope = gate_and_slope(before_ref[...])
    unit, rate = norm_parts(activated)
    activated_grad, feature_grad = norm_back(unit, rate, feature_gain_ref[...], normed_grad)
    before_low = (activated_grad * slope).astype(BF16)
    unfolded_grad_ref[...] = dot_nt(before_low, conv_ref[...])
    conv_grad = jnp.dot(turn(unfolded_ref[...]), before_low, preferred_element_type=F32)
    projection_grad = jnp.dot(turn(normed_ref[...]), projected_grad, preferred_element_type=F32)
    gains = jnp.zeros((mask_n_ref.shape[0], place0.shape[1]), F32)
    for grad, mask, place in (
        (feature_grad, mask_n_ref, place0),
        (encoder_ref[...], mask_w_ref, place1),
        (attention_ref[...], mask_w_ref, place2),
        (final_ref[...], mask_w_ref, place3),
    ):
        gains += jnp.dot((grad * mask[...]).astype(BF16), place[...], preferred_element_type=F32)
    streams, seqs, _, width = packed_ref.shape
    conv_rows = conv_grad.shape[0] // (streams * seqs)
    rows = projection_grad.shape[0] // (streams * seqs)
    first = lax.broadcasted_iota(jnp.int32, (8, gains.shape[1]), 0) == 0
    blank = jnp.zeros((8, width - gains.shape[1]), F32)
    for s in range(seqs):
        for f in range(streams):
            d = s * streams + f
            piece = projection_grad[d * rows : (d + 1) * rows]
            rest = piece[:, width:]
            folded = jnp.concatenate([rest[: rows // 2], rest[rows // 2 :]], axis=1)
            row = jnp.concatenate([jnp.where(first, gains[d : d + 1], 0.0), blank], axis=1)
            block = jnp.concatenate(
                [conv_grad[d * conv_rows : (d + 1) * conv_rows], piece[:, :width], folded, row],
                axis=0,
            )
            packed_ref[f ^ stream, s] = block.astype(BF16)


def front_back(
    stream, back, joined, normed, projection, before, feature_gain, unfolded, conv, gain_grads,
    streams, seqs,
):
    devices = streams * seqs
    narrow, wide = projection.shape
    counts = [narrow // devices] + [wide // devices] * 3
    masks, places, start = [], [], 0
    for size, count in zip((narrow, wide, wide, wide), counts):
        column = np.arange(size)
        masks.append((column[None] // count == np.arange(devices)[:, None]).astype(np.float32))
        place = column[:, None] % count + start == np.arange(128)[None]
        places.append(jnp.asarray(place, BF16))
        start += count
    depth = (conv.shape[0] + narrow + narrow // 2) // devices + 8
    vmem = pl.BlockSpec(memory_space=pltpu.VMEM)
    return pl.pallas_call(
        front_kernel,
        in_specs=[pl.BlockSpec(memory_space=pltpu.SMEM)] + [vmem] * 17,
        out_specs=[vmem] * 2,
        out_shape=[
            jax.ShapeDtypeStruct((streams, seqs, depth, narrow), BF16),
            jax.ShapeDtypeStruct(unfolded.shape, F32),
        ],
        compiler_params=pltpu.CompilerParams(vmem_limit_bytes=VMEM),
        cost_estimate=pl.CostEstimate(flops=0, bytes_accessed=0, transcendentals=0),
        name="front_back",
    )(
        stream, back, joined, normed, projection, before, feature_gain, unfolded, conv,
        *gain_grads, masks[0], masks[1], *places,
    )


def body(
    features,
    lengths,
    conv_weight,
    feature_gain,
    projection_weight,
    position_weight,
    encoder_gain,
    qkv_weight,
    output_weight,
    attention_gain,
    up_weight,
    down_weight,
    final_gain,
    cotangent,
):
    frames = cotangent.shape[2]
    rows = MICROS * frames
    seqs = lax.axis_size("seq")
    streams = lax.axis_size("fsdp")
    devices = seqs * streams
    me = lax.axis_index("seq")
    stream = lax.axis_index("fsdp")
    both = ("seq", "fsdp")
    group = HEAD_PARTS * MICROS
    outer = seqs // group
    near = [[o * group + i for i in range(group)] for o in range(outer)]
    far = [[o * group + i for o in range(outer)] for i in range(group)]

    def near_swap(blocks):
        return lax.all_to_all(blocks, "seq", 0, 0, axis_index_groups=near)

    def seq_sum(blocks):
        shape = (outer, group, -1, blocks.shape[-1])
        blocks = near_swap(blocks.reshape(shape).transpose(1, 0, 2, 3))
        total = jnp.sum(blocks.astype(F32), axis=0)
        if outer == 1:
            return total[0]
        return lax.psum_scatter(total, "seq", scatter_dimension=0, axis_index_groups=far)

    def near_gather(block, again):
        blocks = [block]
        for k in range(1, group):
            pairs = [(i, i - i % group + (i % group ^ k)) for i in range(seqs)]
            blocks.append(lax.ppermute(block if k < 5 else again, "seq", pairs))
        return jnp.stack(flip(blocks, me % group))

    front_rows = (conv_weight.shape[0], projection_weight.size // C_CNN)
    gains = jnp.concatenate([feature_gain, encoder_gain, attention_gain, final_gain])
    front = jnp.concatenate(
        [
            conv_weight,
            projection_weight.reshape(-1, C_CNN),
            jnp.pad(gains[None], ((0, 7), (0, C_CNN - gains.size))),
        ],
        axis=0,
    )
    part = D // HEAD_PARTS
    up_rows = up_weight.shape[0]
    unit_rows = down_weight.shape[0]
    wide = seqs * unit_rows
    up_parts = up_weight.reshape(up_rows, seqs, streams, unit_rows).transpose(2, 0, 1, 3)
    qkv_parts = qkv_weight.reshape(up_rows, 3, streams, part).transpose(2, 0, 1, 3)
    parts = jnp.concatenate(
        [qkv_parts.reshape(streams, up_rows, 3 * part), up_parts.reshape(streams, up_rows, wide)],
        axis=2,
    )
    parts = jnp.concatenate(swap_parts([parts[j] for j in range(streams)], stream), axis=0)
    front_again, parts = lax.optimization_barrier((front, parts))
    front_near = near_gather(front, front_again)
    front = front_near
    if outer > 1:
        front = lax.all_gather(front, "seq", axis=0, tiled=True, axis_index_groups=far)
    front = jnp.stack(flip(gather_blocks(front), stream), axis=1)
    front = front.reshape(devices, -1, C_CNN)
    cut = front_rows[0] + front_rows[1]
    conv_full = front[:, : front_rows[0]].reshape(-1, C_CNN)
    projection_full = front[:, front_rows[0] : cut].reshape(C_CNN, D)
    gains_full = front[:, cut, : gains.size]
    feature_n, model_n = feature_gain.size, encoder_gain.size
    feature_scale = gains_full[:, :feature_n].reshape(-1).astype(F32)
    encoder_scale, attention_scale, final_scale = (
        gains_full[:, feature_n + i * model_n : feature_n + (i + 1) * model_n]
        .reshape(-1)
        .astype(F32)
        for i in range(3)
    )

    share = D // group
    own_rows = position_weight.shape[0]
    taps = jnp.stack(flip(gather_blocks(position_weight.T), stream), axis=1)
    taps = near_swap(taps.reshape(group, share, streams * own_rows))

    out_parts = output_weight.reshape(up_rows, streams, part).transpose(1, 0, 2)
    quarter = jnp.concatenate(
        [parts[:, : 3 * part], out_parts.reshape(-1, part), parts[:, 3 * part :], down_weight],
        axis=1,
    )
    quarter = lax.all_gather(quarter, "seq", axis=0, tiled=True)

    ends = jnp.cumsum(lengths[:, 0], axis=-1, dtype=jnp.int32)
    positions = me * frames + jnp.arange(frames + 1, dtype=jnp.int32)
    segments = segment_of(ends, positions)
    same_next = (segments[:, 1:] == segments[:, :-1])[:, :, None]
    pairs = features[:, 0].reshape(MICROS, frames, 2 * C_CNN)
    next_first = shifted(pairs[:, :1, :C_CNN], "seq", -1)
    following = jnp.concatenate([pairs[:, 1:, :C_CNN], next_first], axis=1)
    following = following * same_next.astype(BF16)
    unfolded = jnp.concatenate([pairs, following], axis=2).reshape(rows, 3 * C_CNN)
    before = plain_dot(unfolded, conv_full)
    normed_low = norm_rows(smooth_gate(before), feature_scale).astype(BF16)
    projected = plain_dot(normed_low, projection_full)

    if outer > 1:
        taps = lax.all_gather(taps, "seq", axis=0, axis_index_groups=far)
    position_full = (
        taps.reshape(outer, group, share, streams * own_rows)
        .transpose(2, 0, 1, 3)
        .reshape(share, COARSE, FINE * CG)
        .transpose(1, 0, 2)
    )

    def to_groups(block):
        across = near_swap(block.reshape(group, share, rows))
        if outer == 1:
            return across, jnp.zeros((share, MICROS * POS_K), BF16)
        first = across[0].reshape(share, MICROS, frames)[:, :, :HALF]
        last = across[-1].reshape(share, MICROS, frames)[:, :, frames - HALF :]
        edge = [shifted(first, "seq", -group), shifted(last, "seq", group)]
        return across, jnp.concatenate(edge, axis=2).reshape(share, MICROS * POS_K)

    window, window_edge = to_groups(projected.astype(BF16).T)
    position = position_conv(window, window_edge, position_full)
    position, quarter = lax.optimization_barrier((position, quarter))
    middle = gather_blocks(quarter[:, : 4 * part])
    position = near_swap(position).reshape(D, rows)
    feed, position = lax.optimization_barrier((quarter[:, 4 * part :], position))
    feed = gather_blocks(feed)
    position_act = smooth_gate(position.T.astype(F32))
    encoded = norm_rows(projected + position_act, encoder_scale)
    encoded_low = encoded.astype(BF16)

    mixed_heads = head_projection(encoded_low, middle, 3 * part)
    mixed_heads = near_swap(mixed_heads)
    mixed_heads = mixed_heads.reshape(group, 3, part, frames)
    micro_ends = lax.dynamic_index_in_dim(ends, me % MICROS, 0, keepdims=False)
    seg_all = segment_of(micro_ends, jnp.arange(seqs * frames, dtype=jnp.int32))
    seg_own = lax.dynamic_slice_in_dim(
        seg_all, (me // group) * group * frames, group * frames, 0
    )
    output_full = jnp.stack(flip([block[:, 3 * part :] for block in middle], stream))
    output_full = (
        output_full.reshape(streams, seqs, streams, up_rows, part)
        .transpose(1, 0, 3, 2, 4)
        .reshape(HEAD_PARTS, part, D)
    )
    output_full = jnp.concatenate(flip([output_full[j] for j in range(HEAD_PARTS)], stream))
    mixed_heads, output_full = lax.optimization_barrier((mixed_heads, output_full))
    if outer > 1:
        mixed_all = lax.all_gather(
            mixed_heads, "seq", axis=0, tiled=True, axis_index_groups=far
        )
    else:
        mixed_all = mixed_heads
    context_heads = attention(mixed_heads, mixed_all, seg_own, seg_all)
    context_low = near_swap(context_heads.astype(BF16))

    (
        block_out, mid_grad, context_grad, attention_grad, final_grad,
        settled_low, hidden_low, fed_low, up_low, branch_low,
    ) = feed_forward(
        context_low, output_full, encoded, attention_scale[None], final_scale[None],
        cotangent[:, 0].reshape(rows, D), feed,
    )
    context_grad = near_swap(context_grad)
    feed_grads = {
        k: feed_grad(k, settled_low, up_low, hidden_low, fed_low) for k in (1, 3, 2, 0)
    }
    feed_grads = [feed_grads[k] for k in range(streams)]
    context_low = context_low.reshape(HEAD_PARTS, MICROS, part, frames).transpose(0, 2, 1, 3)
    output_grad = plain_dot(context_low.reshape(D, rows), branch_low).astype(BF16)
    output_grad = output_grad.reshape(HEAD_PARTS, part, D)
    output_grad = jnp.stack(flip([output_grad[j] for j in range(HEAD_PARTS)], stream))
    output_grad = (
        output_grad.reshape(seqs, streams, up_rows, streams, part)
        .transpose(1, 0, 3, 2, 4)
        .reshape(streams, D, part)
    )
    output_grads = flip([output_grad[j] for j in range(streams)], stream)

    over_core = [swapped(feed_grads[1], 1), swapped(feed_grads[3], 1)]
    context_grad, feed_grads = lax.optimization_barrier((context_grad, feed_grads))
    dq, dk, dv = attention_back(
        mixed_heads, mixed_all, context_grad, context_heads, seg_own, seg_all
    )
    if outer > 1:
        dk, dv = (
            lax.psum_scatter(
                grad, "seq", scatter_dimension=0, tiled=True, axis_index_groups=far
            )
            for grad in (dk, dv)
        )
    over_core = after(over_core, dq)
    sent = low_sum(feed_grads[2], over_core[1])
    kept = low_sum(feed_grads[0], over_core[0])
    chunk = sent.shape[0] // 4
    over_x = [swapped(sent[:chunk], 2)]
    for i in range(1, 4):
        piece = after(sent[i * chunk : (i + 1) * chunk], over_x[-1])
        over_x.append(swapped(piece, 2))
    feed_sum = low_sum(kept, jnp.concatenate(over_x, axis=0))
    mixed_g = near_swap(jnp.stack([dq, dk, dv], axis=1)).reshape(group, 3 * part, frames)
    joined_grad, position_grad, encoder_grad = head_back(
        mixed_g, mid_grad, position, projected, encoder_scale[None], middle, 3 * part
    )
    mixed_g = mixed_g.reshape(HEAD_PARTS, MICROS, 3 * part, frames).transpose(0, 2, 1, 3)
    mixed_g = mixed_g.reshape(HEAD_PARTS, 3 * part, rows)
    middle_grads = [
        jnp.concatenate(
            [
                lax.dot_general(
                    encoded_low, mixed_g[k], (((0,), (1,)), ((), ())), preferred_element_type=F32
                ).astype(BF16),
                output_grads[k],
            ],
            axis=1,
        )
        for k in range(HEAD_PARTS)
    ]

    grad_window, grad_edge = to_groups(position_grad)
    grad_window, middle_pairs, feed_sum = lax.optimization_barrier(
        (grad_window, pair_sums(middle_grads), feed_sum)
    )
    feed_shard = lax.psum_scatter(feed_sum, "seq", scatter_dimension=0, tiled=True)
    middle_sum = low_sum(middle_pairs[0], swapped(middle_pairs[1], 2))
    projected_back, taps_grad = position_back(
        window, window_edge, grad_window, grad_edge, position_full
    )


    projected_back = near_swap(projected_back).reshape(D, rows)
    projected_back, middle_sum = lax.optimization_barrier((projected_back, middle_sum))
    front_grads, unfolded_grad = front_back(
        stream[None], projected_back, joined_grad, normed_low, projection_full, before,
        feature_scale[None], unfolded, conv_full, (encoder_grad, attention_grad, final_grad),
        streams, seqs,
    )
    unfolded_grad = unfolded_grad.reshape(MICROS, frames, 3 * C_CNN)
    middle_shard = seq_sum(after(middle_sum, front_grads))
    following_grad = unfolded_grad[:, :, 2 * C_CNN :] * same_next.astype(F32)
    carried = shifted(following_grad[:, frames - 1 :], "seq", 1)
    even_grad = unfolded_grad[:, :, :C_CNN] + jnp.concatenate(
        [carried, following_grad[:, :-1]], axis=1
    )
    input_grad = jnp.concatenate([even_grad, unfolded_grad[:, :, C_CNN : 2 * C_CNN]], axis=2)
    input_grad = input_grad.reshape(MICROS, 1, 2 * frames, C_CNN)

    front_pairs = pair_sums([front_grads[k] for k in range(streams)])
    taps_grad = after(taps_grad, front_pairs[1])
    front_sum = low_sum(front_pairs[0], swapped(front_pairs[1], 2))
    front_sum, feed_shard = lax.optimization_barrier((front_sum, feed_shard))
    front_shard = seq_sum(front_sum)
    front_shard, middle_shard = lax.optimization_barrier((front_shard, middle_shard))

    taps_grad = (
        taps_grad.transpose(1, 0, 2)
        .reshape(share, outer, group, streams, own_rows)
        .transpose(3, 1, 2, 0, 4)
    )
    taps_grad = reduce_blocks(flip([taps_grad[j] for j in range(streams)], stream))
    if outer > 1:
        taps_grad = lax.psum_scatter(
            taps_grad, "seq", scatter_dimension=0, axis_index_groups=far
        )
    else:
        taps_grad = taps_grad[0]
    position_shard = near_swap(taps_grad).reshape(D, own_rows).T.astype(F32)

    def unswap(block):
        block = block.reshape(streams, up_rows, -1)
        return jnp.stack(swap_parts([block[j] for j in range(streams)], stream)).astype(F32)

    up_shard = (
        unswap(feed_shard[:, :wide])
        .reshape(streams, up_rows, seqs, unit_rows)
        .transpose(1, 2, 0, 3)
        .reshape(up_rows, -1)
    )
    down_shard = feed_shard[:, wide:].astype(F32)
    qkv_shard = (
        unswap(middle_shard[:, : 3 * part])
        .reshape(streams, up_rows, 3, part)
        .transpose(1, 2, 0, 3)
        .reshape(up_rows, -1)
    )
    output_shard = (
        middle_shard[:, 3 * part :]
        .reshape(streams, up_rows, part)
        .transpose(1, 0, 2)
        .reshape(up_rows, D)
        .astype(F32)
    )
    conv_rows, projection_rows = conv_weight.shape[0], projection_weight.shape[0]
    conv_shard = front_shard[:conv_rows]
    cut = conv_rows + projection_rows
    folded = front_shard[cut : cut + projection_rows // 2]
    folded = jnp.concatenate([folded[:, : D - C_CNN], folded[:, D - C_CNN :]], axis=0)
    projection_shard = jnp.concatenate([front_shard[conv_rows:cut], folded], axis=1)
    gain_row = front_shard[cut + projection_rows // 2]
    gain_shards = [
        gain_row[:feature_n],
        *(gain_row[feature_n + i * model_n : feature_n + (i + 1) * model_n] for i in range(3)),
    ]
    return (
        block_out.reshape(MICROS, 1, frames, D),
        input_grad,
        conv_shard,
        gain_shards[0],
        projection_shard,
        position_shard,
        gain_shards[1],
        qkv_shard,
        output_shard,
        gain_shards[2],
        up_shard,
        down_shard,
        gain_shards[3],
    )


def solution(mesh):
    weight, gain = P(("seq", "fsdp"), None), P(("seq", "fsdp"))
    rows = P(None, "fsdp", "seq", None)
    in_specs = (
        rows, P(None, "fsdp", None), weight, gain, weight, weight, gain, weight, weight, gain,
        weight, weight, gain, rows,
    )
    out_specs = (
        rows, rows, weight, gain, weight, weight, gain, weight, weight, gain, weight, weight, gain,
    )
    return jax.shard_map(body, mesh=mesh, in_specs=in_specs, out_specs=out_specs, check_vma=False)
```

```python
import math

import jax
import jax.numpy as jnp
import numpy as np
from jax import lax
from jax.experimental import pallas as pl
from jax.experimental.pallas import tpu as pltpu
from jax.sharding import PartitionSpec as P

D = 768
HEADS = 12
C_CNN = 512
POS_K = 128
GROUPS = 16
HEAD_DIM = 64
CG = 48
HALF = POS_K // 2
FINE = 16
COARSE = POS_K // FINE
HEAD_PARTS = 4
MICROS = 2
LOG2E = 1.4426950408889634
VMEM = 60 * 1024 * 1024

NORM_EPS = 1e-05
F32 = jnp.float32
BF16 = jnp.bfloat16


def shifted(array, axis, by):
    peers = lax.axis_size(axis)
    pairs = [(i, i + by) for i in range(peers) if 0 <= i + by < peers]
    return lax.ppermute(array, axis, pairs)


def flip(blocks, me):
    count = len(blocks)
    return [lax.select_n(me, *(blocks[m ^ k] for m in range(count))) for k in range(count)]


def swapped(array, k):
    count = lax.axis_size("fsdp")
    return lax.ppermute(array, "fsdp", [(i, i ^ k) for i in range(count)])


def swap_parts(parts, me):
    ordered = flip(parts, me)
    return flip([ordered[0]] + [swapped(ordered[k], k) for k in range(1, 4)], me)


def gather_blocks(block):
    over_x = swapped(block, 2)
    return [block, swapped(block, 1), over_x, swapped(over_x, 1)]


def after(value, other):
    return lax.optimization_barrier((value, other))[0]


def low_sum(*terms):
    return sum(term.astype(F32) for term in terms).astype(BF16)


def pair_sums(blocks):
    return low_sum(blocks[0], swapped(blocks[1], 1)), low_sum(blocks[2], swapped(blocks[3], 1))


def reduce_blocks(blocks):
    kept, sent = pair_sums(blocks)
    return low_sum(kept, swapped(sent, 2))


def norm_rows(values, scales):
    center = values - jnp.mean(values, axis=-1, keepdims=True)
    spread = jnp.mean(center * center, axis=-1, keepdims=True)
    return center * lax.rsqrt(spread + NORM_EPS) * scales


def smooth_gate(values):
    return jax.nn.gelu(values, approximate=False)


def segment_of(utterance_ends, positions):
    return jnp.sum(
        (utterance_ends[..., None, :] <= positions[:, None]).astype(jnp.int32),
        axis=-1,
        dtype=jnp.int32,
    )


def plain_dot(left, right):
    return jnp.dot(left, right, preferred_element_type=F32)


def inner_dot(left, right):
    return lax.dot_general(left, right, (((0,), (0,)), ((), ())), preferred_element_type=F32)


def outer_dot(left, right):
    return lax.dot_general(left, right, (((1,), (1,)), ((), ())), preferred_element_type=F32)


def lane_roll(value, shift):
    shift = shift % value.shape[1]
    return pltpu.roll(value, shift, 1) if shift else value


def joined(ref, edge_ref, micro, frames):
    columns = slice(micro * frames, (micro + 1) * frames)
    edge = slice(micro * POS_K, (micro + 1) * POS_K)
    blocks = [ref[s, :, columns] for s in range(ref.shape[0])] + [edge_ref[:, edge]]
    return jnp.concatenate(blocks, axis=1).astype(F32)


def fine_shifts(x_ref, edge_ref, fine_ref, frames, span):
    for m in range(MICROS):
        x = joined(x_ref, edge_ref, m, frames)
        for fine in range(FINE):
            fine_ref[fine * CG : (fine + 1) * CG, m * span : (m + 1) * span] = lane_roll(
                x, HALF - fine
            ).astype(BF16)


def store_frames(out_ref, micro, frames, total):
    for s in range(out_ref.shape[0]):
        out_ref[s, :, micro * frames : (micro + 1) * frames] = total[
            :, s * frames : (s + 1) * frames
        ].astype(BF16)


def position_kernel(span, frames, x_ref, edge_ref, w_ref, out_ref, fine_ref):
    fine_shifts(x_ref, edge_ref, fine_ref, frames, span)
    weights = w_ref[...].reshape(COARSE * CG, FINE * CG)
    for m in range(MICROS):
        terms = jnp.dot(
            weights, fine_ref[:, m * span : (m + 1) * span], preferred_element_type=F32
        )
        total = terms[:CG]
        for coarse in range(1, COARSE):
            total += lane_roll(terms[coarse * CG : (coarse + 1) * CG], -FINE * coarse)
        store_frames(out_ref, m, frames, total)


def position_back_kernel(
    span, frames, x_ref, x_edge_ref, g_ref, g_edge_ref, w_ref, dx_ref, dw_ref,
    fine_ref, coarse_ref, own_ref,
):
    fine_shifts(x_ref, x_edge_ref, fine_ref, frames, span)
    column = lax.broadcasted_iota(jnp.int32, (CG, span), 1)
    for m in range(MICROS):
        columns = slice(m * span, (m + 1) * span)
        g = joined(g_ref, g_edge_ref, m, frames)
        own = jnp.where(column < span - POS_K, g, 0.0)
        for coarse in range(COARSE):
            rows = slice(coarse * CG, (coarse + 1) * CG)
            back = FINE * (COARSE - 1 - coarse)
            coarse_ref[rows, columns] = lane_roll(g, HALF - back).astype(BF16)
            own_ref[rows, columns] = lane_roll(own, FINE * coarse).astype(BF16)
    weights = w_ref[...].reshape(COARSE * CG, FINE * CG)
    turned = weights.astype(F32).T.astype(BF16)
    for m in range(MICROS):
        terms = jnp.dot(
            turned, coarse_ref[:, m * span : (m + 1) * span], preferred_element_type=F32
        )
        total = lane_roll(terms[:CG], -FINE)
        for fine in range(1, FINE):
            total += lane_roll(terms[fine * CG : (fine + 1) * CG], fine - FINE)
        store_frames(dx_ref, m, frames, total)
    grad = lax.dot_general(
        own_ref[...], fine_ref[...], (((1,), (1,)), ((), ())), preferred_element_type=F32
    )
    dw_ref[...] = grad.astype(BF16).reshape(COARSE, CG, FINE * CG)


def group_specs(count, columns):
    wide = pl.BlockSpec((count, CG, columns), lambda g: (0, g, 0))
    edge = pl.BlockSpec((CG, MICROS * POS_K), lambda g: (g, 0))
    weight = pl.BlockSpec((COARSE, CG, FINE * CG), lambda g: (0, g, 0))
    return wide, edge, weight


def position_conv(x, edge, weights):
    count, channels, columns = x.shape
    frames = columns // MICROS
    span = count * frames + POS_K
    groups = channels // CG
    wide, edge_spec, weight = group_specs(count, columns)
    return pl.pallas_call(
        lambda *refs: position_kernel(span, frames, *refs),
        grid=(groups,),
        in_specs=[wide, edge_spec, weight],
        out_specs=wide,
        out_shape=jax.ShapeDtypeStruct(x.shape, BF16),
        scratch_shapes=[pltpu.VMEM((FINE * CG, MICROS * span), BF16)],
        compiler_params=pltpu.CompilerParams(vmem_limit_bytes=VMEM),
        cost_estimate=pl.CostEstimate(flops=0, bytes_accessed=0, transcendentals=0),
        name="position_conv",
    )(x, edge, weights)


def position_back(x, x_edge, grad, grad_edge, weights):
    count, channels, columns = x.shape
    frames = columns // MICROS
    span = count * frames + POS_K
    groups = channels // CG
    wide, edge_spec, weight = group_specs(count, columns)
    return pl.pallas_call(
        lambda *refs: position_back_kernel(span, frames, *refs),
        grid=(groups,),
        in_specs=[wide, edge_spec, wide, edge_spec, weight],
        out_specs=[wide, weight],
        out_shape=[
            jax.ShapeDtypeStruct(x.shape, BF16),
            jax.ShapeDtypeStruct(weights.shape, BF16),
        ],
        scratch_shapes=[
            pltpu.VMEM((FINE * CG, MICROS * span), BF16),
            pltpu.VMEM((COARSE * CG, MICROS * span), BF16),
            pltpu.VMEM((COARSE * CG, MICROS * span), BF16),
        ],
        compiler_params=pltpu.CompilerParams(vmem_limit_bytes=VMEM),
        cost_estimate=pl.CostEstimate(flops=0, bytes_accessed=0, transcendentals=0),
        name="position_back",
    )(x, x_edge, grad, grad_edge, weights)


def side_by_side(ref):
    return jnp.concatenate([ref[s, 0] for s in range(ref.shape[0])], axis=1)


def turn(value):
    return value.astype(F32).T.astype(BF16)


def attention_kernel(block, q_ref, k_ref, v_ref, seg_q_ref, seg_k_ref, out_ref):
    queries = turn(side_by_side(q_ref))
    keys = side_by_side(k_ref)
    values = side_by_side(v_ref)
    frames = out_ref.shape[2]
    factor = HEAD_DIM**-0.5 * LOG2E
    for first in range(0, queries.shape[0], block):
        rows = slice(first, first + block)
        scores = jnp.dot(queries[rows], keys, preferred_element_type=F32)
        expo = jnp.where(seg_q_ref[rows] == seg_k_ref[...], jnp.exp2(scores * factor), 0.0)
        weight_sum = jnp.sum(expo, axis=1, keepdims=True)
        accum = lax.dot_general(
            expo.astype(BF16), values, (((1,), (1,)), ((), ())), preferred_element_type=F32
        )
        context = (accum / weight_sum).T
        for part in range(block // frames):
            out_ref[first // frames + part] = context[:, part * frames : (part + 1) * frames]


def attention_back_kernel(
    block, q_ref, k_ref, v_ref, cg_ref, ctx_ref, seg_q_ref, seg_k_ref,
    dq_ref, dk_ref, dv_ref, dk_sum, dv_sum,
):
    keys_across = side_by_side(k_ref)
    keys = turn(keys_across)
    values = turn(side_by_side(v_ref))
    frames = ctx_ref.shape[2]
    parts = block // frames
    scale = HEAD_DIM**-0.5
    for step in range(q_ref.shape[0] // parts):
        some = range(step * parts, (step + 1) * parts)
        columns = slice(step * block, (step + 1) * block)
        queries = jnp.concatenate([q_ref[s, 0] for s in some], axis=1)
        context_grad = jnp.concatenate([cg_ref[s].astype(F32) for s in some], axis=1)
        context = jnp.concatenate([ctx_ref[s] for s in some], axis=1)
        scores = jnp.dot(keys, queries, preferred_element_type=F32)
        expo = jnp.where(
            seg_k_ref[...] == seg_q_ref[:, columns], jnp.exp2(scores * (scale * LOG2E)), 0.0
        )
        inverse = 1.0 / jnp.sum(expo, axis=0, keepdims=True)
        accum_g = (context_grad * inverse).astype(BF16)
        correction = jnp.sum(context_grad * context, axis=0, keepdims=True) * inverse
        dots = jnp.dot(values, accum_g, preferred_element_type=F32)
        score_g = (expo * (dots - correction)).astype(BF16)
        query_grad = jnp.dot(keys_across, score_g, preferred_element_type=F32) * scale
        for part, s in enumerate(some):
            dq_ref[s] = query_grad[:, part * frames : (part + 1) * frames].astype(BF16)
        key_grad = lax.dot_general(
            score_g, queries, (((1,), (1,)), ((), ())), preferred_element_type=F32
        )
        value_grad = lax.dot_general(
            expo.astype(BF16), accum_g, (((1,), (1,)), ((), ())), preferred_element_type=F32
        )
        if step == 0:
            dk_sum[...] = key_grad
            dv_sum[...] = value_grad
        else:
            dk_sum[...] += key_grad
            dv_sum[...] += value_grad
    key_total = (dk_sum[...] * scale).T.astype(BF16)
    value_total = dv_sum[...].T.astype(BF16)
    for s in range(dk_ref.shape[0]):
        dk_ref[s] = key_total[:, s * frames : (s + 1) * frames]
        dv_ref[s] = value_total[:, s * frames : (s + 1) * frames]


def head_spec(count, frames, which):
    return pl.BlockSpec((count, 1, HEAD_DIM, frames), lambda h: (0, which, h, 0))


def plain_spec(count, frames):
    return pl.BlockSpec((count, HEAD_DIM, frames), lambda h: (0, h, 0))


def whole_spec(array):
    return pl.BlockSpec(array.shape, lambda h: (0,) * array.ndim)


def attention(mixed, mixed_all, seg_q, seg_k):
    count, _, channels, frames = mixed.shape
    total = mixed_all.shape[0]
    heads = channels // HEAD_DIM
    block = math.gcd(count, 2) * frames
    seg_q, seg_k = seg_q[:, None], seg_k[None]
    return pl.pallas_call(
        lambda *refs: attention_kernel(block, *refs),
        grid=(heads,),
        in_specs=[
            head_spec(count, frames, 0),
            head_spec(total, frames, 1),
            head_spec(total, frames, 2),
            whole_spec(seg_q),
            whole_spec(seg_k),
        ],
        out_specs=plain_spec(count, frames),
        out_shape=jax.ShapeDtypeStruct((count, channels, frames), F32),
        compiler_params=pltpu.CompilerParams(vmem_limit_bytes=VMEM),
        cost_estimate=pl.CostEstimate(flops=0, bytes_accessed=0, transcendentals=0),
        name="attention",
    )(mixed, mixed_all, mixed_all, seg_q, seg_k)


def attention_back(mixed, mixed_all, context_grad, context, seg_q, seg_k):
    count, _, channels, frames = mixed.shape
    total = mixed_all.shape[0]
    heads = channels // HEAD_DIM
    block = math.gcd(count, 2) * frames
    seg_q, seg_k = seg_q[None], seg_k[:, None]
    return pl.pallas_call(
        lambda *refs: attention_back_kernel(block, *refs),
        grid=(heads,),
        in_specs=[
            head_spec(count, frames, 0),
            head_spec(total, frames, 1),
            head_spec(total, frames, 2),
            plain_spec(count, frames),
            plain_spec(count, frames),
            whole_spec(seg_q),
            whole_spec(seg_k),
        ],
        out_specs=[
            plain_spec(count, frames),
            plain_spec(total, frames),
            plain_spec(total, frames),
        ],
        out_shape=[
            jax.ShapeDtypeStruct((count, channels, frames), BF16),
            jax.ShapeDtypeStruct((total, channels, frames), BF16),
            jax.ShapeDtypeStruct((total, channels, frames), BF16),
        ],
        scratch_shapes=[pltpu.VMEM((total * frames, HEAD_DIM), F32)] * 2,
        compiler_params=pltpu.CompilerParams(vmem_limit_bytes=VMEM),
        cost_estimate=pl.CostEstimate(flops=0, bytes_accessed=0, transcendentals=0),
        name="attention_back",
    )(mixed, mixed_all, mixed_all, context_grad, context, seg_q, seg_k)


def gate_and_slope(values):
    inner = 0.5 + 0.5 * lax.erf(values * math.sqrt(0.5))
    density = jnp.exp(-0.5 * values * values) * (1.0 / math.sqrt(2.0 * math.pi))
    return values * inner, inner + values * density


def norm_parts(values):
    center = values - jnp.mean(values, axis=1, keepdims=True)
    spread = jnp.mean(center * center, axis=1, keepdims=True)
    rate = lax.rsqrt(spread + NORM_EPS)
    return center * rate, rate


def norm_back(unit, rate, gain, grad):
    scaled = grad * gain
    level = jnp.mean(scaled, axis=1, keepdims=True)
    slope = jnp.mean(scaled * unit, axis=1, keepdims=True)
    return rate * (scaled - level - unit * slope), jnp.sum(grad * unit, axis=0, keepdims=True)


def dot_nt(left, right):
    return lax.dot_general(left, right, (((1,), (1,)), ((), ())), preferred_element_type=F32)


def feed_kernel(
    ctx_ref, out_w_ref, encoded_ref, attention_gain_ref, final_gain_ref, cotangent_ref,
    feed0, feed1, feed2, feed3,
    block_out_ref, mid_ref, context_grad_ref, attention_grad_ref, final_grad_ref,
    settled_ref, hidden_ref, fed_ref, up_ref, branch_ref,
    weights, slopes, sems,
):
    copies = [
        pltpu.make_async_copy(feed, weights.at[k], sems.at[k])
        for k, feed in enumerate((feed0, feed1, feed2, feed3))
    ]
    for copy in copies:
        copy.start()
    kinds, part, frames = ctx_ref.shape
    heads = kinds // MICROS
    width = weights.shape[1]
    units = weights.shape[2] - width
    context = jnp.concatenate(
        [
            jnp.concatenate([ctx_ref[h * MICROS + m] for m in range(MICROS)], axis=1)
            for h in range(heads)
        ],
        axis=0,
    )
    context = turn(context)
    attention_gain = attention_gain_ref[...]
    final_gain = final_gain_ref[...]
    branch = jnp.dot(context, out_w_ref[...], preferred_element_type=F32)
    unit, rate = norm_parts(encoded_ref[...] + branch)
    settled = unit * attention_gain
    settled_low = settled.astype(BF16)
    settled_ref[...] = settled_low
    fed = settled
    for k, copy in enumerate(copies):
        copy.wait()
        columns = slice(k * units, (k + 1) * units)
        up_values = jnp.dot(settled_low, weights[k, :, :units], preferred_element_type=F32)
        hidden, slope = gate_and_slope(up_values)
        slopes[:, columns] = slope
        hidden_low = hidden.astype(BF16)
        hidden_ref[:, columns] = hidden_low
        fed += jnp.dot(hidden_low, weights[k, :, units:], preferred_element_type=F32)
    final_unit, final_rate = norm_parts(fed)
    block_out_ref[...] = final_unit * final_gain
    sum_grad, final_grad_ref[...] = norm_back(
        final_unit, final_rate, final_gain, cotangent_ref[...].astype(F32)
    )
    fed_low = sum_grad.astype(BF16)
    fed_ref[...] = fed_low
    settled_grad = sum_grad
    for k in range(len(copies)):
        columns = slice(k * units, (k + 1) * units)
        up_low = (dot_nt(fed_low, weights[k, :, units:]) * slopes[:, columns]).astype(BF16)
        up_ref[:, columns] = up_low
        settled_grad += dot_nt(up_low, weights[k, :, :units])
    mid_grad, attention_grad_ref[...] = norm_back(unit, rate, attention_gain, settled_grad)
    mid_ref[...] = mid_grad
    branch_low = mid_grad.astype(BF16)
    branch_ref[...] = branch_low
    context_grad = dot_nt(out_w_ref[...], branch_low).astype(BF16)
    for h in range(heads):
        for m in range(MICROS):
            context_grad_ref[h * MICROS + m] = context_grad[
                h * part : (h + 1) * part, m * frames : (m + 1) * frames
            ]


def feed_forward(context, out_w, encoded, attention_gain, final_gain, cotangent, feeds):
    rows, width = encoded.shape
    units = feeds[0].shape[1] - width
    wide = len(feeds) * units
    vmem = pl.BlockSpec(memory_space=pltpu.VMEM)
    return pl.pallas_call(
        feed_kernel,
        in_specs=[vmem] * 6 + [pl.BlockSpec(memory_space=pl.ANY)] * 4,
        out_specs=[vmem] * 10,
        out_shape=[
            jax.ShapeDtypeStruct((rows, width), F32),
            jax.ShapeDtypeStruct((rows, width), F32),
            jax.ShapeDtypeStruct(context.shape, BF16),
            jax.ShapeDtypeStruct((1, width), F32),
            jax.ShapeDtypeStruct((1, width), F32),
            jax.ShapeDtypeStruct((rows, width), BF16),
            jax.ShapeDtypeStruct((rows, wide), BF16),
            jax.ShapeDtypeStruct((rows, width), BF16),
            jax.ShapeDtypeStruct((rows, wide), BF16),
            jax.ShapeDtypeStruct((rows, width), BF16),
        ],
        scratch_shapes=[
            pltpu.VMEM((len(feeds), width, width + units), BF16),
            pltpu.VMEM((rows, wide), F32),
            pltpu.SemaphoreType.DMA((len(feeds),)),
        ],
        compiler_params=pltpu.CompilerParams(vmem_limit_bytes=VMEM),
        cost_estimate=pl.CostEstimate(flops=0, bytes_accessed=0, transcendentals=0),
        name="feed_forward",
    )(context, out_w, encoded, attention_gain, final_gain, cotangent, *feeds)


def feed_grad_kernel(stream_ref, settled_ref, up_ref, hidden_ref, fed_ref, out_ref):
    stream = stream_ref[0]
    seqs, streams, _, _, rows, width = out_ref.shape
    units = up_ref.shape[1] // streams
    settled = turn(settled_ref[...])
    fed = fed_ref[...]
    for k in range(streams):
        f = k ^ stream
        columns = slice(k * units, (k + 1) * units)
        down_grad = jnp.dot(turn(hidden_ref[:, columns]), fed, preferred_element_type=F32)
        up_grad = jnp.dot(settled, up_ref[:, columns], preferred_element_type=F32)
        for s in range(seqs):
            for j in range(streams):
                first = (s * streams + j) * rows
                piece = slice(first, first + rows)
                out_ref[s, f, 0, j] = down_grad[piece].astype(BF16)
                out_ref[s, j, 1, f] = up_grad[piece].astype(BF16)


def feed_grad(stream, settled, up, hidden, fed, seqs):
    rows, width = settled.shape
    streams = up.shape[1] // width
    vmem = pl.BlockSpec(memory_space=pltpu.VMEM)
    shape = (seqs, streams, 2, streams, width // (seqs * streams), width)
    return pl.pallas_call(
        feed_grad_kernel,
        in_specs=[pl.BlockSpec(memory_space=pltpu.SMEM)] + [vmem] * 4,
        out_specs=vmem,
        out_shape=jax.ShapeDtypeStruct(shape, BF16),
        compiler_params=pltpu.CompilerParams(vmem_limit_bytes=VMEM),
        cost_estimate=pl.CostEstimate(flops=0, bytes_accessed=0, transcendentals=0),
        name="feed_grad",
    )(stream, settled, up, hidden, fed)


def head_kernel(width, encoded_ref, *refs):
    blocks, out_ref = refs[:-1], refs[-1]
    frames = out_ref.shape[2]
    encoded = encoded_ref[...]
    for k, block in enumerate(blocks):
        mixed = jnp.dot(encoded, block[:, :width], preferred_element_type=F32).T.astype(BF16)
        for m in range(MICROS):
            out_ref[k * MICROS + m] = mixed[:, m * frames : (m + 1) * frames]


def head_projection(encoded, blocks, width):
    rows, depth = encoded.shape
    vmem = pl.BlockSpec(memory_space=pltpu.VMEM)
    shape = (len(blocks) * MICROS, width, rows // MICROS)
    return pl.pallas_call(
        lambda *refs: head_kernel(width, *refs),
        in_specs=[vmem] * (1 + len(blocks)),
        out_specs=vmem,
        out_shape=jax.ShapeDtypeStruct(shape, BF16),
        compiler_params=pltpu.CompilerParams(vmem_limit_bytes=VMEM),
        cost_estimate=pl.CostEstimate(flops=0, bytes_accessed=0, transcendentals=0),
        name="head_projection",
    )(encoded, *blocks)


def head_back_kernel(
    width, mixed_ref, mid_ref, position_ref, projected_ref, gain_ref, block0, block1, block2,
    block3, joined_ref, position_grad_ref, gain_grad_ref,
):
    total = mid_ref[...]
    for k, block in enumerate((block0, block1, block2, block3)):
        pieces = [mixed_ref[k * MICROS + m].astype(F32).T for m in range(MICROS)]
        mixed = jnp.concatenate(pieces, axis=0).astype(BF16)
        total += dot_nt(mixed, block[:, :width])
    position, slope = gate_and_slope(position_ref[...].astype(F32).T)
    unit, rate = norm_parts(projected_ref[...] + position)
    joined, gain_grad_ref[...] = norm_back(unit, rate, gain_ref[...], total)
    joined_ref[...] = joined
    position_grad_ref[...] = (joined * slope).T.astype(BF16)


def head_back(mixed, mid_grad, position, projected, gain, blocks, width):
    rows, depth = mid_grad.shape
    vmem = pl.BlockSpec(memory_space=pltpu.VMEM)
    return pl.pallas_call(
        lambda *refs: head_back_kernel(width, *refs),
        in_specs=[vmem] * (5 + len(blocks)),
        out_specs=[vmem] * 3,
        out_shape=[
            jax.ShapeDtypeStruct((rows, depth), F32),
            jax.ShapeDtypeStruct((depth, rows), BF16),
            jax.ShapeDtypeStruct((1, depth), F32),
        ],
        compiler_params=pltpu.CompilerParams(vmem_limit_bytes=VMEM),
        cost_estimate=pl.CostEstimate(flops=0, bytes_accessed=0, transcendentals=0),
        name="head_back",
    )(mixed, mid_grad, position, projected, gain, *blocks)


def front_kernel(
    stream_ref, back_ref, joined_ref, normed_ref, projection_ref, before_ref, feature_gain_ref,
    unfolded_ref, conv_ref, encoder_ref, attention_ref, final_ref, mask_n_ref, mask_w_ref,
    place0, place1, place2, place3, packed_ref, unfolded_grad_ref,
):
    stream = stream_ref[0]
    projected_grad = (joined_ref[...] + back_ref[...].astype(F32).T).astype(BF16)
    normed_grad = dot_nt(projected_grad, projection_ref[...])
    activated, slope = gate_and_slope(before_ref[...])
    unit, rate = norm_parts(activated)
    activated_grad, feature_grad = norm_back(unit, rate, feature_gain_ref[...], normed_grad)
    before_low = (activated_grad * slope).astype(BF16)
    unfolded_grad_ref[...] = dot_nt(before_low, conv_ref[...])
    conv_grad = jnp.dot(turn(unfolded_ref[...]), before_low, preferred_element_type=F32)
    projection_grad = jnp.dot(turn(normed_ref[...]), projected_grad, preferred_element_type=F32)
    gains = jnp.zeros((mask_n_ref.shape[0], place0.shape[1]), F32)
    for grad, mask, place in (
        (feature_grad, mask_n_ref, place0),
        (encoder_ref[...], mask_w_ref, place1),
        (attention_ref[...], mask_w_ref, place2),
        (final_ref[...], mask_w_ref, place3),
    ):
        gains += jnp.dot((grad * mask[...]).astype(BF16), place[...], preferred_element_type=F32)
    streams, seqs, _, width = packed_ref.shape
    conv_rows = conv_grad.shape[0] // (streams * seqs)
    rows = projection_grad.shape[0] // (streams * seqs)
    first = lax.broadcasted_iota(jnp.int32, (8, gains.shape[1]), 0) == 0
    blank = jnp.zeros((8, width - gains.shape[1]), F32)
    for s in range(seqs):
        for f in range(streams):
            d = s * streams + f
            piece = projection_grad[d * rows : (d + 1) * rows]
            rest = piece[:, width:]
            folded = jnp.concatenate([rest[: rows // 2], rest[rows // 2 :]], axis=1)
            row = jnp.concatenate([jnp.where(first, gains[d : d + 1], 0.0), blank], axis=1)
            block = jnp.concatenate(
                [conv_grad[d * conv_rows : (d + 1) * conv_rows], piece[:, :width], folded, row],
                axis=0,
            )
            packed_ref[f ^ stream, s] = block.astype(BF16)


def front_back(
    stream, back, joined, normed, projection, before, feature_gain, unfolded, conv, gain_grads,
    streams, seqs,
):
    devices = streams * seqs
    narrow, wide = projection.shape
    counts = [narrow // devices] + [wide // devices] * 3
    masks, places, start = [], [], 0
    for size, count in zip((narrow, wide, wide, wide), counts):
        column = np.arange(size)
        masks.append((column[None] // count == np.arange(devices)[:, None]).astype(np.float32))
        place = column[:, None] % count + start == np.arange(128)[None]
        places.append(jnp.asarray(place, BF16))
        start += count
    depth = (conv.shape[0] + narrow + narrow // 2) // devices + 8
    vmem = pl.BlockSpec(memory_space=pltpu.VMEM)
    return pl.pallas_call(
        front_kernel,
        in_specs=[pl.BlockSpec(memory_space=pltpu.SMEM)] + [vmem] * 17,
        out_specs=[vmem] * 2,
        out_shape=[
            jax.ShapeDtypeStruct((streams, seqs, depth, narrow), BF16),
            jax.ShapeDtypeStruct(unfolded.shape, F32),
        ],
        compiler_params=pltpu.CompilerParams(vmem_limit_bytes=VMEM),
        cost_estimate=pl.CostEstimate(flops=0, bytes_accessed=0, transcendentals=0),
        name="front_back",
    )(
        stream, back, joined, normed, projection, before, feature_gain, unfolded, conv,
        *gain_grads, masks[0], masks[1], *places,
    )


def body(
    features,
    lengths,
    conv_weight,
    feature_gain,
    projection_weight,
    position_weight,
    encoder_gain,
    qkv_weight,
    output_weight,
    attention_gain,
    up_weight,
    down_weight,
    final_gain,
    cotangent,
):
    frames = cotangent.shape[2]
    rows = MICROS * frames
    seqs = lax.axis_size("seq")
    streams = lax.axis_size("fsdp")
    devices = seqs * streams
    me = lax.axis_index("seq")
    stream = lax.axis_index("fsdp")
    both = ("seq", "fsdp")
    group = HEAD_PARTS * MICROS
    outer = seqs // group
    near = [[o * group + i for i in range(group)] for o in range(outer)]
    far = [[o * group + i for o in range(outer)] for i in range(group)]

    def near_swap(blocks):
        return lax.all_to_all(blocks, "seq", 0, 0, axis_index_groups=near)

    def seq_sum(blocks):
        shape = (outer, group, -1, blocks.shape[-1])
        blocks = near_swap(blocks.reshape(shape).transpose(1, 0, 2, 3))
        total = jnp.sum(blocks.astype(F32), axis=0)
        if outer == 1:
            return total[0]
        return lax.psum_scatter(total, "seq", scatter_dimension=0, axis_index_groups=far)

    def near_gather(block, again):
        blocks = [block]
        for k in range(1, group):
            pairs = [(i, i - i % group + (i % group ^ k)) for i in range(seqs)]
            blocks.append(lax.ppermute(block if k < 5 else again, "seq", pairs))
        return jnp.stack(flip(blocks, me % group))

    front_rows = (conv_weight.shape[0], projection_weight.size // C_CNN)
    gains = jnp.concatenate([feature_gain, encoder_gain, attention_gain, final_gain])
    front = jnp.concatenate(
        [
            conv_weight,
            projection_weight.reshape(-1, C_CNN),
            jnp.pad(gains[None], ((0, 7), (0, C_CNN - gains.size))),
        ],
        axis=0,
    )
    part = D // HEAD_PARTS
    up_rows = up_weight.shape[0]
    unit_rows = down_weight.shape[0]
    wide = seqs * unit_rows
    up_parts = up_weight.reshape(up_rows, seqs, streams, unit_rows).transpose(2, 0, 1, 3)
    qkv_parts = qkv_weight.reshape(up_rows, 3, streams, part).transpose(2, 0, 1, 3)
    parts = jnp.concatenate(
        [qkv_parts.reshape(streams, up_rows, 3 * part), up_parts.reshape(streams, up_rows, wide)],
        axis=2,
    )
    parts = jnp.concatenate(swap_parts([parts[j] for j in range(streams)], stream), axis=0)
    front_again, parts = lax.optimization_barrier((front, parts))
    front_near = near_gather(front, front_again)
    front = front_near
    if outer > 1:
        front = lax.all_gather(front, "seq", axis=0, tiled=True, axis_index_groups=far)
    front = jnp.stack(flip(gather_blocks(front), stream), axis=1)
    front = front.reshape(devices, -1, C_CNN)
    cut = front_rows[0] + front_rows[1]
    conv_full = front[:, : front_rows[0]].reshape(-1, C_CNN)
    projection_full = front[:, front_rows[0] : cut].reshape(C_CNN, D)
    gains_full = front[:, cut, : gains.size]
    feature_n, model_n = feature_gain.size, encoder_gain.size
    feature_scale = gains_full[:, :feature_n].reshape(-1).astype(F32)
    encoder_scale, attention_scale, final_scale = (
        gains_full[:, feature_n + i * model_n : feature_n + (i + 1) * model_n]
        .reshape(-1)
        .astype(F32)
        for i in range(3)
    )

    share = D // group
    own_rows = position_weight.shape[0]
    taps = near_swap(after(position_weight, front_near).T.reshape(group, share, own_rows))

    out_parts = output_weight.reshape(up_rows, streams, part).transpose(1, 0, 2)
    quarter = jnp.concatenate(
        [parts[:, : 3 * part], out_parts.reshape(-1, part), parts[:, 3 * part :], down_weight],
        axis=1,
    )
    quarter = lax.all_gather(quarter, "seq", axis=0, tiled=True)

    ends = jnp.cumsum(lengths[:, 0], axis=-1, dtype=jnp.int32)
    positions = me * frames + jnp.arange(frames + 1, dtype=jnp.int32)
    segments = segment_of(ends, positions)
    same_next = (segments[:, 1:] == segments[:, :-1])[:, :, None]
    pairs = features[:, 0].reshape(MICROS, frames, 2 * C_CNN)
    next_first = shifted(pairs[:, :1, :C_CNN], "seq", -1)
    following = jnp.concatenate([pairs[:, 1:, :C_CNN], next_first], axis=1)
    following = following * same_next.astype(BF16)
    unfolded = jnp.concatenate([pairs, following], axis=2).reshape(rows, 3 * C_CNN)
    before = plain_dot(unfolded, conv_full)
    normed_low = norm_rows(smooth_gate(before), feature_scale).astype(BF16)
    projected = plain_dot(normed_low, projection_full)

    if outer > 1:
        taps = lax.all_gather(taps, "seq", axis=0, axis_index_groups=far)
    taps = after(taps.reshape(outer, group, share, own_rows), projected)
    position_full = (
        jnp.stack(flip([taps] + [swapped(taps, k) for k in range(1, 4)], stream))
        .transpose(3, 1, 2, 0, 4)
        .reshape(share, COARSE, FINE * CG)
        .transpose(1, 0, 2)
    )

    def to_groups(block):
        across = near_swap(block.reshape(group, share, rows))
        if outer == 1:
            return across, jnp.zeros((share, MICROS * POS_K), BF16)
        first = across[0].reshape(share, MICROS, frames)[:, :, :HALF]
        last = across[-1].reshape(share, MICROS, frames)[:, :, frames - HALF :]
        edge = [shifted(first, "seq", -group), shifted(last, "seq", group)]
        return across, jnp.concatenate(edge, axis=2).reshape(share, MICROS * POS_K)

    window, window_edge = to_groups(projected.astype(BF16).T)
    position = position_conv(window, window_edge, position_full)
    position, quarter = lax.optimization_barrier((position, quarter))
    middle = gather_blocks(quarter[:, : 4 * part])
    position = near_swap(position).reshape(D, rows)
    feed, position = lax.optimization_barrier((quarter[:, 4 * part :], position))
    feed = gather_blocks(feed)
    position_act = smooth_gate(position.T.astype(F32))
    encoded = norm_rows(projected + position_act, encoder_scale)
    encoded_low = encoded.astype(BF16)

    mixed_heads = head_projection(encoded_low, middle, 3 * part)
    mixed_heads = near_swap(mixed_heads)
    mixed_heads = mixed_heads.reshape(group, 3, part, frames)
    micro_ends = lax.dynamic_index_in_dim(ends, me % MICROS, 0, keepdims=False)
    seg_all = segment_of(micro_ends, jnp.arange(seqs * frames, dtype=jnp.int32))
    seg_own = lax.dynamic_slice_in_dim(
        seg_all, (me // group) * group * frames, group * frames, 0
    )
    output_full = jnp.stack(flip([block[:, 3 * part :] for block in middle], stream))
    output_full = (
        output_full.reshape(streams, seqs, streams, up_rows, part)
        .transpose(1, 0, 3, 2, 4)
        .reshape(HEAD_PARTS, part, D)
    )
    output_full = jnp.concatenate(flip([output_full[j] for j in range(HEAD_PARTS)], stream))
    mixed_heads, output_full = lax.optimization_barrier((mixed_heads, output_full))
    if outer > 1:
        mixed_all = lax.all_gather(
            mixed_heads, "seq", axis=0, tiled=True, axis_index_groups=far
        )
    else:
        mixed_all = mixed_heads
    context_heads = attention(mixed_heads, mixed_all, seg_own, seg_all)
    context_low = near_swap(context_heads.astype(BF16))

    (
        block_out, mid_grad, context_grad, attention_grad, final_grad,
        settled_low, hidden_low, fed_low, up_low, branch_low,
    ) = feed_forward(
        context_low, output_full, encoded, attention_scale[None], final_scale[None],
        cotangent[:, 0].reshape(rows, D), feed,
    )
    context_grad = near_swap(context_grad)
    feed_grads = feed_grad(stream[None], settled_low, up_low, hidden_low, fed_low, seqs)
    context_grad, feed_grads = lax.optimization_barrier((context_grad, feed_grads))
    feed_grads = feed_grads.reshape(devices, -1, D)
    feed_shard = lax.psum_scatter(feed_grads, both, scatter_dimension=0)
    context_low = context_low.reshape(HEAD_PARTS, MICROS, part, frames).transpose(0, 2, 1, 3)
    output_grad = plain_dot(context_low.reshape(D, rows), branch_low).astype(BF16)
    output_grad = output_grad.reshape(HEAD_PARTS, part, D)
    output_grad = jnp.stack(flip([output_grad[j] for j in range(HEAD_PARTS)], stream))
    output_grad = (
        output_grad.reshape(seqs, streams, up_rows, streams, part)
        .transpose(1, 0, 3, 2, 4)
        .reshape(streams, D, part)
    )
    output_grads = flip([output_grad[j] for j in range(streams)], stream)

    dq, dk, dv = attention_back(
        mixed_heads, mixed_all, context_grad, context_heads, seg_own, seg_all
    )
    if outer > 1:
        dk, dv = (
            lax.psum_scatter(
                grad, "seq", scatter_dimension=0, tiled=True, axis_index_groups=far
            )
            for grad in (dk, dv)
        )
    mixed_g = near_swap(jnp.stack([dq, dk, dv], axis=1)).reshape(group, 3 * part, frames)
    joined_grad, position_grad, encoder_grad = head_back(
        mixed_g, mid_grad, position, projected, encoder_scale[None], middle, 3 * part
    )
    mixed_g = mixed_g.reshape(HEAD_PARTS, MICROS, 3 * part, frames).transpose(0, 2, 1, 3)
    mixed_g = mixed_g.reshape(HEAD_PARTS, 3 * part, rows)
    middle_grads = [
        jnp.concatenate(
            [
                lax.dot_general(
                    encoded_low, mixed_g[k], (((0,), (1,)), ((), ())), preferred_element_type=F32
                ).astype(BF16),
                output_grads[k],
            ],
            axis=1,
        )
        for k in range(HEAD_PARTS)
    ]

    grad_window, grad_edge = to_groups(position_grad)
    grad_window, middle_pairs = lax.optimization_barrier((grad_window, pair_sums(middle_grads)))
    middle_sum = low_sum(middle_pairs[0], swapped(middle_pairs[1], 2))
    projected_back, taps_grad = position_back(
        window, window_edge, grad_window, grad_edge, position_full
    )


    projected_back = near_swap(projected_back).reshape(D, rows)
    projected_back, middle_sum = lax.optimization_barrier((projected_back, middle_sum))
    front_grads, unfolded_grad = front_back(
        stream[None], projected_back, joined_grad, normed_low, projection_full, before,
        feature_scale[None], unfolded, conv_full, (encoder_grad, attention_grad, final_grad),
        streams, seqs,
    )
    unfolded_grad = unfolded_grad.reshape(MICROS, frames, 3 * C_CNN)
    middle_shard = seq_sum(after(middle_sum, front_grads))
    following_grad = unfolded_grad[:, :, 2 * C_CNN :] * same_next.astype(F32)
    carried = shifted(following_grad[:, frames - 1 :], "seq", 1)
    even_grad = unfolded_grad[:, :, :C_CNN] + jnp.concatenate(
        [carried, following_grad[:, :-1]], axis=1
    )
    input_grad = jnp.concatenate([even_grad, unfolded_grad[:, :, C_CNN : 2 * C_CNN]], axis=2)
    input_grad = input_grad.reshape(MICROS, 1, 2 * frames, C_CNN)

    front_pairs = pair_sums([front_grads[k] for k in range(streams)])
    taps_grad = after(taps_grad, front_pairs[1])
    front_sum = low_sum(front_pairs[0], swapped(front_pairs[1], 2))
    front_shard = seq_sum(front_sum)
    front_shard, middle_shard = lax.optimization_barrier((front_shard, middle_shard))

    taps_grad = (
        taps_grad.transpose(1, 0, 2)
        .reshape(share, outer, group, streams, own_rows)
        .transpose(3, 1, 2, 0, 4)
    )
    taps_grad = reduce_blocks(flip([taps_grad[j] for j in range(streams)], stream))
    taps_grad = after(taps_grad, front_sum)
    if outer > 1:
        taps_grad = lax.psum_scatter(
            taps_grad, "seq", scatter_dimension=0, axis_index_groups=far
        )
    else:
        taps_grad = taps_grad[0]
    position_shard = near_swap(taps_grad).reshape(D, own_rows).T.astype(F32)

    def unswap(block):
        block = block.reshape(streams, up_rows, -1)
        return jnp.stack(swap_parts([block[j] for j in range(streams)], stream)).astype(F32)

    feed_shard = feed_shard.reshape(2, streams, up_rows, wide).astype(F32)
    down_shard = feed_shard[0].reshape(unit_rows, D)
    up_shard = (
        feed_shard[1]
        .reshape(streams, up_rows, seqs, unit_rows)
        .transpose(1, 2, 0, 3)
        .reshape(up_rows, -1)
    )
    qkv_shard = (
        unswap(middle_shard[:, : 3 * part])
        .reshape(streams, up_rows, 3, part)
        .transpose(1, 2, 0, 3)
        .reshape(up_rows, -1)
    )
    output_shard = (
        middle_shard[:, 3 * part :]
        .reshape(streams, up_rows, part)
        .transpose(1, 0, 2)
        .reshape(up_rows, D)
        .astype(F32)
    )
    conv_rows, projection_rows = conv_weight.shape[0], projection_weight.shape[0]
    conv_shard = front_shard[:conv_rows]
    cut = conv_rows + projection_rows
    folded = front_shard[cut : cut + projection_rows // 2]
    folded = jnp.concatenate([folded[:, : D - C_CNN], folded[:, D - C_CNN :]], axis=0)
    projection_shard = jnp.concatenate([front_shard[conv_rows:cut], folded], axis=1)
    gain_row = front_shard[cut + projection_rows // 2]
    gain_shards = [
        gain_row[:feature_n],
        *(gain_row[feature_n + i * model_n : feature_n + (i + 1) * model_n] for i in range(3)),
    ]
    return (
        block_out.reshape(MICROS, 1, frames, D),
        input_grad,
        conv_shard,
        gain_shards[0],
        projection_shard,
        position_shard,
        gain_shards[1],
        qkv_shard,
        output_shard,
        gain_shards[2],
        up_shard,
        down_shard,
        gain_shards[3],
    )


def solution(mesh):
    weight, gain = P(("seq", "fsdp"), None), P(("seq", "fsdp"))
    rows = P(None, "fsdp", "seq", None)
    in_specs = (
        rows, P(None, "fsdp", None), weight, gain, weight, weight, gain, weight, weight, gain,
        weight, weight, gain, rows,
    )
    out_specs = (
        rows, rows, weight, gain, weight, weight, gain, weight, weight, gain, weight, weight, gain,
    )
    return jax.shard_map(body, mesh=mesh, in_specs=in_specs, out_specs=out_specs, check_vma=False)
```

```python
import math

import jax
import jax.numpy as jnp
import numpy as np
from jax import lax
from jax.experimental import pallas as pl
from jax.experimental.pallas import tpu as pltpu
from jax.sharding import PartitionSpec as P

D = 768
HEADS = 12
C_CNN = 512
POS_K = 128
GROUPS = 16
HEAD_DIM = 64
CG = 48
HALF = POS_K // 2
FINE = 16
COARSE = POS_K // FINE
HEAD_PARTS = 4
MICROS = 2
LOG2E = 1.4426950408889634
VMEM = 60 * 1024 * 1024

NORM_EPS = 1e-05
F32 = jnp.float32
BF16 = jnp.bfloat16


def shifted(array, axis, by):
    peers = lax.axis_size(axis)
    pairs = [(i, i + by) for i in range(peers) if 0 <= i + by < peers]
    return lax.ppermute(array, axis, pairs)


def flip(blocks, me):
    count = len(blocks)
    return [lax.select_n(me, *(blocks[m ^ k] for m in range(count))) for k in range(count)]


def swapped(array, k):
    count = lax.axis_size("fsdp")
    return lax.ppermute(array, "fsdp", [(i, i ^ k) for i in range(count)])


def swap_parts(parts, me):
    ordered = flip(parts, me)
    return flip([ordered[0]] + [swapped(ordered[k], k) for k in range(1, 4)], me)


def gather_blocks(block):
    over_x = swapped(block, 2)
    return [block, swapped(block, 1), over_x, swapped(over_x, 1)]


def after(value, other):
    return lax.optimization_barrier((value, other))[0]


def low_sum(*terms):
    return sum(term.astype(F32) for term in terms).astype(BF16)


def pair_sums(blocks):
    return low_sum(blocks[0], swapped(blocks[1], 1)), low_sum(blocks[2], swapped(blocks[3], 1))


def reduce_blocks(blocks):
    kept, sent = pair_sums(blocks)
    return low_sum(kept, swapped(sent, 2))


def norm_rows(values, scales):
    center = values - jnp.mean(values, axis=-1, keepdims=True)
    spread = jnp.mean(center * center, axis=-1, keepdims=True)
    return center * lax.rsqrt(spread + NORM_EPS) * scales


def smooth_gate(values):
    return jax.nn.gelu(values, approximate=False)


def segment_of(utterance_ends, positions):
    return jnp.sum(
        (utterance_ends[..., None, :] <= positions[:, None]).astype(jnp.int32),
        axis=-1,
        dtype=jnp.int32,
    )


def plain_dot(left, right):
    return jnp.dot(left, right, preferred_element_type=F32)


def inner_dot(left, right):
    return lax.dot_general(left, right, (((0,), (0,)), ((), ())), preferred_element_type=F32)


def outer_dot(left, right):
    return lax.dot_general(left, right, (((1,), (1,)), ((), ())), preferred_element_type=F32)


def lane_roll(value, shift):
    shift = shift % value.shape[1]
    return pltpu.roll(value, shift, 1) if shift else value


def joined(ref, edge_ref, micro, frames):
    columns = slice(micro * frames, (micro + 1) * frames)
    edge = slice(micro * POS_K, (micro + 1) * POS_K)
    blocks = [ref[s, :, columns] for s in range(ref.shape[0])] + [edge_ref[:, edge]]
    return jnp.concatenate(blocks, axis=1).astype(F32)


def fine_shifts(x_ref, edge_ref, fine_ref, frames, span):
    for m in range(MICROS):
        x = joined(x_ref, edge_ref, m, frames)
        for fine in range(FINE):
            fine_ref[fine * CG : (fine + 1) * CG, m * span : (m + 1) * span] = lane_roll(
                x, HALF - fine
            ).astype(BF16)


def store_frames(out_ref, micro, frames, total):
    for s in range(out_ref.shape[0]):
        out_ref[s, :, micro * frames : (micro + 1) * frames] = total[
            :, s * frames : (s + 1) * frames
        ].astype(BF16)


def position_kernel(span, frames, x_ref, edge_ref, w_ref, out_ref, fine_ref):
    fine_shifts(x_ref, edge_ref, fine_ref, frames, span)
    weights = w_ref[...].reshape(COARSE * CG, FINE * CG)
    for m in range(MICROS):
        terms = jnp.dot(
            weights, fine_ref[:, m * span : (m + 1) * span], preferred_element_type=F32
        )
        total = terms[:CG]
        for coarse in range(1, COARSE):
            total += lane_roll(terms[coarse * CG : (coarse + 1) * CG], -FINE * coarse)
        store_frames(out_ref, m, frames, total)


def position_back_kernel(
    span, frames, x_ref, x_edge_ref, g_ref, g_edge_ref, w_ref, dx_ref, dw_ref,
    fine_ref, coarse_ref, own_ref,
):
    fine_shifts(x_ref, x_edge_ref, fine_ref, frames, span)
    column = lax.broadcasted_iota(jnp.int32, (CG, span), 1)
    for m in range(MICROS):
        columns = slice(m * span, (m + 1) * span)
        g = joined(g_ref, g_edge_ref, m, frames)
        own = jnp.where(column < span - POS_K, g, 0.0)
        for coarse in range(COARSE):
            rows = slice(coarse * CG, (coarse + 1) * CG)
            back = FINE * (COARSE - 1 - coarse)
            coarse_ref[rows, columns] = lane_roll(g, HALF - back).astype(BF16)
            own_ref[rows, columns] = lane_roll(own, FINE * coarse).astype(BF16)
    weights = w_ref[...].reshape(COARSE * CG, FINE * CG)
    turned = weights.astype(F32).T.astype(BF16)
    for m in range(MICROS):
        terms = jnp.dot(
            turned, coarse_ref[:, m * span : (m + 1) * span], preferred_element_type=F32
        )
        total = lane_roll(terms[:CG], -FINE)
        for fine in range(1, FINE):
            total += lane_roll(terms[fine * CG : (fine + 1) * CG], fine - FINE)
        store_frames(dx_ref, m, frames, total)
    grad = lax.dot_general(
        own_ref[...], fine_ref[...], (((1,), (1,)), ((), ())), preferred_element_type=F32
    )
    dw_ref[...] = grad.astype(BF16).reshape(COARSE, CG, FINE * CG)


def group_specs(count, columns):
    wide = pl.BlockSpec((count, CG, columns), lambda g: (0, g, 0))
    edge = pl.BlockSpec((CG, MICROS * POS_K), lambda g: (g, 0))
    weight = pl.BlockSpec((COARSE, CG, FINE * CG), lambda g: (0, g, 0))
    return wide, edge, weight


def position_conv(x, edge, weights):
    count, channels, columns = x.shape
    frames = columns // MICROS
    span = count * frames + POS_K
    groups = channels // CG
    wide, edge_spec, weight = group_specs(count, columns)
    return pl.pallas_call(
        lambda *refs: position_kernel(span, frames, *refs),
        grid=(groups,),
        in_specs=[wide, edge_spec, weight],
        out_specs=wide,
        out_shape=jax.ShapeDtypeStruct(x.shape, BF16),
        scratch_shapes=[pltpu.VMEM((FINE * CG, MICROS * span), BF16)],
        compiler_params=pltpu.CompilerParams(vmem_limit_bytes=VMEM),
        cost_estimate=pl.CostEstimate(flops=0, bytes_accessed=0, transcendentals=0),
        name="position_conv",
    )(x, edge, weights)


def position_back(x, x_edge, grad, grad_edge, weights):
    count, channels, columns = x.shape
    frames = columns // MICROS
    span = count * frames + POS_K
    groups = channels // CG
    wide, edge_spec, weight = group_specs(count, columns)
    return pl.pallas_call(
        lambda *refs: position_back_kernel(span, frames, *refs),
        grid=(groups,),
        in_specs=[wide, edge_spec, wide, edge_spec, weight],
        out_specs=[wide, weight],
        out_shape=[
            jax.ShapeDtypeStruct(x.shape, BF16),
            jax.ShapeDtypeStruct(weights.shape, BF16),
        ],
        scratch_shapes=[
            pltpu.VMEM((FINE * CG, MICROS * span), BF16),
            pltpu.VMEM((COARSE * CG, MICROS * span), BF16),
            pltpu.VMEM((COARSE * CG, MICROS * span), BF16),
        ],
        compiler_params=pltpu.CompilerParams(vmem_limit_bytes=VMEM),
        cost_estimate=pl.CostEstimate(flops=0, bytes_accessed=0, transcendentals=0),
        name="position_back",
    )(x, x_edge, grad, grad_edge, weights)


def side_by_side(ref):
    return jnp.concatenate([ref[s, 0] for s in range(ref.shape[0])], axis=1)


def turn(value):
    return value.astype(F32).T.astype(BF16)


def attention_kernel(block, q_ref, k_ref, v_ref, seg_q_ref, seg_k_ref, out_ref):
    queries = turn(side_by_side(q_ref))
    keys = side_by_side(k_ref)
    values = side_by_side(v_ref)
    frames = out_ref.shape[2]
    factor = HEAD_DIM**-0.5 * LOG2E
    for first in range(0, queries.shape[0], block):
        rows = slice(first, first + block)
        scores = jnp.dot(queries[rows], keys, preferred_element_type=F32)
        expo = jnp.where(seg_q_ref[rows] == seg_k_ref[...], jnp.exp2(scores * factor), 0.0)
        weight_sum = jnp.sum(expo, axis=1, keepdims=True)
        accum = lax.dot_general(
            expo.astype(BF16), values, (((1,), (1,)), ((), ())), preferred_element_type=F32
        )
        context = (accum / weight_sum).T
        for part in range(block // frames):
            out_ref[first // frames + part] = context[:, part * frames : (part + 1) * frames]


def attention_back_kernel(
    block, q_ref, k_ref, v_ref, cg_ref, ctx_ref, seg_q_ref, seg_k_ref,
    dq_ref, dk_ref, dv_ref, dk_sum, dv_sum,
):
    keys_across = side_by_side(k_ref)
    keys = turn(keys_across)
    values = turn(side_by_side(v_ref))
    frames = ctx_ref.shape[2]
    parts = block // frames
    scale = HEAD_DIM**-0.5
    for step in range(q_ref.shape[0] // parts):
        some = range(step * parts, (step + 1) * parts)
        columns = slice(step * block, (step + 1) * block)
        queries = jnp.concatenate([q_ref[s, 0] for s in some], axis=1)
        context_grad = jnp.concatenate([cg_ref[s].astype(F32) for s in some], axis=1)
        context = jnp.concatenate([ctx_ref[s] for s in some], axis=1)
        scores = jnp.dot(keys, queries, preferred_element_type=F32)
        expo = jnp.where(
            seg_k_ref[...] == seg_q_ref[:, columns], jnp.exp2(scores * (scale * LOG2E)), 0.0
        )
        inverse = 1.0 / jnp.sum(expo, axis=0, keepdims=True)
        accum_g = (context_grad * inverse).astype(BF16)
        correction = jnp.sum(context_grad * context, axis=0, keepdims=True) * inverse
        dots = jnp.dot(values, accum_g, preferred_element_type=F32)
        score_g = (expo * (dots - correction)).astype(BF16)
        query_grad = jnp.dot(keys_across, score_g, preferred_element_type=F32) * scale
        for part, s in enumerate(some):
            dq_ref[s] = query_grad[:, part * frames : (part + 1) * frames].astype(BF16)
        key_grad = lax.dot_general(
            score_g, queries, (((1,), (1,)), ((), ())), preferred_element_type=F32
        )
        value_grad = lax.dot_general(
            expo.astype(BF16), accum_g, (((1,), (1,)), ((), ())), preferred_element_type=F32
        )
        if step == 0:
            dk_sum[...] = key_grad
            dv_sum[...] = value_grad
        else:
            dk_sum[...] += key_grad
            dv_sum[...] += value_grad
    key_total = (dk_sum[...] * scale).T.astype(BF16)
    value_total = dv_sum[...].T.astype(BF16)
    for s in range(dk_ref.shape[0]):
        dk_ref[s] = key_total[:, s * frames : (s + 1) * frames]
        dv_ref[s] = value_total[:, s * frames : (s + 1) * frames]


def head_spec(count, frames, which):
    return pl.BlockSpec((count, 1, HEAD_DIM, frames), lambda h: (0, which, h, 0))


def plain_spec(count, frames):
    return pl.BlockSpec((count, HEAD_DIM, frames), lambda h: (0, h, 0))


def whole_spec(array):
    return pl.BlockSpec(array.shape, lambda h: (0,) * array.ndim)


def attention(mixed, mixed_all, seg_q, seg_k):
    count, _, channels, frames = mixed.shape
    total = mixed_all.shape[0]
    heads = channels // HEAD_DIM
    block = math.gcd(count, 2) * frames
    seg_q, seg_k = seg_q[:, None], seg_k[None]
    return pl.pallas_call(
        lambda *refs: attention_kernel(block, *refs),
        grid=(heads,),
        in_specs=[
            head_spec(count, frames, 0),
            head_spec(total, frames, 1),
            head_spec(total, frames, 2),
            whole_spec(seg_q),
            whole_spec(seg_k),
        ],
        out_specs=plain_spec(count, frames),
        out_shape=jax.ShapeDtypeStruct((count, channels, frames), F32),
        compiler_params=pltpu.CompilerParams(vmem_limit_bytes=VMEM),
        cost_estimate=pl.CostEstimate(flops=0, bytes_accessed=0, transcendentals=0),
        name="attention",
    )(mixed, mixed_all, mixed_all, seg_q, seg_k)


def attention_back(mixed, mixed_all, context_grad, context, seg_q, seg_k):
    count, _, channels, frames = mixed.shape
    total = mixed_all.shape[0]
    heads = channels // HEAD_DIM
    block = math.gcd(count, 2) * frames
    seg_q, seg_k = seg_q[None], seg_k[:, None]
    return pl.pallas_call(
        lambda *refs: attention_back_kernel(block, *refs),
        grid=(heads,),
        in_specs=[
            head_spec(count, frames, 0),
            head_spec(total, frames, 1),
            head_spec(total, frames, 2),
            plain_spec(count, frames),
            plain_spec(count, frames),
            whole_spec(seg_q),
            whole_spec(seg_k),
        ],
        out_specs=[
            plain_spec(count, frames),
            plain_spec(total, frames),
            plain_spec(total, frames),
        ],
        out_shape=[
            jax.ShapeDtypeStruct((count, channels, frames), BF16),
            jax.ShapeDtypeStruct((total, channels, frames), BF16),
            jax.ShapeDtypeStruct((total, channels, frames), BF16),
        ],
        scratch_shapes=[pltpu.VMEM((total * frames, HEAD_DIM), F32)] * 2,
        compiler_params=pltpu.CompilerParams(vmem_limit_bytes=VMEM),
        cost_estimate=pl.CostEstimate(flops=0, bytes_accessed=0, transcendentals=0),
        name="attention_back",
    )(mixed, mixed_all, mixed_all, context_grad, context, seg_q, seg_k)


def gate_and_slope(values):
    inner = 0.5 + 0.5 * lax.erf(values * math.sqrt(0.5))
    density = jnp.exp(-0.5 * values * values) * (1.0 / math.sqrt(2.0 * math.pi))
    return values * inner, inner + values * density


def norm_parts(values):
    center = values - jnp.mean(values, axis=1, keepdims=True)
    spread = jnp.mean(center * center, axis=1, keepdims=True)
    rate = lax.rsqrt(spread + NORM_EPS)
    return center * rate, rate


def norm_back(unit, rate, gain, grad):
    scaled = grad * gain
    level = jnp.mean(scaled, axis=1, keepdims=True)
    slope = jnp.mean(scaled * unit, axis=1, keepdims=True)
    return rate * (scaled - level - unit * slope), jnp.sum(grad * unit, axis=0, keepdims=True)


def dot_nt(left, right):
    return lax.dot_general(left, right, (((1,), (1,)), ((), ())), preferred_element_type=F32)


def feed_kernel(
    ctx_ref, out_w_ref, encoded_ref, attention_gain_ref, final_gain_ref, cotangent_ref,
    feed0, feed1, feed2, feed3,
    block_out_ref, mid_ref, context_grad_ref, attention_grad_ref, final_grad_ref,
    settled_ref, hidden_ref, fed_ref, up_ref, branch_ref,
    weights, slopes, sems,
):
    copies = [
        pltpu.make_async_copy(feed, weights.at[k], sems.at[k])
        for k, feed in enumerate((feed0, feed1, feed2, feed3))
    ]
    for copy in copies:
        copy.start()
    kinds, part, frames = ctx_ref.shape
    heads = kinds // MICROS
    width = weights.shape[1]
    units = weights.shape[2] - width
    context = jnp.concatenate(
        [
            jnp.concatenate([ctx_ref[h * MICROS + m] for m in range(MICROS)], axis=1)
            for h in range(heads)
        ],
        axis=0,
    )
    context = turn(context)
    attention_gain = attention_gain_ref[...]
    final_gain = final_gain_ref[...]
    branch = jnp.dot(context, out_w_ref[...], preferred_element_type=F32)
    unit, rate = norm_parts(encoded_ref[...] + branch)
    settled = unit * attention_gain
    settled_low = settled.astype(BF16)
    settled_ref[...] = settled_low
    fed = settled
    for k, copy in enumerate(copies):
        copy.wait()
        columns = slice(k * units, (k + 1) * units)
        up_values = jnp.dot(settled_low, weights[k, :, :units], preferred_element_type=F32)
        hidden, slope = gate_and_slope(up_values)
        slopes[:, columns] = slope
        hidden_low = hidden.astype(BF16)
        hidden_ref[:, columns] = hidden_low
        fed += jnp.dot(hidden_low, weights[k, :, units:], preferred_element_type=F32)
    final_unit, final_rate = norm_parts(fed)
    block_out_ref[...] = final_unit * final_gain
    sum_grad, final_grad_ref[...] = norm_back(
        final_unit, final_rate, final_gain, cotangent_ref[...].astype(F32)
    )
    fed_low = sum_grad.astype(BF16)
    fed_ref[...] = fed_low
    settled_grad = sum_grad
    for k in range(len(copies)):
        columns = slice(k * units, (k + 1) * units)
        up_low = (dot_nt(fed_low, weights[k, :, units:]) * slopes[:, columns]).astype(BF16)
        up_ref[:, columns] = up_low
        settled_grad += dot_nt(up_low, weights[k, :, :units])
    mid_grad, attention_grad_ref[...] = norm_back(unit, rate, attention_gain, settled_grad)
    mid_ref[...] = mid_grad
    branch_low = mid_grad.astype(BF16)
    branch_ref[...] = branch_low
    context_grad = dot_nt(out_w_ref[...], branch_low).astype(BF16)
    for h in range(heads):
        for m in range(MICROS):
            context_grad_ref[h * MICROS + m] = context_grad[
                h * part : (h + 1) * part, m * frames : (m + 1) * frames
            ]


def feed_forward(context, out_w, encoded, attention_gain, final_gain, cotangent, feeds):
    rows, width = encoded.shape
    units = feeds[0].shape[1] - width
    wide = len(feeds) * units
    vmem = pl.BlockSpec(memory_space=pltpu.VMEM)
    return pl.pallas_call(
        feed_kernel,
        in_specs=[vmem] * 6 + [pl.BlockSpec(memory_space=pl.ANY)] * 4,
        out_specs=[vmem] * 10,
        out_shape=[
            jax.ShapeDtypeStruct((rows, width), F32),
            jax.ShapeDtypeStruct((rows, width), F32),
            jax.ShapeDtypeStruct(context.shape, BF16),
            jax.ShapeDtypeStruct((1, width), F32),
            jax.ShapeDtypeStruct((1, width), F32),
            jax.ShapeDtypeStruct((rows, width), BF16),
            jax.ShapeDtypeStruct((rows, wide), BF16),
            jax.ShapeDtypeStruct((rows, width), BF16),
            jax.ShapeDtypeStruct((rows, wide), BF16),
            jax.ShapeDtypeStruct((rows, width), BF16),
        ],
        scratch_shapes=[
            pltpu.VMEM((len(feeds), width, width + units), BF16),
            pltpu.VMEM((rows, wide), F32),
            pltpu.SemaphoreType.DMA((len(feeds),)),
        ],
        compiler_params=pltpu.CompilerParams(vmem_limit_bytes=VMEM),
        cost_estimate=pl.CostEstimate(flops=0, bytes_accessed=0, transcendentals=0),
        name="feed_forward",
    )(context, out_w, encoded, attention_gain, final_gain, cotangent, *feeds)


def feed_grad_kernel(stream_ref, settled_ref, up_ref, hidden_ref, fed_ref, out_ref):
    stream = stream_ref[0]
    seqs, streams, _, _, rows, width = out_ref.shape
    units = up_ref.shape[1] // streams
    settled = turn(settled_ref[...])
    fed = fed_ref[...]
    for k in range(streams):
        f = k ^ stream
        columns = slice(k * units, (k + 1) * units)
        down_grad = jnp.dot(turn(hidden_ref[:, columns]), fed, preferred_element_type=F32)
        up_grad = jnp.dot(settled, up_ref[:, columns], preferred_element_type=F32)
        for s in range(seqs):
            for j in range(streams):
                first = (s * streams + j) * rows
                piece = slice(first, first + rows)
                out_ref[s, f, 0, j] = down_grad[piece].astype(BF16)
                out_ref[s, j, 1, f] = up_grad[piece].astype(BF16)


def feed_grad(stream, settled, up, hidden, fed, seqs):
    rows, width = settled.shape
    streams = up.shape[1] // width
    vmem = pl.BlockSpec(memory_space=pltpu.VMEM)
    shape = (seqs, streams, 2, streams, width // (seqs * streams), width)
    return pl.pallas_call(
        feed_grad_kernel,
        in_specs=[pl.BlockSpec(memory_space=pltpu.SMEM)] + [vmem] * 4,
        out_specs=vmem,
        out_shape=jax.ShapeDtypeStruct(shape, BF16),
        compiler_params=pltpu.CompilerParams(vmem_limit_bytes=VMEM),
        cost_estimate=pl.CostEstimate(flops=0, bytes_accessed=0, transcendentals=0),
        name="feed_grad",
    )(stream, settled, up, hidden, fed)


def head_kernel(width, encoded_ref, *refs):
    blocks, out_ref = refs[:-1], refs[-1]
    frames = out_ref.shape[2]
    encoded = encoded_ref[...]
    for k, block in enumerate(blocks):
        mixed = jnp.dot(encoded, block[:, :width], preferred_element_type=F32).T.astype(BF16)
        for m in range(MICROS):
            out_ref[k * MICROS + m] = mixed[:, m * frames : (m + 1) * frames]


def head_projection(encoded, blocks, width):
    rows, depth = encoded.shape
    vmem = pl.BlockSpec(memory_space=pltpu.VMEM)
    shape = (len(blocks) * MICROS, width, rows // MICROS)
    return pl.pallas_call(
        lambda *refs: head_kernel(width, *refs),
        in_specs=[vmem] * (1 + len(blocks)),
        out_specs=vmem,
        out_shape=jax.ShapeDtypeStruct(shape, BF16),
        compiler_params=pltpu.CompilerParams(vmem_limit_bytes=VMEM),
        cost_estimate=pl.CostEstimate(flops=0, bytes_accessed=0, transcendentals=0),
        name="head_projection",
    )(encoded, *blocks)


def head_back_kernel(
    width, mixed_ref, mid_ref, position_ref, projected_ref, gain_ref, block0, block1, block2,
    block3, joined_ref, position_grad_ref, gain_grad_ref,
):
    total = mid_ref[...]
    for k, block in enumerate((block0, block1, block2, block3)):
        pieces = [mixed_ref[k * MICROS + m].astype(F32).T for m in range(MICROS)]
        mixed = jnp.concatenate(pieces, axis=0).astype(BF16)
        total += dot_nt(mixed, block[:, :width])
    position, slope = gate_and_slope(position_ref[...].astype(F32).T)
    unit, rate = norm_parts(projected_ref[...] + position)
    joined, gain_grad_ref[...] = norm_back(unit, rate, gain_ref[...], total)
    joined_ref[...] = joined
    position_grad_ref[...] = (joined * slope).T.astype(BF16)


def head_back(mixed, mid_grad, position, projected, gain, blocks, width):
    rows, depth = mid_grad.shape
    vmem = pl.BlockSpec(memory_space=pltpu.VMEM)
    return pl.pallas_call(
        lambda *refs: head_back_kernel(width, *refs),
        in_specs=[vmem] * (5 + len(blocks)),
        out_specs=[vmem] * 3,
        out_shape=[
            jax.ShapeDtypeStruct((rows, depth), F32),
            jax.ShapeDtypeStruct((depth, rows), BF16),
            jax.ShapeDtypeStruct((1, depth), F32),
        ],
        compiler_params=pltpu.CompilerParams(vmem_limit_bytes=VMEM),
        cost_estimate=pl.CostEstimate(flops=0, bytes_accessed=0, transcendentals=0),
        name="head_back",
    )(mixed, mid_grad, position, projected, gain, *blocks)


def front_kernel(
    stream_ref, back_ref, joined_ref, normed_ref, projection_ref, before_ref, feature_gain_ref,
    unfolded_ref, conv_ref, encoder_ref, attention_ref, final_ref, mask_n_ref, mask_w_ref,
    place0, place1, place2, place3, packed_ref, unfolded_grad_ref,
):
    stream = stream_ref[0]
    projected_grad = (joined_ref[...] + back_ref[...].astype(F32).T).astype(BF16)
    normed_grad = dot_nt(projected_grad, projection_ref[...])
    activated, slope = gate_and_slope(before_ref[...])
    unit, rate = norm_parts(activated)
    activated_grad, feature_grad = norm_back(unit, rate, feature_gain_ref[...], normed_grad)
    before_low = (activated_grad * slope).astype(BF16)
    unfolded_grad_ref[...] = dot_nt(before_low, conv_ref[...])
    conv_grad = jnp.dot(turn(unfolded_ref[...]), before_low, preferred_element_type=F32)
    projection_grad = jnp.dot(turn(normed_ref[...]), projected_grad, preferred_element_type=F32)
    gains = jnp.zeros((mask_n_ref.shape[0], place0.shape[1]), F32)
    for grad, mask, place in (
        (feature_grad, mask_n_ref, place0),
        (encoder_ref[...], mask_w_ref, place1),
        (attention_ref[...], mask_w_ref, place2),
        (final_ref[...], mask_w_ref, place3),
    ):
        gains += jnp.dot((grad * mask[...]).astype(BF16), place[...], preferred_element_type=F32)
    streams, seqs, _, width = packed_ref.shape
    conv_rows = conv_grad.shape[0] // (streams * seqs)
    rows = projection_grad.shape[0] // (streams * seqs)
    first = lax.broadcasted_iota(jnp.int32, (8, gains.shape[1]), 0) == 0
    blank = jnp.zeros((8, width - gains.shape[1]), F32)
    for s in range(seqs):
        for f in range(streams):
            d = s * streams + f
            piece = projection_grad[d * rows : (d + 1) * rows]
            rest = piece[:, width:]
            folded = jnp.concatenate([rest[: rows // 2], rest[rows // 2 :]], axis=1)
            row = jnp.concatenate([jnp.where(first, gains[d : d + 1], 0.0), blank], axis=1)
            block = jnp.concatenate(
                [conv_grad[d * conv_rows : (d + 1) * conv_rows], piece[:, :width], folded, row],
                axis=0,
            )
            packed_ref[f ^ stream, s] = block.astype(BF16)


def front_back(
    stream, back, joined, normed, projection, before, feature_gain, unfolded, conv, gain_grads,
    streams, seqs,
):
    devices = streams * seqs
    narrow, wide = projection.shape
    counts = [narrow // devices] + [wide // devices] * 3
    masks, places, start = [], [], 0
    for size, count in zip((narrow, wide, wide, wide), counts):
        column = np.arange(size)
        masks.append((column[None] // count == np.arange(devices)[:, None]).astype(np.float32))
        place = column[:, None] % count + start == np.arange(128)[None]
        places.append(jnp.asarray(place, BF16))
        start += count
    depth = (conv.shape[0] + narrow + narrow // 2) // devices + 8
    vmem = pl.BlockSpec(memory_space=pltpu.VMEM)
    return pl.pallas_call(
        front_kernel,
        in_specs=[pl.BlockSpec(memory_space=pltpu.SMEM)] + [vmem] * 17,
        out_specs=[vmem] * 2,
        out_shape=[
            jax.ShapeDtypeStruct((streams, seqs, depth, narrow), BF16),
            jax.ShapeDtypeStruct(unfolded.shape, F32),
        ],
        compiler_params=pltpu.CompilerParams(vmem_limit_bytes=VMEM),
        cost_estimate=pl.CostEstimate(flops=0, bytes_accessed=0, transcendentals=0),
        name="front_back",
    )(
        stream, back, joined, normed, projection, before, feature_gain, unfolded, conv,
        *gain_grads, masks[0], masks[1], *places,
    )


def body(
    features,
    lengths,
    conv_weight,
    feature_gain,
    projection_weight,
    position_weight,
    encoder_gain,
    qkv_weight,
    output_weight,
    attention_gain,
    up_weight,
    down_weight,
    final_gain,
    cotangent,
):
    frames = cotangent.shape[2]
    rows = MICROS * frames
    seqs = lax.axis_size("seq")
    streams = lax.axis_size("fsdp")
    devices = seqs * streams
    me = lax.axis_index("seq")
    stream = lax.axis_index("fsdp")
    both = ("seq", "fsdp")
    group = HEAD_PARTS * MICROS
    outer = seqs // group
    near = [[o * group + i for i in range(group)] for o in range(outer)]
    far = [[o * group + i for o in range(outer)] for i in range(group)]

    def near_swap(blocks):
        return lax.all_to_all(blocks, "seq", 0, 0, axis_index_groups=near)

    def seq_blocks(blocks):
        shape = (outer, group, -1, blocks.shape[-1])
        return near_swap(blocks.reshape(shape).transpose(1, 0, 2, 3))

    def seq_total(blocks):
        total = jnp.sum(blocks.astype(F32), axis=0)
        if outer == 1:
            return total[0]
        return lax.psum_scatter(total, "seq", scatter_dimension=0, axis_index_groups=far)

    def near_gather(block, again):
        blocks = [block]
        for k in range(1, group):
            pairs = [(i, i - i % group + (i % group ^ k)) for i in range(seqs)]
            blocks.append(lax.ppermute(block if k < 5 else again, "seq", pairs))
        return jnp.stack(flip(blocks, me % group))

    front_rows = (conv_weight.shape[0], projection_weight.size // C_CNN)
    gains = jnp.concatenate([feature_gain, encoder_gain, attention_gain, final_gain])
    front = jnp.concatenate(
        [
            conv_weight,
            projection_weight.reshape(-1, C_CNN),
            jnp.pad(gains[None], ((0, 7), (0, C_CNN - gains.size))),
        ],
        axis=0,
    )
    part = D // HEAD_PARTS
    up_rows = up_weight.shape[0]
    unit_rows = down_weight.shape[0]
    wide = seqs * unit_rows
    up_parts = up_weight.reshape(up_rows, seqs, streams, unit_rows).transpose(2, 0, 1, 3)
    qkv_parts = qkv_weight.reshape(up_rows, 3, streams, part).transpose(2, 0, 1, 3)
    parts = jnp.concatenate(
        [qkv_parts.reshape(streams, up_rows, 3 * part), up_parts.reshape(streams, up_rows, wide)],
        axis=2,
    )
    parts = jnp.concatenate(swap_parts([parts[j] for j in range(streams)], stream), axis=0)
    front_again, parts = lax.optimization_barrier((front, parts))
    front_near = near_gather(front, front_again)
    front = front_near
    if outer > 1:
        front = lax.all_gather(front, "seq", axis=0, tiled=True, axis_index_groups=far)
    own_rows = position_weight.shape[0]
    share = D // group
    taps = near_swap(after(position_weight, front_near).T.reshape(group, share, own_rows))
    over_x, taps = lax.optimization_barrier((swapped(front, 2), taps))
    front = [front, swapped(front, 1), over_x, swapped(over_x, 1)]
    front = jnp.stack(flip(front, stream), axis=1)
    front = front.reshape(devices, -1, C_CNN)
    cut = front_rows[0] + front_rows[1]
    conv_full = front[:, : front_rows[0]].reshape(-1, C_CNN)
    projection_full = front[:, front_rows[0] : cut].reshape(C_CNN, D)
    gains_full = front[:, cut, : gains.size]
    feature_n, model_n = feature_gain.size, encoder_gain.size
    feature_scale = gains_full[:, :feature_n].reshape(-1).astype(F32)
    encoder_scale, attention_scale, final_scale = (
        gains_full[:, feature_n + i * model_n : feature_n + (i + 1) * model_n]
        .reshape(-1)
        .astype(F32)
        for i in range(3)
    )

    out_parts = output_weight.reshape(up_rows, streams, part).transpose(1, 0, 2)
    quarter = jnp.concatenate(
        [parts[:, : 3 * part], out_parts.reshape(-1, part), parts[:, 3 * part :], down_weight],
        axis=1,
    )
    quarter = lax.all_gather(quarter, "seq", axis=0, tiled=True)

    ends = jnp.cumsum(lengths[:, 0], axis=-1, dtype=jnp.int32)
    positions = me * frames + jnp.arange(frames + 1, dtype=jnp.int32)
    segments = segment_of(ends, positions)
    same_next = (segments[:, 1:] == segments[:, :-1])[:, :, None]
    pairs = features[:, 0].reshape(MICROS, frames, 2 * C_CNN)
    next_first = shifted(pairs[:, :1, :C_CNN], "seq", -1)
    following = jnp.concatenate([pairs[:, 1:, :C_CNN], next_first], axis=1)
    following = following * same_next.astype(BF16)
    unfolded = jnp.concatenate([pairs, following], axis=2).reshape(rows, 3 * C_CNN)
    before = plain_dot(unfolded, conv_full)
    normed_low = norm_rows(smooth_gate(before), feature_scale).astype(BF16)
    projected = plain_dot(normed_low, projection_full)

    if outer > 1:
        taps = lax.all_gather(taps, "seq", axis=0, axis_index_groups=far)
    taps = after(taps.reshape(outer, group, share, own_rows), projected)
    position_full = (
        jnp.stack(flip([taps] + [swapped(taps, k) for k in range(1, 4)], stream))
        .transpose(3, 1, 2, 0, 4)
        .reshape(share, COARSE, FINE * CG)
        .transpose(1, 0, 2)
    )

    def to_groups(block):
        across = near_swap(block.reshape(group, share, rows))
        if outer == 1:
            return across, jnp.zeros((share, MICROS * POS_K), BF16)
        first = across[0].reshape(share, MICROS, frames)[:, :, :HALF]
        last = across[-1].reshape(share, MICROS, frames)[:, :, frames - HALF :]
        edge = [shifted(first, "seq", -group), shifted(last, "seq", group)]
        return across, jnp.concatenate(edge, axis=2).reshape(share, MICROS * POS_K)

    window, window_edge = to_groups(projected.astype(BF16).T)
    position = position_conv(window, window_edge, position_full)
    middle = gather_blocks(after(quarter[:, : 4 * part], position))
    position = near_swap(position).reshape(D, rows)
    feed, position = lax.optimization_barrier((quarter[:, 4 * part :], position))
    feed = gather_blocks(feed)
    position_act = smooth_gate(position.T.astype(F32))
    encoded = norm_rows(projected + position_act, encoder_scale)
    encoded_low = encoded.astype(BF16)

    mixed_heads = head_projection(encoded_low, middle, 3 * part)
    mixed_heads = near_swap(mixed_heads)
    mixed_heads = mixed_heads.reshape(group, 3, part, frames)
    micro_ends = lax.dynamic_index_in_dim(ends, me % MICROS, 0, keepdims=False)
    seg_all = segment_of(micro_ends, jnp.arange(seqs * frames, dtype=jnp.int32))
    seg_own = lax.dynamic_slice_in_dim(
        seg_all, (me // group) * group * frames, group * frames, 0
    )
    output_full = jnp.stack(flip([block[:, 3 * part :] for block in middle], stream))
    output_full = (
        output_full.reshape(streams, seqs, streams, up_rows, part)
        .transpose(1, 0, 3, 2, 4)
        .reshape(HEAD_PARTS, part, D)
    )
    output_full = jnp.concatenate(flip([output_full[j] for j in range(HEAD_PARTS)], stream))
    mixed_heads, output_full = lax.optimization_barrier((mixed_heads, output_full))
    if outer > 1:
        mixed_all = lax.all_gather(
            mixed_heads, "seq", axis=0, tiled=True, axis_index_groups=far
        )
    else:
        mixed_all = mixed_heads
    context_heads = attention(mixed_heads, mixed_all, seg_own, seg_all)
    context_low = near_swap(context_heads.astype(BF16))

    (
        block_out, mid_grad, context_grad, attention_grad, final_grad,
        settled_low, hidden_low, fed_low, up_low, branch_low,
    ) = feed_forward(
        context_low, output_full, encoded, attention_scale[None], final_scale[None],
        cotangent[:, 0].reshape(rows, D), feed,
    )
    context_grad = near_swap(context_grad)
    feed_grads = feed_grad(stream[None], settled_low, up_low, hidden_low, fed_low, seqs)
    context_grad, feed_grads = lax.optimization_barrier((context_grad, feed_grads))
    feed_grads = feed_grads.reshape(devices, -1, D)
    feed_shard = lax.psum_scatter(feed_grads, both, scatter_dimension=0)
    context_low = context_low.reshape(HEAD_PARTS, MICROS, part, frames).transpose(0, 2, 1, 3)
    output_grad = plain_dot(context_low.reshape(D, rows), branch_low).astype(BF16)
    output_grad = output_grad.reshape(HEAD_PARTS, part, D)
    output_grad = jnp.stack(flip([output_grad[j] for j in range(HEAD_PARTS)], stream))
    output_grad = (
        output_grad.reshape(seqs, streams, up_rows, streams, part)
        .transpose(1, 0, 3, 2, 4)
        .reshape(streams, D, part)
    )
    output_grads = flip([output_grad[j] for j in range(streams)], stream)

    dq, dk, dv = attention_back(
        mixed_heads, mixed_all, context_grad, context_heads, seg_own, seg_all
    )
    if outer > 1:
        dk, dv = (
            lax.psum_scatter(
                grad, "seq", scatter_dimension=0, tiled=True, axis_index_groups=far
            )
            for grad in (dk, dv)
        )
    mixed_g = near_swap(jnp.stack([dq, dk, dv], axis=1)).reshape(group, 3 * part, frames)
    joined_grad, position_grad, encoder_grad = head_back(
        mixed_g, mid_grad, position, projected, encoder_scale[None], middle, 3 * part
    )
    mixed_g = mixed_g.reshape(HEAD_PARTS, MICROS, 3 * part, frames).transpose(0, 2, 1, 3)
    mixed_g = mixed_g.reshape(HEAD_PARTS, 3 * part, rows)
    middle_grads = [
        jnp.concatenate(
            [
                lax.dot_general(
                    encoded_low, mixed_g[k], (((0,), (1,)), ((), ())), preferred_element_type=F32
                ).astype(BF16),
                output_grads[k],
            ],
            axis=1,
        )
        for k in range(HEAD_PARTS)
    ]

    grad_window, grad_edge = to_groups(position_grad)
    grad_window, middle_pairs = lax.optimization_barrier((grad_window, pair_sums(middle_grads)))
    middle_sum = low_sum(middle_pairs[0], swapped(middle_pairs[1], 2))
    projected_back, taps_grad = position_back(
        window, window_edge, grad_window, grad_edge, position_full
    )


    projected_back = near_swap(projected_back).reshape(D, rows)
    projected_back, middle_sum = lax.optimization_barrier((projected_back, middle_sum))
    front_grads, unfolded_grad = front_back(
        stream[None], projected_back, joined_grad, normed_low, projection_full, before,
        feature_scale[None], unfolded, conv_full, (encoder_grad, attention_grad, final_grad),
        streams, seqs,
    )
    unfolded_grad = unfolded_grad.reshape(MICROS, frames, 3 * C_CNN)
    middle_halves = [seq_blocks(middle_sum[:, : 2 * part])]
    middle_halves.append(seq_blocks(after(middle_sum[:, 2 * part :], middle_halves[0])))
    following_grad = unfolded_grad[:, :, 2 * C_CNN :] * same_next.astype(F32)
    carried = shifted(following_grad[:, frames - 1 :], "seq", 1)
    even_grad = unfolded_grad[:, :, :C_CNN] + jnp.concatenate(
        [carried, following_grad[:, :-1]], axis=1
    )
    input_grad = jnp.concatenate([even_grad, unfolded_grad[:, :, C_CNN : 2 * C_CNN]], axis=2)
    input_grad = input_grad.reshape(MICROS, 1, 2 * frames, C_CNN)

    front_pairs = pair_sums([front_grads[k] for k in range(streams)])
    front_sum = low_sum(front_pairs[0], swapped(front_pairs[1], 2))
    taps_grad = after(taps_grad, front_pairs[1])
    taps_grad = (
        taps_grad.transpose(1, 0, 2)
        .reshape(share, outer, group, streams, own_rows)
        .transpose(3, 1, 2, 0, 4)
    )
    taps_grad = reduce_blocks(flip([taps_grad[j] for j in range(streams)], stream))
    front_rows = front_sum.shape[1]
    front_sum = front_sum.reshape(outer, group, front_rows, C_CNN)
    half = share // 2
    taps_rows = jnp.concatenate([taps_grad[:, :, :half], taps_grad[:, :, half:]], axis=3)
    taps_rows = jnp.pad(taps_rows, ((0, 0),) * 3 + ((0, C_CNN - 2 * own_rows),))
    last = jnp.concatenate([front_sum, taps_rows], axis=2)
    last, middle_halves = lax.optimization_barrier((last, middle_halves))
    last = near_swap(last.transpose(1, 0, 2, 3))
    front_shard = seq_total(last[:, :, :front_rows])
    taps_rows = last[:, :, front_rows:]
    if outer > 1:
        taps_rows = lax.psum_scatter(
            taps_rows, "seq", scatter_dimension=1, axis_index_groups=far
        )
    else:
        taps_rows = taps_rows[:, 0]
    taps_grad = jnp.concatenate(
        [taps_rows[:, :, :own_rows], taps_rows[:, :, own_rows : 2 * own_rows]], axis=1
    )
    position_shard = taps_grad.reshape(D, own_rows).T.astype(F32)
    middle_shard = jnp.concatenate([seq_total(half) for half in middle_halves], axis=1)

    def unswap(block):
        block = block.reshape(streams, up_rows, -1)
        return jnp.stack(swap_parts([block[j] for j in range(streams)], stream)).astype(F32)

    feed_shard = feed_shard.reshape(2, streams, up_rows, wide).astype(F32)
    down_shard = feed_shard[0].reshape(unit_rows, D)
    up_shard = (
        feed_shard[1]
        .reshape(streams, up_rows, seqs, unit_rows)
        .transpose(1, 2, 0, 3)
        .reshape(up_rows, -1)
    )
    qkv_shard = (
        unswap(middle_shard[:, : 3 * part])
        .reshape(streams, up_rows, 3, part)
        .transpose(1, 2, 0, 3)
        .reshape(up_rows, -1)
    )
    output_shard = (
        middle_shard[:, 3 * part :]
        .reshape(streams, up_rows, part)
        .transpose(1, 0, 2)
        .reshape(up_rows, D)
        .astype(F32)
    )
    conv_rows, projection_rows = conv_weight.shape[0], projection_weight.shape[0]
    conv_shard = front_shard[:conv_rows]
    cut = conv_rows + projection_rows
    folded = front_shard[cut : cut + projection_rows // 2]
    folded = jnp.concatenate([folded[:, : D - C_CNN], folded[:, D - C_CNN :]], axis=0)
    projection_shard = jnp.concatenate([front_shard[conv_rows:cut], folded], axis=1)
    gain_row = front_shard[cut + projection_rows // 2]
    gain_shards = [
        gain_row[:feature_n],
        *(gain_row[feature_n + i * model_n : feature_n + (i + 1) * model_n] for i in range(3)),
    ]
    return (
        block_out.reshape(MICROS, 1, frames, D),
        input_grad,
        conv_shard,
        gain_shards[0],
        projection_shard,
        position_shard,
        gain_shards[1],
        qkv_shard,
        output_shard,
        gain_shards[2],
        up_shard,
        down_shard,
        gain_shards[3],
    )


def solution(mesh):
    weight, gain = P(("seq", "fsdp"), None), P(("seq", "fsdp"))
    rows = P(None, "fsdp", "seq", None)
    in_specs = (
        rows, P(None, "fsdp", None), weight, gain, weight, weight, gain, weight, weight, gain,
        weight, weight, gain, rows,
    )
    out_specs = (
        rows, rows, weight, gain, weight, weight, gain, weight, weight, gain, weight, weight, gain,
    )
    return jax.shard_map(body, mesh=mesh, in_specs=in_specs, out_specs=out_specs, check_vma=False)
```
